512 devices in a mesh: dom: 256 (over z, y, x), blk: 2 (over core).
Axes of the slice: x: 4, y: 8, z: 8, core: 2. Of those that a mesh axis runs over, the one named last changes fastest.
Arguments:
- pd_disp: float32 [1024, 2, 128], P(('dom', 'blk')), may hold values from -4 to 4
- pd_vel: float32 [1024, 2, 128], P(('dom', 'blk')), may hold values from -4 to 4
- pd_coord: float32 [1024, 2, 128], P(('dom', 'blk')), may hold values from -4 to 4
- pd_modulus: float32 [1024, 128], P(('dom', 'blk')), may hold values from 2 to 20
- pd_step: float32 [1024, 128], P(('dom', 'blk')), may hold values from 0.03 to 0.3
- family_tile_lists: int32 [1024, 3], P(('dom', 'blk')), may hold values from 0 to 11, as said below
- live_tiles: int32 [256], P('dom'), may hold values from 3 to 4, as said below
- patch_tile: int32 [512], P('dom'), may hold values from 0 to 3, as said below
- patch_blend: float32 [512, 128], P('dom'), may hold values from 0.1 to 0.9
- patch_nodes: int32 [512, 128], P(('dom', 'blk')), may hold values from 0 to 12799, as said below
- patch_matrix: float32 [512, 128, 128], P(('dom', 'blk')), may hold values from -0.5 to 0.5
- fe_disp: float32 [2, 3276800], P(None, ('dom', 'blk')), may hold values from -4 to 4
- fe_vel: float32 [2, 3276800], P(None, ('dom', 'blk')), may hold values from -4 to 4
- fe_step: float32 [3276800], P(('dom', 'blk')), may hold values from 0.03 to 0.3
- fe_modulus: float32 [65536], P(('dom', 'blk')), may hold values from 0.5 to 2
- element_nodes: int32 [64, 65536], P(None, ('dom', 'blk')), may hold values from 0 to 12799, as said below
- shape_grad: float32 [2, 64, 64], replicated, may hold values from -0.75 to 0.75
- quad_weight: float32 [64], replicated, may hold values from 0.5 to 2
- shared_left: int32 [256, 113], P('dom'), may hold values from 0 to 12799, as said below
- shared_right: int32 [256, 113], P('dom'), may hold values from 0 to 12799, as said below
Outputs:
- pd_disp_out: float32 [1024, 2, 128], P(('dom', 'blk'))
- pd_vel_out: float32 [1024, 2, 128], P(('dom', 'blk'))
- fe_disp_out: float32 [2, 3276800], P(None, ('dom', 'blk'))
- fe_vel_out: float32 [2, 3276800], P(None, ('dom', 'blk'))
The draws below stay inside these ranges and needn't reach their ends.
Inputs may be any that keep to these rules, and one draw needn't show every extreme that they name: Local tiles at index live_tiles[d] or above in subdomain d are padding: their inputs are ignored and their outputs are zero. `family_tile_lists`: each entry names a live tile by extended index; the first subdomain names no entry below 4, the last none at 8 or above. `patch_tile`: within a subdomain the 2 patch tiles are distinct live tiles. `patch_nodes`: node ids of a subdomain's patches are distinct and belong to its elements. `element_nodes`: local node ids of each element's subdomain. `shared_left`: row d lists distinct nodes; entry r is the same physical node as shared_right[d - 1, r]. `shared_right`: row d lists distinct nodes, none in shared_left[d].
All inputs are finite; a program needn't handle non-finite values.
Results may differ from the reference program's by a relative error of at most 0.0003.
Values sent between devices are 32-bit elements; how exact they have to be, the bound alone decides.
A program may use at most 64 MiB of HBM per device.

```python
import math
import jax
import jax.numpy as jnp
from jax import lax

TILE = 128
NB = 3
EX = 16
EY = 16
PT = 4
TILES = 1024
PATCH_DOM = 2
PATCHES = 512
NODE_DEV = 12800
NODES = 3276800
SH = 113
ELEMS = 65536
N_DOM = 256


def node_layout(key):
    base = jax.random.fold_in(key, 7)
    real_nodes = (7 * EX + 1) * (7 * EY + 1)
    keys = jax.vmap(lambda index: jax.random.fold_in(base, index))(jnp.arange(N_DOM))
    shuffle = jax.vmap(lambda sub: jax.random.permutation(sub, NODE_DEV))(keys).astype(jnp.int32)
    chosen = jax.vmap(lambda sub: jax.random.permutation(jax.random.fold_in(sub, 1), real_nodes))(keys).astype(jnp.int32)
    return (shuffle, chosen)


def tile_layout(key):
    base = jax.random.fold_in(key, 21)
    counts = jax.random.randint(jax.random.fold_in(base, 1), (N_DOM,), 3 * PT // 4, PT + 1)
    counts = counts.at[0].set(PT).at[N_DOM - 1].set(3 * PT // 4)
    return (counts.astype(jnp.int32), base)


def draw_live_tiles(key, part):
    counts, base = tile_layout(key)
    return counts


def draw_family_tile_lists(key, part):
    counts, base = tile_layout(key)
    shape = (N_DOM, PT, NB)
    side = jax.random.randint(jax.random.fold_in(base, 2), shape, 0, 3)
    domain = jnp.arange(N_DOM)[:, None, None]
    side = jnp.where((domain == 0) & (side == 0), 1, side)
    side = jnp.where((domain == N_DOM - 1) & (side == 2), 1, side)
    source = jnp.clip(domain + side - 1, 0, N_DOM - 1)
    raw = jax.random.randint(jax.random.fold_in(base, 3), shape, 0, 1 << 20)
    local = raw % counts[source]
    return (side * PT + local).reshape(TILES, NB).astype(jnp.int32)


def draw_patch_tile(key, part):
    counts, base = tile_layout(key)
    slots = jnp.arange(PT)[None, :]
    scores = jax.random.randint(jax.random.fold_in(base, 4), (N_DOM, PT), 0, 1 << 16) * PT + slots
    scores = jnp.where(slots < counts[:, None], scores, (1 << 24) + slots)
    sorting_permutation = jnp.argsort(scores, axis=1)
    return sorting_permutation[:, :PATCH_DOM].reshape(PATCHES).astype(jnp.int32)


def draw_element_nodes(key, part):
    shuffle, chosen = node_layout(key)
    rows_n = 7 * EY + 1
    element = jnp.arange(EX * EY)
    col_el = element // EY
    row_el = element % EY
    local = jnp.arange(64)
    col_n = local // 8
    row_n = local % 8
    structured = (7 * col_el[None, :] + col_n[:, None]) * rows_n + 7 * row_el[None, :] + row_n[:, None]
    mapped = jax.vmap(lambda table: table[structured])(shuffle)
    return jnp.transpose(mapped, (1, 0, 2)).reshape(64, ELEMS).astype(jnp.int32)


def draw_patch_nodes(key, part):
    shuffle, chosen = node_layout(key)
    picked = chosen[:, :PATCH_DOM * TILE]
    mapped = jax.vmap(lambda table, tile_indices: table[tile_indices])(shuffle, picked)
    return mapped.reshape(PATCHES, TILE).astype(jnp.int32)


def draw_shared_left(key, part):
    shuffle, chosen = node_layout(key)
    return shuffle[:, :SH].astype(jnp.int32)


def draw_shared_right(key, part):
    shuffle, chosen = node_layout(key)
    start = 7 * EX * (7 * EY + 1)
    return shuffle[:, start:start + SH].astype(jnp.int32)


def block_scale(key, shape, pieces, smallest, high):
    def one(position, shards_of):
        steps = jax.random.uniform(jax.random.fold_in(jax.random.fold_in(key, 6), position), (shards_of,), jnp.float32, smallest / len(pieces), high / len(pieces))
        return jnp.repeat(jnp.exp(steps), shape[position] // shards_of).reshape((-1,) + (1,) * (len(shape) - position - 1))

    factor_of = one(*pieces[0])
    for cut in pieces[1:]:
        factor_of = factor_of * one(*cut)
    return factor_of


def centred(stream_key, extent, spread, most, split=(), kind=jnp.bfloat16):
    drawn = spread * jax.random.normal(stream_key, extent, jnp.float32)
    if split:
        drawn = drawn * block_scale(stream_key, extent, split, -0.22, 0.18)
    return jnp.clip(drawn, -most, most).astype(kind)


def setup_inputs(seed: int = 0) -> dict:
    arg_keys = jax.random.split(jax.random.key(seed), 21)
    pd_disp = centred(arg_keys[0], (TILES, 2, TILE), 0.3, 4.0, ((0, 512),), jnp.float32)
    pd_vel = centred(arg_keys[1], (TILES, 2, TILE), 0.3, 4.0, ((0, 512),), jnp.float32)
    pd_coord = centred(arg_keys[2], (TILES, 2, TILE), 1.0, 4.0, ((0, 512),), jnp.float32)
    pd_modulus = jnp.clip(jnp.exp(math.log(20.0) - 2.3025851 * jax.random.uniform(arg_keys[3], (TILES, TILE), jnp.float32) ** block_scale(arg_keys[3], (TILES, TILE), ((0, 512),), -0.2, 0.2)), 2.0, 20.0)
    pd_step = jnp.clip(jnp.exp(math.log(0.3) - 2.3025852 * jax.random.uniform(arg_keys[4], (TILES, TILE), jnp.float32) ** block_scale(arg_keys[4], (TILES, TILE), ((0, 512),), -0.2, 0.2)), 0.03, 0.3)
    family_tile_lists = draw_family_tile_lists(jax.random.fold_in(arg_keys[20], 71), 0)
    live_tiles = draw_live_tiles(jax.random.fold_in(arg_keys[20], 71), 0)
    patch_tile = draw_patch_tile(jax.random.fold_in(arg_keys[20], 71), 0)
    patch_blend = jnp.clip(0.1 + 0.79999997 * jax.random.uniform(arg_keys[8], (PATCHES, TILE), jnp.float32) ** block_scale(arg_keys[8], (PATCHES, TILE), ((0, 256),), -0.2, 0.2), 0.1, 0.9)
    patch_nodes = draw_patch_nodes(jax.random.fold_in(arg_keys[20], 71), 0)
    patch_matrix = centred(arg_keys[10], (PATCHES, TILE, TILE), TILE ** -0.5, 0.5, ((0, 512),), jnp.float32)
    fe_disp = centred(arg_keys[11], (2, NODES), 0.3, 4.0, ((1, 512),), jnp.float32)
    fe_vel = centred(arg_keys[12], (2, NODES), 0.3, 4.0, ((1, 512),), jnp.float32)
    fe_step = jnp.clip(jnp.exp(math.log(0.3) - 2.3025852 * jax.random.uniform(arg_keys[13], (NODES,), jnp.float32) ** block_scale(arg_keys[13], (NODES,), ((0, 512),), -0.2, 0.2)), 0.03, 0.3)
    fe_modulus = jnp.clip(jnp.exp(math.log(2.0) - 1.3862944 * jax.random.uniform(arg_keys[14], (ELEMS,), jnp.float32) ** block_scale(arg_keys[14], (ELEMS,), ((0, 512),), -0.2, 0.2)), 0.5, 2.0)
    element_nodes = draw_element_nodes(jax.random.fold_in(arg_keys[20], 71), 0)
    shape_grad = centred(arg_keys[16], (2, 64, 64), 64 ** -0.5, 0.75, (), jnp.float32)
    quad_weight = jnp.clip(jnp.exp(jax.random.uniform(arg_keys[17], (64,), jnp.float32, math.log(0.5), math.log(2.0))), 0.5, 2.0)
    shared_left = draw_shared_left(jax.random.fold_in(arg_keys[20], 71), 0)
    shared_right = draw_shared_right(jax.random.fold_in(arg_keys[20], 71), 0)
    return {"pd_disp": pd_disp, "pd_vel": pd_vel, "pd_coord": pd_coord, "pd_modulus": pd_modulus, "pd_step": pd_step, "family_tile_lists": family_tile_lists, "live_tiles": live_tiles, "patch_tile": patch_tile, "patch_blend": patch_blend, "patch_nodes": patch_nodes, "patch_matrix": patch_matrix, "fe_disp": fe_disp, "fe_vel": fe_vel, "fe_step": fe_step, "fe_modulus": fe_modulus, "element_nodes": element_nodes, "shape_grad": shape_grad, "quad_weight": quad_weight, "shared_left": shared_left, "shared_right": shared_right}


time_step = 0.5
horizon_sq = 2.0
core_sq = 0.01
stretch_scale = 0.3
group_size = 16

def bond_terms(x_own, u_own, x_far, u_far):
    offset = x_far[:, :, None, :] - x_own[None, :, :, None]
    deformed = offset + u_far[:, :, None, :] - u_own[None, :, :, None]
    rest_sq = lax.optimization_barrier(jnp.sum(offset * offset, axis=1))
    rest_len = jnp.sqrt(rest_sq + core_sq)
    length = jnp.sqrt(lax.optimization_barrier(jnp.sum(deformed * deformed, axis=1)) + core_sq)
    stretch = length - rest_len
    ratio = stretch / stretch_scale
    influence = jnp.exp(-rest_sq / horizon_sq) / (1.0 + ratio * ratio)
    return (deformed, length, rest_len, stretch, influence)

def dilatation(x_own, u_own, x_far, u_far):
    deformed, length, rest_len, stretch, influence = bond_terms(x_own, u_own, x_far, u_far)
    point_volume = lax.optimization_barrier(jnp.sum(influence * rest_len * rest_len, axis=(0, 2)))
    volumetric_dilatation = 2.0 * lax.optimization_barrier(jnp.sum(influence * rest_len * stretch, axis=(0, 2))) / point_volume
    return (volumetric_dilatation, point_volume)

def bond_force(x_own, u_own, x_far, u_far, k_own, th_own, m_own, k_far, th_far, m_far):
    deformed, length, rest_len, stretch, influence = bond_terms(x_own, u_own, x_far, u_far)
    ko, to, mo = (k_own[None, :, None], th_own[None, :, None], m_own[None, :, None])
    kf, tf, mf = (k_far[:, None, :], th_far[:, None, :], m_far[:, None, :])
    t_own = influence * (2.0 * ko * to * rest_len / mo + 4.0 * ko * (stretch - 0.5 * to * rest_len) / mo)
    t_far = influence * (2.0 * kf * tf * rest_len / mf + 4.0 * kf * (stretch - 0.5 * tf * rest_len) / mf)
    scalar = (t_own + t_far) / length
    return lax.optimization_barrier(jnp.sum(scalar[:, None] * deformed, axis=(0, 3)))

def element_force(disp_el, modulus, shape_grad, quad_weight):
    precise = lax.Precision.HIGHEST
    grad = jnp.einsum('aqn,cne->caqe', shape_grad, disp_el, precision=precise)
    strain_xx = grad[0, 0]
    strain_yy = grad[1, 1]
    strain_xy = 0.5 * (grad[0, 1] + grad[1, 0])
    stiffen = 1.0 + strain_xx * strain_xx + strain_yy * strain_yy + 2.0 * strain_xy * strain_xy
    scaled = modulus[None, :] * quad_weight[:, None] * stiffen
    trace_sum = strain_xx + strain_yy
    s_xx = scaled * (trace_sum + 2.0 * strain_xx)
    s_yy = scaled * (trace_sum + 2.0 * strain_yy)
    s_xy = scaled * 2.0 * strain_xy
    stress = jnp.stack([jnp.stack([s_xx, s_xy]), jnp.stack([s_xy, s_yy])])
    return jnp.einsum('aqn,caqe->cne', shape_grad, stress, precision=precise)

def reference(pd_disp, pd_vel, pd_coord, pd_modulus, pd_step, family_tile_lists, live_tiles, patch_tile, patch_blend, patch_nodes, patch_matrix, fe_disp, fe_vel, fe_step, fe_modulus, element_nodes, shape_grad, quad_weight, shared_left, shared_right):
    precise = lax.Precision.HIGHEST
    tile_dom = jnp.arange(TILES, dtype=jnp.int32) // PT
    alive = (jnp.arange(TILES, dtype=jnp.int32) % PT < live_tiles[tile_dom]).astype(jnp.float32)
    far_index = family_tile_lists + (tile_dom * PT)[:, None]
    patch_dom = jnp.arange(PATCHES, dtype=jnp.int32) // PATCH_DOM
    patch_global = patch_tile + patch_dom * PT
    node_global = patch_nodes + (patch_dom * NODE_DEV)[:, None]
    elem_global = element_nodes + (jnp.arange(ELEMS, dtype=jnp.int32) // (EX * EY) * NODE_DEV)[None, :]
    dom_base = (jnp.arange(N_DOM, dtype=jnp.int32) * NODE_DEV)[:, None]
    left_global = shared_left + dom_base
    right_global = shared_right + dom_base
    coord_pad = jnp.pad(pd_coord, ((PT, PT), (0, 0), (0, 0)))
    modulus_pad = jnp.pad(pd_modulus, ((PT, PT), (0, 0)))
    tile_groups = jnp.arange(TILES, dtype=jnp.int32).reshape(-1, group_size)
    for section in range(2):
        picked = fe_disp[:, node_global]
        target = jnp.einsum('qpn,cqn->qcp', patch_matrix, picked, precision=precise)
        current = pd_disp[patch_global]
        blended = pd_disp.at[patch_global].add(patch_blend[:, None, :] * (target - current))
        disp_pad = jnp.pad(blended, ((PT, PT), (0, 0), (0, 0)))

        def dilatation_per_group(tile_indices):

            def single(tile_number):
                far = far_index[tile_number]
                return dilatation(coord_pad[PT + tile_number], disp_pad[PT + tile_number], coord_pad[far], disp_pad[far])
            return jax.vmap(single)(tile_indices)
        volumetric_dilatation, point_volume = lax.map(dilatation_per_group, tile_groups)
        volumetric_dilatation = volumetric_dilatation.reshape(TILES, TILE)
        point_volume = point_volume.reshape(TILES, TILE)
        theta_pad = jnp.pad(volumetric_dilatation, ((PT, PT), (0, 0)))
        volume_pad = jnp.pad(point_volume, ((PT, PT), (0, 0)), constant_values=1.0)

        def force_group(tile_indices):

            def single(tile_number):
                far = far_index[tile_number]
                own = PT + tile_number
                return bond_force(coord_pad[own], disp_pad[own], coord_pad[far], disp_pad[far], modulus_pad[own], theta_pad[own], volume_pad[own], modulus_pad[far], theta_pad[far], volume_pad[far])
            return jax.vmap(single)(tile_indices)
        pd_force = lax.map(force_group, tile_groups).reshape(TILES, 2, TILE)
        pd_force = pd_force * alive[:, None, None]
        pd_vel = (pd_vel + pd_step[:, None, :] * pd_force) * alive[:, None, None]
        new_disp = (blended + time_step * pd_vel) * alive[:, None, None]
        disp_el = fe_disp[:, elem_global]
        forces_el = element_force(disp_el, fe_modulus, shape_grad, quad_weight)
        nodal = jnp.zeros((2, NODES), jnp.float32).at[:, elem_global.reshape(-1)].add(forces_el.reshape(2, -1))
        nodal = -nodal
        weighted = pd_force[patch_global] * patch_blend[:, None, :]
        reaction = jnp.einsum('qpn,qcp->cqn', patch_matrix, weighted, precision=precise)
        nodal = nodal.at[:, node_global.reshape(-1)].add(reaction.reshape(2, -1))
        left_vals = nodal[:, left_global]
        right_vals = nodal[:, right_global]
        zeros_row = jnp.zeros((2, 1, SH), jnp.float32)
        from_prev = jnp.concatenate([zeros_row, right_vals[:, :-1]], axis=1)
        from_next = jnp.concatenate([left_vals[:, 1:], zeros_row], axis=1)
        nodal = nodal.at[:, left_global].add(from_prev).at[:, right_global].add(from_next)
        fe_vel = fe_vel + fe_step[None, :] * nodal
        fe_disp = fe_disp + time_step * fe_vel
        pd_disp = new_disp
    return (pd_disp, pd_vel, fe_disp, fe_vel)
```

```python
import functools

import jax
import jax.numpy as jnp
from jax import lax
from jax.experimental import pallas as pl
from jax.experimental.pallas import tpu as pltpu
from jax.sharding import PartitionSpec as P

MESH = pl.DeviceIdType.MESH
F32 = jnp.float32
BF16 = jnp.bfloat16
I32 = jnp.int32
EXACT = lax.Precision.HIGHEST

TIME_STEP = 0.5
CORE_SQ = 0.01
STRETCH = 0.3

LO = 256
HALF_ROWS = 25
PAD_ROWS = 32
CHUNK = 8
N_COPIES = 34


def split2(x):
    top = x.astype(BF16)
    return top, (x - top.astype(F32)).astype(BF16)


def nt(a, b, **kw):
    return lax.dot_general(
        a, b, (((1,), (1,)), ((), ())), preferred_element_type=F32, **kw
    )


def kernel(
    n_dom,
    disp,
    vel,
    coord,
    modulus,
    step,
    family,
    live,
    ptile,
    pblend,
    pnodes,
    pmat,
    fdisp,
    fvel,
    fstep,
    fmod,
    enodes,
    sgrad,
    qweight,
    sleft,
    sright,
    disp_out,
    vel_out,
    fdisp_out,
    fvel_out,
    pdx,
    ub0,
    ub1,
    st0,
    st1,
    pm,
    table,
    speed,
    split_table,
    onehot,
    hrow,
    ids,
    link,
    del_,
    fel,
    sgt,
    acc,
    bonds,
    sums,
    cur,
    pel_send,
    pel_recv,
    late_send,
    late_recv,
    bd_send,
    bd_recv,
    ssem,
    rsem,
):
    d = lax.axis_index("dom")
    b = lax.axis_index("blk")
    o = 1 - b
    left = lax.rem(d + n_dom - 1, n_dom)
    right = lax.rem(d + 1, n_dom)
    peers = ((d, o), (left, 0), (left, 1), (right, 0), (right, 1))

    barrier = pltpu.get_barrier_semaphore()
    for peer in peers:
        pl.semaphore_signal(barrier, inc=1, device_id=peer, device_id_type=MESH)

    started = []

    def send(src, dst, ssem_at, rsem_at, peer):
        copy = pltpu.make_async_remote_copy(
            src_ref=src,
            dst_ref=dst,
            send_sem=ssem.at[ssem_at],
            recv_sem=rsem.at[rsem_at],
            device_id=peer,
            device_id_type=MESH,
        )
        copy.start()
        started.append(copy)

    def arrived(dst, rsem_at):
        pltpu.make_async_remote_copy(
            src_ref=dst,
            dst_ref=dst,
            send_sem=ssem.at[0],
            recv_sem=rsem.at[rsem_at],
            device_id=(d, o),
            device_id_type=MESH,
        ).wait_recv()

    own = 4 + 2 * b
    theirs = 4 + 2 * o

    for t in range(2):
        pdx[own + t] = jnp.concatenate(
            [
                coord[t],
                modulus[t : t + 1, :],
                disp[t],
                pnodes[...].astype(F32),
                jnp.zeros((2, 128), F32),
            ],
            axis=0,
        )
    table[b, 24:32, :] = jnp.zeros((8, LO), F32)
    table[b, 56:64, :] = jnp.zeros((8, LO), F32)
    for r in range(HALF_ROWS):
        lanes = slice(r * LO, (r + 1) * LO)
        table[b, r : r + 1, :] = fdisp[0:1, lanes]
        table[b, PAD_ROWS + r : PAD_ROWS + r + 1, :] = fdisp[1:2, lanes]
    pl.semaphore_wait(barrier, 5)

    send(table.at[b], table.at[b], 0, 0, (d, o))
    slots = (own, 8 + 2 * b, 8 + 2 * b, 2 * b, 2 * b)
    marks = (0, 3 + b, 3 + b, 1 + b, 1 + b)
    for j in range(5):
        send(
            pdx.at[pl.ds(own, 2)],
            pdx.at[pl.ds(slots[j], 2)],
            3 + j,
            3 + marks[j],
            peers[j],
        )
    send(pmat.at[0], pm.at[b], 1, 1, (d, o))
    sources = (theirs, 0, 2, 8, 10)

    speed[b, 24:32, :] = jnp.zeros((8, LO), F32)
    speed[b, 56:64, :] = jnp.zeros((8, LO), F32)
    speed[b, 88:96, :] = jnp.zeros((8, LO), F32)
    for r in range(HALF_ROWS):
        lanes = slice(r * LO, (r + 1) * LO)
        speed[b, r : r + 1, :] = fvel[0:1, lanes]
        speed[b, PAD_ROWS + r : PAD_ROWS + r + 1, :] = fvel[1:2, lanes]
        speed[b, 2 * PAD_ROWS + r : 2 * PAD_ROWS + r + 1, :] = fstep[0:1, lanes]
    send(speed.at[b], speed.at[b], 2, 2, (d, o))
    pm[b] = pmat[0]
    states = (started[0], started.pop())
    del started[0]

    lo_iota = lax.broadcasted_iota(I32, (LO, 128), 0)

    def table_row(node):
        hi = lax.shift_right_arithmetic(node, 8)
        return jnp.where(hi >= HALF_ROWS, hi + (PAD_ROWS - HALF_ROWS), hi)

    def onehot_of(lo_row):
        return jnp.where(
            lo_iota == jnp.broadcast_to(lo_row, (LO, 128)), 1.0, 0.0
        ).astype(BF16)

    @pl.loop(0, 64 // CHUNK)
    def _(i):
        node = enodes[pl.ds(pl.multiple_of(i * CHUNK, CHUNK), CHUNK), :]
        hrow[pl.ds(pl.multiple_of(i * CHUNK, CHUNK), CHUNK), :] = table_row(node)
        lo = lax.bitwise_and(node, LO - 1)
        base = pl.multiple_of(i * (CHUNK * 128), CHUNK * 128)
        for g in range(CHUNK):
            onehot[:, pl.ds(base + g * 128, 128)] = onehot_of(lo[g : g + 1, :])

    sgt[...] = sgrad[...].T
    eye = lax.broadcasted_iota(I32, (64, 64), 0) == lax.broadcasted_iota(
        I32, (64, 64), 1
    )
    weight = jnp.sum(
        jnp.where(eye, jnp.broadcast_to(qweight[...], (64, 64)), 0.0),
        axis=1,
        keepdims=True,
    )
    scale = weight * fmod[...]

    for j in range(5):
        arrived(pdx.at[pl.ds(sources[j], 2)], 3 + j)

    ids[...] = jnp.full((8, 128), -1, I32)
    ids[pl.ds(b, 1), :] = pnodes[...]
    ids[pl.ds(o, 1), :] = pdx[theirs, 5:6, :].astype(I32)
    ids[2:3, 0:113] = sleft[...]
    ids[3:4, 0:113] = sright[...]
    few = ids[...]
    hrow[64:72, :] = table_row(few)
    few_lo = lax.bitwise_and(few, LO - 1)
    for g in range(4):
        onehot[:, 8192 + g * 128 : 8320 + g * 128] = onehot_of(few_lo[g : g + 1, :])
    few_f = few.astype(F32)
    few_t = few_f.T
    for q in range(2):
        for side in range(2):
            link[q * 128 : (q + 1) * 128, side * 128 : (side + 1) * 128] = jnp.where(
                few_t[:, q : q + 1] == few_f[2 + side : 3 + side, :], 1.0, 0.0
            ).astype(BF16)

    OX, OY, REST, INFL0, NX, NY, STR, INFL = range(8)

    @pl.loop(0, 6)
    def _(p):
        t = p // 3
        far = pdx[family[t, p - 3 * t]]
        far_t = far.T
        me = pdx[own + t]
        ox = far_t[:, 0:1] - me[0:1, :]
        oy = far_t[:, 1:2] - me[1:2, :]
        r2 = ox * ox + oy * oy
        bonds[OX, p] = ox
        bonds[OY, p] = oy
        bonds[REST, p] = jnp.sqrt(r2 + CORE_SQ)
        bonds[INFL0, p] = jnp.exp(-0.5 * r2)

    cur[...] = vel[...]
    row_iota = lax.broadcasted_iota(I32, (64, 128), 0)

    def masked_rows(product, row):
        both = product[0:128] + product[128:256]
        hit = row_iota == jnp.broadcast_to(row, (64, 128))
        out = []
        for c in range(2):
            x = jnp.where(hit[0:32], both[c * 32 : c * 32 + 32], 0.0)
            x = x + jnp.where(hit[32:64], both[64 + c * 32 : 96 + c * 32], 0.0)
            out.append(jnp.sum(x, axis=0, keepdims=True))
        return out

    def spread(values, row):
        hit = row_iota == jnp.broadcast_to(row, (64, 128))
        blocks = []
        for part in range(2):
            wide = [
                jnp.where(hit, jnp.broadcast_to(values[part][c], (64, 128)), 0.0)
                for c in range(2)
            ]
            for half in range(2):
                for c in range(2):
                    blocks.append(wide[c][half * 32 : half * 32 + 32])
        return jnp.concatenate(blocks, axis=0).astype(BF16)

    for s in range(2):
        ub, st = (ub0, ub1)[s], (st0, st1)[s]
        base = 8 + 13 * s
        if s == 0:
            arrived(table.at[o], 0)
            arrived(pm.at[o], 1)

        top, low = split2(table[...].reshape(128, LO))
        split_table[0:128, :] = top
        split_table[128:256, :] = low
        product = jnp.dot(
            split_table[...], onehot[:, 8192:8448], preferred_element_type=F32
        )
        targets = []
        for q in range(2):
            picked = masked_rows(
                product[:, q * 128 : (q + 1) * 128], hrow[64 + q : 65 + q, :]
            )
            picked = jnp.concatenate(picked + [jnp.zeros((6, 128), F32)], axis=0)
            targets.append(nt(picked, pm[q], precision=EXACT)[0:2, :])
        for k in range(4):
            if s == 0:
                u = pdx[4 + k, 3:5, :]
            else:
                t = k % 2
                mine = ub[4 + k]
                u = mine
            new = u
            for q in range(2):
                hit = jnp.full((2, 128), ptile[q], I32) == k
                new = jnp.where(
                    hit, u + pblend[q : q + 1, :] * (targets[q] - u), new
                )
            ub[4 + k] = new
        send(ub.at[pl.ds(4, 4)], ub.at[pl.ds(8, 4)], base, base + 1, (left, b))
        send(ub.at[pl.ds(4, 4)], ub.at[pl.ds(0, 4)], base + 1, base, (right, b))

        @pl.loop(0, 64 // CHUNK)
        def _(i):
            rows = pl.ds(pl.multiple_of(i * CHUNK, CHUNK), CHUNK)
            lanes = pl.ds(pl.multiple_of(i * (CHUNK * 128), CHUNK * 128), CHUNK * 128)
            product = jnp.dot(
                split_table[...], onehot[:, lanes], preferred_element_type=F32
            )
            row = hrow[rows, :]
            found = [
                masked_rows(product[:, g * 128 : (g + 1) * 128], row[g : g + 1, :])
                for g in range(CHUNK)
            ]
            for c in range(2):
                del_[rows, c * 128 : (c + 1) * 128] = jnp.concatenate(
                    [f[c] for f in found], axis=0
                )

        arrived(ub.at[pl.ds(0, 4)], base)
        arrived(ub.at[pl.ds(8, 4)], base + 1)

        @pl.loop(0, 6)
        def _(p):
            t = p // 3
            far = ub[family[t, p - 3 * t]]
            far_t = jnp.concatenate([far, jnp.zeros((6, 128), F32)], axis=0).T
            me = ub[own + t]
            yx = bonds[OX, p] + (far_t[:, 0:1] - me[0:1, :])
            yy = bonds[OY, p] + (far_t[:, 1:2] - me[1:2, :])
            y2 = yx * yx + yy * yy + CORE_SQ
            length = jnp.sqrt(y2)
            inverse = 1.0 / length
            rest = bonds[REST, p]
            stretch = length - rest
            ratio = stretch * (1.0 / STRETCH)
            influence = bonds[INFL0, p] / (1.0 + ratio * ratio)
            bonds[NX, p] = yx * inverse
            bonds[NY, p] = yy * inverse
            bonds[STR, p] = stretch
            bonds[INFL, p] = influence
            weighted = influence * rest
            sums[p] = jnp.concatenate(
                [
                    jnp.sum(weighted * stretch, axis=0, keepdims=True),
                    jnp.sum(weighted * rest, axis=0, keepdims=True),
                ],
                axis=0,
            )

        for t in range(2):
            total = sums[3 * t] + sums[3 * t + 1] + sums[3 * t + 2]
            volume = total[1:2, :]
            st[own + t] = jnp.concatenate(
                [2.0 * total[0:1, :] / volume, volume], axis=0
            )
        for j in range(5):
            send(
                st.at[pl.ds(own, 2)],
                st.at[pl.ds(slots[j], 2)],
                base + 2 + j,
                base + 2 + marks[j],
                peers[j],
            )

        grad = jnp.dot(sgrad[...], del_[...], precision=EXACT, preferred_element_type=F32)
        exx = grad[0:64, 0:128]
        eyy = grad[64:128, 128:256]
        exy = 0.5 * (grad[64:128, 0:128] + grad[0:64, 128:256])
        scaled = scale * (1.0 + exx * exx + eyy * eyy + 2.0 * exy * exy)
        both = exx + eyy
        sxx = scaled * (both + 2.0 * exx)
        syy = scaled * (both + 2.0 * eyy)
        sxy = scaled * 2.0 * exy
        stress = jnp.concatenate(
            [
                jnp.concatenate([sxx, sxy], axis=1),
                jnp.concatenate([sxy, syy], axis=1),
            ],
            axis=0,
        )
        fel[...] = jnp.dot(sgt[...], stress, precision=EXACT, preferred_element_type=F32)
        acc[...] = jnp.zeros((256, LO), F32)

        @pl.loop(0, 64 // CHUNK)
        def _(i):
            rows = pl.ds(pl.multiple_of(i * CHUNK, CHUNK), CHUNK)
            lanes = pl.ds(pl.multiple_of(i * (CHUNK * 128), CHUNK * 128), CHUNK * 128)
            row = hrow[rows, :]
            f = fel[rows, :]
            f_top = f.astype(BF16).astype(F32)
            f_low = f - f_top
            left_side = jnp.concatenate(
                [
                    spread(
                        [
                            [x[g : g + 1, 0:128], x[g : g + 1, 128:256]]
                            for x in (f_top, f_low)
                        ],
                        row[g : g + 1, :],
                    )
                    for g in range(CHUNK)
                ],
                axis=1,
            )
            acc[...] += nt(left_side, onehot[:, lanes])

        partial = acc[0:128, :] + acc[128:256, :]
        pel_send[s] = partial
        if s == 0:
            send(pel_send.at[s], pel_recv.at[s], base + 7, base + 7, (d, o))
        else:
            cut = pl.ds(o * 64, 64)
            send(
                pel_send.at[s, cut], pel_recv.at[s, cut], base + 7, base + 7, (d, o)
            )
        top, low = split2(partial)
        product = jnp.dot(
            jnp.concatenate([top, low], axis=0),
            onehot[:, 8448:8704],
            preferred_element_type=F32,
        )
        border = []
        for side in range(2):
            found = masked_rows(
                product[:, side * 128 : (side + 1) * 128],
                hrow[66 + side : 67 + side, :],
            )
            border.append(jnp.concatenate(found, axis=0))

        for j in range(5):
            arrived(st.at[pl.ds(sources[j], 2)], base + 2 + j)

        def coefficients(k, state):
            theta, volume = state[0:1, :], state[1:2, :]
            return 2.0 * k * theta / volume, 4.0 * k / volume, 0.5 * theta

        @pl.loop(0, 6)
        def _(p):
            t = p // 3
            j = family[t, p - 3 * t]
            fa, fb, fc = coefficients(pdx[j][2:3, :], st[j])
            far_t = jnp.concatenate([fa, fb, fc, jnp.zeros((5, 128), F32)], axis=0).T
            oa, ob, oc = coefficients(pdx[own + t][2:3, :], st[own + t])
            rest = bonds[REST, p]
            stretch = bonds[STR, p]
            near = oa * rest + ob * (stretch - oc * rest)
            away = far_t[:, 0:1] * rest + far_t[:, 1:2] * (stretch - far_t[:, 2:3] * rest)
            force = bonds[INFL, p] * (near + away)
            sums[p] = jnp.concatenate(
                [
                    jnp.sum(force * bonds[NX, p], axis=0, keepdims=True),
                    jnp.sum(force * bonds[NY, p], axis=0, keepdims=True),
                ],
                axis=0,
            )

        forces, moved = [], []
        for t in range(2):
            alive = jnp.full((2, 128), 2 * b + t, I32) < live[0]
            total = sums[3 * t] + sums[3 * t + 1] + sums[3 * t + 2]
            force = jnp.where(alive, total, 0.0)
            forces.append(force)
            v = jnp.where(alive, cur[t] + step[t : t + 1, :] * force, 0.0)
            u = jnp.where(alive, ub[own + t] + TIME_STEP * v, 0.0)
            cur[t] = v
            moved.append(u)

        reaction = []
        for q in range(2):
            w = jnp.zeros((2, 128), F32)
            for t in range(2):
                hit = jnp.full((2, 128), ptile[q], I32) == 2 * b + t
                w = w + jnp.where(hit, pblend[q : q + 1, :] * forces[t], 0.0)
            w = jnp.concatenate([w, jnp.zeros((6, 128), F32)], axis=0)
            reaction.append(
                jnp.dot(w, pm[q], precision=EXACT, preferred_element_type=F32)[0:2, :]
            )
        late = jnp.concatenate(reaction + moved, axis=0)
        late_send[s] = late
        send(late_send.at[s], late_recv.at[s], base + 8, base + 8, (d, o))
        wide = jnp.concatenate(reaction, axis=1)
        top, low = split2(wide)
        met = jnp.dot(
            jnp.concatenate([top, low, jnp.zeros((12, 256), BF16)], axis=0),
            link[...],
            preferred_element_type=F32,
        )
        met = met[0:2, :] + met[2:4, :]
        for side in range(2):
            bd_send[s, side] = met[:, side * 128 : (side + 1) * 128] - border[side]
        for j in range(4):
            side = j // 2
            send(
                bd_send.at[s, side],
                bd_recv.at[s, 2 * (1 - side) + b],
                base + 9 + j,
                base + 9 + 2 * (1 - side) + b,
                peers[1 + j],
            )
        if s == 0:
            for t in range(2):
                ub1[own + t] = moved[t]
        else:
            for t in range(2):
                disp_out[t] = moved[t]
                vel_out[t] = cur[t]

        arrived(late_recv.at[s], base + 8)
        other = late_recv[s]
        if s == 0:
            for t in range(2):
                ub1[theirs + t] = other[4 + 2 * t : 6 + 2 * t, :]
        for j in range(4):
            arrived(bd_recv.at[s, j], base + 9 + j)
        shared = [
            jnp.where(
                jnp.full((2, 128), d, I32) > 0, bd_recv[s, 0] + bd_recv[s, 1], 0.0
            ),
            jnp.where(
                jnp.full((2, 128), d, I32) < n_dom - 1,
                bd_recv[s, 2] + bd_recv[s, 3],
                0.0,
            ),
        ]
        sides = []
        for g, x in enumerate(
            [late[0:2, :] + other[0:2, :], late[2:4, :] + other[2:4, :]] + shared
        ):
            x_top = x.astype(BF16).astype(F32)
            x_low = x - x_top
            sides.append(
                spread(
                    [[y[0:1, :], y[1:2, :]] for y in (x_top, x_low)],
                    hrow[64 + g : 65 + g, :],
                )
            )
        extra = nt(jnp.concatenate(sides, axis=1), onehot[:, 8192:8704])
        acc[0:128, :] = extra[0:128, :] + extra[128:256, :]
        if s == 0:
            arrived(speed.at[o], 2)
            arrived(pel_recv.at[s], base + 7)
            for copy in states:
                copy.wait_send()
        else:
            arrived(pel_recv.at[s, pl.ds(b * 64, 64)], base + 7)
        for h in range(2) if s == 0 else (b,):
            for c in range(2):
                cut = pl.ds(h * 64 + c * 32, 32)
                rows = slice(c * 32, c * 32 + 32)
                nodal = acc[cut, :] - (pel_send[s, cut, :] + pel_recv[s, cut, :])
                v = speed[h, rows, :] + speed[h, 64:96, :] * nodal
                speed[h, rows, :] = v
                table[h, rows, :] = table[h, rows, :] + TIME_STEP * v

    for r in range(HALF_ROWS):
        lanes = slice(r * LO, (r + 1) * LO)
        for c in range(2):
            at = PAD_ROWS * c + r
            fdisp_out[c : c + 1, lanes] = table[b, at : at + 1, :]
            fvel_out[c : c + 1, lanes] = speed[b, at : at + 1, :]
    for copy in started:
        copy.wait_send()


def shards(n_dom, *args):
    (
        pd_disp,
        pd_vel,
        pd_coord,
        pd_modulus,
        pd_step,
        family,
        live,
        patch_tile,
        patch_blend,
        patch_nodes,
        patch_matrix,
        fe_disp,
        fe_vel,
        fe_step,
        fe_modulus,
        element_nodes,
        shape_grad,
        quad_weight,
        shared_left,
        shared_right,
    ) = args
    vmem = pl.BlockSpec(memory_space=pltpu.VMEM)
    smem = pl.BlockSpec(memory_space=pltpu.SMEM)
    in_specs = [vmem] * 20
    for at in (5, 6, 7):
        in_specs[at] = smem

    def f32(*shape):
        return pltpu.VMEM(shape, F32)

    return pl.pallas_call(
        functools.partial(kernel, n_dom),
        out_shape=[
            jax.ShapeDtypeStruct(pd_disp.shape, F32),
            jax.ShapeDtypeStruct(pd_vel.shape, F32),
            jax.ShapeDtypeStruct(fe_disp.shape, F32),
            jax.ShapeDtypeStruct(fe_vel.shape, F32),
        ],
        in_specs=in_specs,
        out_specs=[vmem] * 4,
        scratch_shapes=[
            f32(12, 8, 128),
            f32(12, 2, 128),
            f32(12, 2, 128),
            f32(12, 2, 128),
            f32(12, 2, 128),
            f32(2, 128, 128),
            f32(2, 64, LO),
            f32(2, 96, LO),
            pltpu.VMEM((256, LO), BF16),
            pltpu.VMEM((LO, 8704), BF16),
            pltpu.VMEM((72, 128), I32),
            pltpu.VMEM((8, 128), I32),
            pltpu.VMEM((256, 256), BF16),
            f32(64, 256),
            f32(64, 256),
            f32(64, 128),
            f32(256, LO),
            f32(8, 6, 128, 128),
            f32(6, 2, 128),
            f32(2, 2, 128),
            f32(2, 128, LO),
            f32(2, 128, LO),
            f32(2, 8, 128),
            f32(2, 8, 128),
            f32(2, 2, 2, 128),
            f32(2, 4, 2, 128),
            pltpu.SemaphoreType.DMA((N_COPIES,)),
            pltpu.SemaphoreType.DMA((N_COPIES,)),
        ],
        compiler_params=pltpu.CompilerParams(
            collective_id=0, has_side_effects=True, vmem_limit_bytes=40 * 2**20
        ),
    )(
        pd_disp,
        pd_vel,
        pd_coord,
        pd_modulus,
        pd_step,
        family,
        live,
        patch_tile,
        patch_blend,
        patch_nodes,
        patch_matrix,
        fe_disp,
        fe_vel,
        fe_step.reshape(1, -1),
        fe_modulus.reshape(1, -1),
        element_nodes,
        shape_grad.reshape(-1, shape_grad.shape[2]),
        quad_weight.reshape(1, -1),
        shared_left,
        shared_right,
    )


def solution(mesh):
    both = ("dom", "blk")
    return jax.shard_map(
        functools.partial(shards, mesh.shape["dom"]),
        mesh=mesh,
        in_specs=(
            P(both, None, None),
            P(both, None, None),
            P(both, None, None),
            P(both, None),
            P(both, None),
            P(both, None),
            P("dom"),
            P("dom"),
            P("dom", None),
            P(both, None),
            P(both, None, None),
            P(None, both),
            P(None, both),
            P(both),
            P(both),
            P(None, both),
            P(),
            P(),
            P("dom", None),
            P("dom", None),
        ),
        out_specs=(
            P(both, None, None),
            P(both, None, None),
            P(None, both),
            P(None, both),
        ),
        check_vma=False,
    )
```

```python
import functools

import jax
import jax.numpy as jnp
from jax import lax
from jax.experimental import pallas as pl
from jax.experimental.pallas import tpu as pltpu
from jax.sharding import PartitionSpec as P

MESH = pl.DeviceIdType.MESH
F32 = jnp.float32
BF16 = jnp.bfloat16
I32 = jnp.int32
EXACT = lax.Precision.HIGHEST

TIME_STEP = 0.5
CORE_SQ = 0.01
STRETCH = 0.3

LO = 256
HALF_ROWS = 25
PAD_ROWS = 32
CHUNK = 8
N_COPIES = 34
VMEM_BYTES = 60 * 2**20


def split2(x):
    top = x.astype(BF16)
    return top, (x - top.astype(F32)).astype(BF16)


def nt(a, b, **kw):
    return lax.dot_general(
        a, b, (((1,), (1,)), ((), ())), preferred_element_type=F32, **kw
    )


def kernel(
    n_dom,
    disp_in,
    vel_in,
    coord_in,
    modulus_in,
    step_in,
    family_in,
    live_in,
    ptile_in,
    pblend_in,
    pnodes_in,
    pmat_in,
    fdisp_in,
    fvel_in,
    fstep_in,
    fmod_in,
    enodes_in,
    sgrad_in,
    qweight_in,
    sleft_in,
    sright_in,
    disp_out,
    vel_out,
    fdisp_out,
    fvel_out,
    disp,
    vel,
    coord,
    modulus,
    step,
    family,
    live,
    ptile,
    pblend,
    pnodes,
    fdisp,
    fvel,
    fstep,
    fmod,
    enodes,
    sgrad,
    qweight,
    sleft,
    sright,
    pdx,
    ub0,
    ub1,
    st0,
    st1,
    pm,
    table,
    speed,
    split_table,
    onehot,
    hrow,
    ids,
    link,
    del_,
    fel,
    sgt,
    acc,
    bonds,
    sums,
    cur,
    pel_send,
    pel_recv,
    late_send,
    late_recv,
    bd_send,
    bd_recv,
    ssem,
    rsem,
    lsem,
):
    d = lax.axis_index("dom")
    b = lax.axis_index("blk")
    o = 1 - b
    has_left = d > 0
    has_right = d < n_dom - 1
    left = jnp.maximum(d - 1, 0)
    right = jnp.minimum(d + 1, n_dom - 1)
    peers = ((d, o), (left, 0), (left, 1), (right, 0), (right, 1))
    there = (None, has_left, has_left, has_right, has_right)

    def if_there(cond, act):
        if cond is None:
            act()
        else:
            pl.when(cond)(act)

    barrier = pltpu.get_barrier_semaphore()
    for peer, cond in zip(peers, there):
        if_there(
            cond,
            functools.partial(
                pl.semaphore_signal,
                barrier,
                inc=1,
                device_id=peer,
                device_id_type=MESH,
            ),
        )

    loads = {}
    for at, (src, dst) in enumerate(
        (
            (fdisp_in, fdisp),
            (coord_in, coord),
            (modulus_in, modulus),
            (disp_in, disp),
            (pnodes_in, pnodes),
            (pmat_in.at[0], pm.at[b]),
            (fvel_in, fvel),
            (fstep_in, fstep),
            (enodes_in, enodes),
            (vel_in, vel),
            (step_in, step),
            (family_in, family),
            (live_in, live),
            (ptile_in, ptile),
            (pblend_in, pblend),
            (fmod_in, fmod),
            (sgrad_in, sgrad),
            (qweight_in, qweight),
            (sleft_in, sleft),
            (sright_in, sright),
        )
    ):
        loads[at] = pltpu.make_async_copy(src, dst, lsem.at[at])
        loads[at].start()

    def loaded(*which):
        for at in which:
            loads[at].wait()

    started = []

    def send(src, dst, ssem_at, rsem_at, peer, cond):
        copy = pltpu.make_async_remote_copy(
            src_ref=src,
            dst_ref=dst,
            send_sem=ssem.at[ssem_at],
            recv_sem=rsem.at[rsem_at],
            device_id=peer,
            device_id_type=MESH,
        )
        if_there(cond, copy.start)
        started.append((copy, cond))

    def arrived(dst, rsem_at, cond):
        copy = pltpu.make_async_remote_copy(
            src_ref=dst,
            dst_ref=dst,
            send_sem=ssem.at[0],
            recv_sem=rsem.at[rsem_at],
            device_id=(d, o),
            device_id_type=MESH,
        )
        if_there(cond, copy.wait_recv)

    own = 4 + 2 * b
    theirs = 4 + 2 * o

    loaded(1, 2, 3, 4)
    for t in range(2):
        pdx[own + t] = jnp.concatenate(
            [
                coord[t],
                modulus[t : t + 1, :],
                disp[t],
                pnodes[...].astype(F32),
                jnp.zeros((2, 128), F32),
            ],
            axis=0,
        )
    loaded(0)
    table[b, 24:32, :] = jnp.zeros((8, LO), F32)
    table[b, 56:64, :] = jnp.zeros((8, LO), F32)
    for r in range(HALF_ROWS):
        for c in range(2):
            at = PAD_ROWS * c + r
            table[b, at : at + 1, :] = fdisp[c : c + 1, r * LO : (r + 1) * LO]
    pl.semaphore_wait(
        barrier, 1 + 2 * has_left.astype(I32) + 2 * has_right.astype(I32)
    )

    send(table.at[b], table.at[b], 0, 0, (d, o), None)
    slots = (own, 8 + 2 * b, 8 + 2 * b, 2 * b, 2 * b)
    marks = (0, 3 + b, 3 + b, 1 + b, 1 + b)
    for j in range(5):
        send(
            pdx.at[pl.ds(own, 2)],
            pdx.at[pl.ds(slots[j], 2)],
            3 + j,
            3 + marks[j],
            peers[j],
            there[j],
        )
    loaded(5)
    send(pm.at[b], pm.at[b], 1, 1, (d, o), None)
    sources = (theirs, 0, 2, 8, 10)

    speed[b, 24:32, :] = jnp.zeros((8, LO), F32)
    speed[b, 56:64, :] = jnp.zeros((8, LO), F32)
    speed[b, 88:96, :] = jnp.zeros((8, LO), F32)
    loaded(6, 7)
    for r in range(HALF_ROWS):
        for c in range(2):
            at = PAD_ROWS * c + r
            speed[b, at : at + 1, :] = fvel[c : c + 1, r * LO : (r + 1) * LO]
    for p in range(2):
        lanes = slice(p * 128, (p + 1) * 128)
        speed[b, 2 * PAD_ROWS : 2 * PAD_ROWS + HALF_ROWS, lanes] = fstep[
            pl.ds(p, HALF_ROWS, stride=2), :
        ]
    send(speed.at[b], speed.at[b], 2, 2, (d, o), None)
    states = (started[0][0], started.pop()[0])
    del started[0]
    loaded(*range(8, 20))

    lo_iota = lax.broadcasted_iota(I32, (LO, 128), 0)

    def table_row(node):
        hi = lax.shift_right_arithmetic(node, 8)
        return jnp.where(hi >= HALF_ROWS, hi + (PAD_ROWS - HALF_ROWS), hi)

    def onehot_of(lo_row):
        return jnp.where(
            lo_iota == jnp.broadcast_to(lo_row, (LO, 128)), 1.0, 0.0
        ).astype(BF16)

    @pl.loop(0, 64 // CHUNK)
    def _(i):
        node = enodes[pl.ds(pl.multiple_of(i * CHUNK, CHUNK), CHUNK), :]
        hrow[pl.ds(pl.multiple_of(i * CHUNK, CHUNK), CHUNK), :] = table_row(node)
        lo = lax.bitwise_and(node, LO - 1)
        base = pl.multiple_of(i * (CHUNK * 128), CHUNK * 128)
        for g in range(CHUNK):
            onehot[:, pl.ds(base + g * 128, 128)] = onehot_of(lo[g : g + 1, :])

    sgt[...] = sgrad[...].T
    eye = lax.broadcasted_iota(I32, (64, 64), 0) == lax.broadcasted_iota(
        I32, (64, 64), 1
    )
    weight = jnp.sum(
        jnp.where(eye, jnp.broadcast_to(qweight[...], (64, 64)), 0.0),
        axis=1,
        keepdims=True,
    )
    scale = weight * fmod[...]

    for j in range(5):
        arrived(pdx.at[pl.ds(sources[j], 2)], 3 + j, there[j])

    ids[...] = jnp.full((8, 128), -1, I32)
    ids[pl.ds(b, 1), :] = pnodes[...]
    ids[pl.ds(o, 1), :] = pdx[theirs, 5:6, :].astype(I32)
    ids[2:3, 0:113] = sleft[...]
    ids[3:4, 0:113] = sright[...]
    few = ids[...]
    hrow[64:72, :] = table_row(few)
    few_lo = lax.bitwise_and(few, LO - 1)
    for g in range(4):
        onehot[:, 8192 + g * 128 : 8320 + g * 128] = onehot_of(few_lo[g : g + 1, :])
    few_f = few.astype(F32)
    few_t = few_f.T
    for q in range(2):
        for side in range(2):
            link[q * 128 : (q + 1) * 128, side * 128 : (side + 1) * 128] = jnp.where(
                few_t[:, q : q + 1] == few_f[2 + side : 3 + side, :], 1.0, 0.0
            ).astype(BF16)

    OX, OY, REST, INFL0, NX, NY, STR, INFL = range(8)

    @pl.loop(0, 6)
    def _(p):
        t = p // 3
        far = pdx[family[t, p - 3 * t]]
        far_t = far.T
        me = pdx[own + t]
        ox = far_t[:, 0:1] - me[0:1, :]
        oy = far_t[:, 1:2] - me[1:2, :]
        r2 = ox * ox + oy * oy
        bonds[OX, p] = ox
        bonds[OY, p] = oy
        bonds[REST, p] = jnp.sqrt(r2 + CORE_SQ)
        bonds[INFL0, p] = jnp.exp(-0.5 * r2)

    cur[...] = vel[...]
    row_iota = lax.broadcasted_iota(I32, (64, 128), 0)

    def masked_rows(product, row):
        both = product[0:128] + product[128:256]
        hit = row_iota == jnp.broadcast_to(row, (64, 128))
        out = []
        for c in range(2):
            x = jnp.where(hit[0:32], both[c * 32 : c * 32 + 32], 0.0)
            x = x + jnp.where(hit[32:64], both[64 + c * 32 : 96 + c * 32], 0.0)
            out.append(jnp.sum(x, axis=0, keepdims=True))
        return out

    def spread(values, row):
        hit = row_iota == jnp.broadcast_to(row, (64, 128))
        blocks = []
        for part in range(2):
            wide = [
                jnp.where(hit, jnp.broadcast_to(values[part][c], (64, 128)), 0.0)
                for c in range(2)
            ]
            for half in range(2):
                for c in range(2):
                    blocks.append(wide[c][half * 32 : half * 32 + 32])
        return jnp.concatenate(blocks, axis=0).astype(BF16)

    for s in range(2):
        ub, st = (ub0, ub1)[s], (st0, st1)[s]
        base = 8 + 13 * s
        if s == 0:
            arrived(table.at[o], 0, None)
            arrived(pm.at[o], 1, None)

        top, low = split2(table[...].reshape(128, LO))
        split_table[0:128, :] = top
        split_table[128:256, :] = low
        product = jnp.dot(
            split_table[...], onehot[:, 8192:8448], preferred_element_type=F32
        )
        targets = []
        for q in range(2):
            picked = masked_rows(
                product[:, q * 128 : (q + 1) * 128], hrow[64 + q : 65 + q, :]
            )
            picked = jnp.concatenate(picked + [jnp.zeros((6, 128), F32)], axis=0)
            targets.append(nt(picked, pm[q], precision=EXACT)[0:2, :])
        for k in range(4):
            if s == 0:
                u = pdx[4 + k, 3:5, :]
            else:
                t = k % 2
                mine = ub[4 + k]
                u = mine
            new = u
            for q in range(2):
                hit = jnp.full((2, 128), ptile[q], I32) == k
                new = jnp.where(
                    hit, u + pblend[q : q + 1, :] * (targets[q] - u), new
                )
            ub[4 + k] = new
        send(ub.at[pl.ds(4, 4)], ub.at[pl.ds(8, 4)], base, base + 1, (left, b), has_left)
        send(ub.at[pl.ds(4, 4)], ub.at[pl.ds(0, 4)], base + 1, base, (right, b), has_right)

        @pl.loop(0, 64 // CHUNK)
        def _(i):
            rows = pl.ds(pl.multiple_of(i * CHUNK, CHUNK), CHUNK)
            lanes = pl.ds(pl.multiple_of(i * (CHUNK * 128), CHUNK * 128), CHUNK * 128)
            product = jnp.dot(
                split_table[...], onehot[:, lanes], preferred_element_type=F32
            )
            row = hrow[rows, :]
            found = [
                masked_rows(product[:, g * 128 : (g + 1) * 128], row[g : g + 1, :])
                for g in range(CHUNK)
            ]
            for c in range(2):
                del_[rows, c * 128 : (c + 1) * 128] = jnp.concatenate(
                    [f[c] for f in found], axis=0
                )

        arrived(ub.at[pl.ds(0, 4)], base, has_left)
        arrived(ub.at[pl.ds(8, 4)], base + 1, has_right)

        @pl.loop(0, 6)
        def _(p):
            t = p // 3
            far = ub[family[t, p - 3 * t]]
            far_t = jnp.concatenate([far, jnp.zeros((6, 128), F32)], axis=0).T
            me = ub[own + t]
            yx = bonds[OX, p] + (far_t[:, 0:1] - me[0:1, :])
            yy = bonds[OY, p] + (far_t[:, 1:2] - me[1:2, :])
            y2 = yx * yx + yy * yy + CORE_SQ
            length = jnp.sqrt(y2)
            inverse = 1.0 / length
            rest = bonds[REST, p]
            stretch = length - rest
            ratio = stretch * (1.0 / STRETCH)
            influence = bonds[INFL0, p] / (1.0 + ratio * ratio)
            bonds[NX, p] = yx * inverse
            bonds[NY, p] = yy * inverse
            bonds[STR, p] = stretch
            bonds[INFL, p] = influence
            weighted = influence * rest
            sums[p] = jnp.concatenate(
                [
                    jnp.sum(weighted * stretch, axis=0, keepdims=True),
                    jnp.sum(weighted * rest, axis=0, keepdims=True),
                ],
                axis=0,
            )

        for t in range(2):
            total = sums[3 * t] + sums[3 * t + 1] + sums[3 * t + 2]
            volume = total[1:2, :]
            st[own + t] = jnp.concatenate(
                [2.0 * total[0:1, :] / volume, volume], axis=0
            )
        for j in range(5):
            send(
                st.at[pl.ds(own, 2)],
                st.at[pl.ds(slots[j], 2)],
                base + 2 + j,
                base + 2 + marks[j],
                peers[j],
                there[j],
            )

        grad = jnp.dot(sgrad[...], del_[...], precision=EXACT, preferred_element_type=F32)
        exx = grad[0:64, 0:128]
        eyy = grad[64:128, 128:256]
        exy = 0.5 * (grad[64:128, 0:128] + grad[0:64, 128:256])
        scaled = scale * (1.0 + exx * exx + eyy * eyy + 2.0 * exy * exy)
        both = exx + eyy
        sxx = scaled * (both + 2.0 * exx)
        syy = scaled * (both + 2.0 * eyy)
        sxy = scaled * 2.0 * exy
        stress = jnp.concatenate(
            [
                jnp.concatenate([sxx, sxy], axis=1),
                jnp.concatenate([sxy, syy], axis=1),
            ],
            axis=0,
        )
        fel[...] = jnp.dot(sgt[...], stress, precision=EXACT, preferred_element_type=F32)
        acc[...] = jnp.zeros((256, LO), F32)

        @pl.loop(0, 64 // CHUNK)
        def _(i):
            rows = pl.ds(pl.multiple_of(i * CHUNK, CHUNK), CHUNK)
            lanes = pl.ds(pl.multiple_of(i * (CHUNK * 128), CHUNK * 128), CHUNK * 128)
            row = hrow[rows, :]
            f = fel[rows, :]
            f_top = f.astype(BF16).astype(F32)
            f_low = f - f_top
            left_side = jnp.concatenate(
                [
                    spread(
                        [
                            [x[g : g + 1, 0:128], x[g : g + 1, 128:256]]
                            for x in (f_top, f_low)
                        ],
                        row[g : g + 1, :],
                    )
                    for g in range(CHUNK)
                ],
                axis=1,
            )
            acc[...] += nt(left_side, onehot[:, lanes])

        partial = acc[0:128, :] + acc[128:256, :]
        pel_send[s] = partial
        if s == 0:
            send(pel_send.at[s], pel_recv.at[s], base + 7, base + 7, (d, o), None)
        else:
            cut = pl.ds(o * 64, 64)
            send(
                pel_send.at[s, cut],
                pel_recv.at[s, cut],
                base + 7,
                base + 7,
                (d, o),
                None,
            )
        top, low = split2(partial)
        product = jnp.dot(
            jnp.concatenate([top, low], axis=0),
            onehot[:, 8448:8704],
            preferred_element_type=F32,
        )
        border = []
        for side in range(2):
            found = masked_rows(
                product[:, side * 128 : (side + 1) * 128],
                hrow[66 + side : 67 + side, :],
            )
            border.append(jnp.concatenate(found, axis=0))

        for j in range(5):
            arrived(st.at[pl.ds(sources[j], 2)], base + 2 + j, there[j])

        def coefficients(k, state):
            theta, volume = state[0:1, :], state[1:2, :]
            return 2.0 * k * theta / volume, 4.0 * k / volume, 0.5 * theta

        @pl.loop(0, 6)
        def _(p):
            t = p // 3
            j = family[t, p - 3 * t]
            fa, fb, fc = coefficients(pdx[j][2:3, :], st[j])
            far_t = jnp.concatenate([fa, fb, fc, jnp.zeros((5, 128), F32)], axis=0).T
            oa, ob, oc = coefficients(pdx[own + t][2:3, :], st[own + t])
            rest = bonds[REST, p]
            stretch = bonds[STR, p]
            near = oa * rest + ob * (stretch - oc * rest)
            away = far_t[:, 0:1] * rest + far_t[:, 1:2] * (stretch - far_t[:, 2:3] * rest)
            force = bonds[INFL, p] * (near + away)
            sums[p] = jnp.concatenate(
                [
                    jnp.sum(force * bonds[NX, p], axis=0, keepdims=True),
                    jnp.sum(force * bonds[NY, p], axis=0, keepdims=True),
                ],
                axis=0,
            )

        forces, moved = [], []
        for t in range(2):
            alive = jnp.full((2, 128), 2 * b + t, I32) < live[0]
            total = sums[3 * t] + sums[3 * t + 1] + sums[3 * t + 2]
            force = jnp.where(alive, total, 0.0)
            forces.append(force)
            v = jnp.where(alive, cur[t] + step[t : t + 1, :] * force, 0.0)
            u = jnp.where(alive, ub[own + t] + TIME_STEP * v, 0.0)
            cur[t] = v
            moved.append(u)

        reaction = []
        for q in range(2):
            w = jnp.zeros((2, 128), F32)
            for t in range(2):
                hit = jnp.full((2, 128), ptile[q], I32) == 2 * b + t
                w = w + jnp.where(hit, pblend[q : q + 1, :] * forces[t], 0.0)
            w = jnp.concatenate([w, jnp.zeros((6, 128), F32)], axis=0)
            reaction.append(
                jnp.dot(w, pm[q], precision=EXACT, preferred_element_type=F32)[0:2, :]
            )
        late = jnp.concatenate(reaction + moved, axis=0)
        late_send[s] = late
        send(late_send.at[s], late_recv.at[s], base + 8, base + 8, (d, o), None)
        wide = jnp.concatenate(reaction, axis=1)
        top, low = split2(wide)
        met = jnp.dot(
            jnp.concatenate([top, low, jnp.zeros((12, 256), BF16)], axis=0),
            link[...],
            preferred_element_type=F32,
        )
        met = met[0:2, :] + met[2:4, :]
        for side in range(2):
            bd_send[s, side] = met[:, side * 128 : (side + 1) * 128] - border[side]
        for j in range(4):
            side = j // 2
            send(
                bd_send.at[s, side],
                bd_recv.at[s, 2 * (1 - side) + b],
                base + 9 + j,
                base + 9 + 2 * (1 - side) + b,
                peers[1 + j],
                there[1 + j],
            )
        if s == 0:
            for t in range(2):
                ub1[own + t] = moved[t]
        else:
            for t in range(2):
                disp_out[t] = moved[t]
                vel_out[t] = cur[t]

        arrived(late_recv.at[s], base + 8, None)
        other = late_recv[s]
        if s == 0:
            for t in range(2):
                ub1[theirs + t] = other[4 + 2 * t : 6 + 2 * t, :]
        for j in range(4):
            arrived(bd_recv.at[s, j], base + 9 + j, there[1 + j])
        shared = [
            jnp.where(
                jnp.full((2, 128), d, I32) > 0, bd_recv[s, 0] + bd_recv[s, 1], 0.0
            ),
            jnp.where(
                jnp.full((2, 128), d, I32) < n_dom - 1,
                bd_recv[s, 2] + bd_recv[s, 3],
                0.0,
            ),
        ]
        sides = []
        for g, x in enumerate(
            [late[0:2, :] + other[0:2, :], late[2:4, :] + other[2:4, :]] + shared
        ):
            x_top = x.astype(BF16).astype(F32)
            x_low = x - x_top
            sides.append(
                spread(
                    [[y[0:1, :], y[1:2, :]] for y in (x_top, x_low)],
                    hrow[64 + g : 65 + g, :],
                )
            )
        extra = nt(jnp.concatenate(sides, axis=1), onehot[:, 8192:8704])
        acc[0:128, :] = extra[0:128, :] + extra[128:256, :]
        if s == 0:
            arrived(speed.at[o], 2, None)
            arrived(pel_recv.at[s], base + 7, None)
            for copy in states:
                copy.wait_send()
        else:
            arrived(pel_recv.at[s, pl.ds(b * 64, 64)], base + 7, None)
        for h in range(2) if s == 0 else (b,):
            for c in range(2):
                cut = pl.ds(h * 64 + c * 32, 32)
                rows = slice(c * 32, c * 32 + 32)
                nodal = acc[cut, :] - (pel_send[s, cut, :] + pel_recv[s, cut, :])
                v = speed[h, rows, :] + speed[h, 64:96, :] * nodal
                speed[h, rows, :] = v
                table[h, rows, :] = table[h, rows, :] + TIME_STEP * v

    for r in range(HALF_ROWS):
        lanes = slice(r * LO, (r + 1) * LO)
        for c in range(2):
            at = PAD_ROWS * c + r
            fdisp_out[c : c + 1, lanes] = table[b, at : at + 1, :]
            fvel_out[c : c + 1, lanes] = speed[b, at : at + 1, :]
    for copy, cond in started:
        if_there(cond, copy.wait_send)


def hand_over(*refs):
    ins, outs, sems = refs[:4], refs[4:8], refs[8]
    copies = [
        pltpu.make_async_copy(src, dst, sems.at[at])
        for at, (src, dst) in enumerate(zip(ins, outs))
    ]
    for copy in copies:
        copy.start()
    for copy in copies:
        copy.wait()


def shards(n_dom, *args):
    (
        pd_disp,
        pd_vel,
        pd_coord,
        pd_modulus,
        pd_step,
        family,
        live,
        patch_tile,
        patch_blend,
        patch_nodes,
        patch_matrix,
        fe_disp,
        fe_vel,
        fe_step,
        fe_modulus,
        element_nodes,
        shape_grad,
        quad_weight,
        shared_left,
        shared_right,
    ) = args
    vmem = pl.BlockSpec(memory_space=pltpu.VMEM)
    hbm = pl.BlockSpec(memory_space=pltpu.HBM)
    rows = fe_step.shape[0] // 128

    def f32(*shape):
        return pltpu.VMEM(shape, F32)

    results = pl.pallas_call(
        functools.partial(kernel, n_dom),
        out_shape=[
            jax.ShapeDtypeStruct(pd_disp.shape, F32),
            jax.ShapeDtypeStruct(pd_vel.shape, F32),
            jax.ShapeDtypeStruct(fe_disp.shape, F32),
            jax.ShapeDtypeStruct(fe_vel.shape, F32),
        ],
        in_specs=[hbm] * 20,
        out_specs=[vmem] * 4,
        scratch_shapes=[
            f32(2, 2, 128),
            f32(2, 2, 128),
            f32(2, 2, 128),
            f32(2, 128),
            f32(2, 128),
            pltpu.SMEM((2, 3), I32),
            pltpu.SMEM((1,), I32),
            pltpu.SMEM((2,), I32),
            f32(2, 128),
            pltpu.VMEM((1, 128), I32),
            f32(*fe_disp.shape),
            f32(*fe_vel.shape),
            f32(rows, 128),
            f32(1, 128),
            pltpu.VMEM((64, 128), I32),
            f32(128, 64),
            f32(1, 64),
            pltpu.VMEM((1, 113), I32),
            pltpu.VMEM((1, 113), I32),
            f32(12, 8, 128),
            f32(12, 2, 128),
            f32(12, 2, 128),
            f32(12, 2, 128),
            f32(12, 2, 128),
            f32(2, 128, 128),
            f32(2, 64, LO),
            f32(2, 96, LO),
            pltpu.VMEM((256, LO), BF16),
            pltpu.VMEM((LO, 8704), BF16),
            pltpu.VMEM((72, 128), I32),
            pltpu.VMEM((8, 128), I32),
            pltpu.VMEM((256, 256), BF16),
            f32(64, 256),
            f32(64, 256),
            f32(64, 128),
            f32(256, LO),
            f32(8, 6, 128, 128),
            f32(6, 2, 128),
            f32(2, 2, 128),
            f32(2, 128, LO),
            f32(2, 128, LO),
            f32(2, 8, 128),
            f32(2, 8, 128),
            f32(2, 2, 2, 128),
            f32(2, 4, 2, 128),
            pltpu.SemaphoreType.DMA((N_COPIES,)),
            pltpu.SemaphoreType.DMA((N_COPIES,)),
            pltpu.SemaphoreType.DMA((20,)),
        ],
        compiler_params=pltpu.CompilerParams(
            collective_id=0, has_side_effects=True, vmem_limit_bytes=VMEM_BYTES
        ),
    )(
        pd_disp,
        pd_vel,
        pd_coord,
        pd_modulus,
        pd_step,
        family,
        live,
        patch_tile,
        patch_blend,
        patch_nodes,
        patch_matrix,
        fe_disp,
        fe_vel,
        fe_step.reshape(-1, 128),
        fe_modulus.reshape(1, -1),
        element_nodes,
        shape_grad.reshape(-1, shape_grad.shape[2]),
        quad_weight.reshape(1, -1),
        shared_left,
        shared_right,
    )
    return pl.pallas_call(
        hand_over,
        out_shape=[jax.ShapeDtypeStruct(x.shape, F32) for x in results],
        in_specs=[hbm] * 4,
        out_specs=[hbm] * 4,
        scratch_shapes=[pltpu.SemaphoreType.DMA((4,))],
        compiler_params=pltpu.CompilerParams(vmem_limit_bytes=VMEM_BYTES),
    )(*results)


def solution(mesh):
    both = ("dom", "blk")
    return jax.shard_map(
        functools.partial(shards, mesh.shape["dom"]),
        mesh=mesh,
        in_specs=(
            P(both, None, None),
            P(both, None, None),
            P(both, None, None),
            P(both, None),
            P(both, None),
            P(both, None),
            P("dom"),
            P("dom"),
            P("dom", None),
            P(both, None),
            P(both, None, None),
            P(None, both),
            P(None, both),
            P(both),
            P(both),
            P(None, both),
            P(),
            P(),
            P("dom", None),
            P("dom", None),
        ),
        out_specs=(
            P(both, None, None),
            P(both, None, None),
            P(None, both),
            P(None, both),
        ),
        check_vma=False,
    )
```

```python
import functools

import jax
import jax.numpy as jnp
from jax import lax
from jax.experimental import pallas as pl
from jax.experimental.pallas import tpu as pltpu
from jax.sharding import PartitionSpec as P

MESH = pl.DeviceIdType.MESH
F32 = jnp.float32
BF16 = jnp.bfloat16
I32 = jnp.int32
EXACT = lax.Precision.HIGHEST

TIME_STEP = 0.5
CORE_SQ = 0.01
STRETCH = 0.3

LO = 256
HALF_ROWS = 25
PAD_ROWS = 32
CHUNK = 8
N_COPIES = 34
VMEM_BYTES = 60 * 2**20


def split2(x):
    top = x.astype(BF16)
    return top, (x - top.astype(F32)).astype(BF16)


def folded(x):
    return jnp.sum(x.reshape(-1, 8, x.shape[1]), axis=0)


def inverted(x):
    y = pl.reciprocal(x, approx=True)
    return y * (2.0 - x * y)


def nt(a, b, **kw):
    return lax.dot_general(
        a, b, (((1,), (1,)), ((), ())), preferred_element_type=F32, **kw
    )


def kernel(
    n_dom,
    disp_in,
    vel_in,
    coord_in,
    modulus_in,
    step_in,
    family_in,
    live_in,
    ptile_in,
    pblend_in,
    pnodes_in,
    pmat_in,
    fdisp_in,
    fvel_in,
    fstep_in,
    fmod_in,
    enodes_in,
    sgrad_in,
    qweight_in,
    sleft_in,
    sright_in,
    disp_out,
    vel_out,
    fdisp_out,
    fvel_out,
    disp,
    vel,
    coord,
    modulus,
    step,
    family,
    live,
    ptile,
    pblend,
    pnodes,
    fdisp,
    fvel,
    fstep,
    fmod,
    enodes,
    sgrad,
    qweight,
    sleft,
    sright,
    pdx,
    ub0,
    ub1,
    st0,
    st1,
    pm,
    table,
    speed,
    split_table,
    onehot,
    hrow,
    ids,
    link,
    del_,
    fel,
    sgt,
    acc,
    bonds,
    cur,
    pel_send,
    pel_recv,
    late_send,
    late_recv,
    bd_send,
    bd_recv,
    ssem,
    rsem,
    lsem,
):
    d = lax.axis_index("dom")
    b = lax.axis_index("blk")
    o = 1 - b
    has_left = d > 0
    has_right = d < n_dom - 1
    left = jnp.maximum(d - 1, 0)
    right = jnp.minimum(d + 1, n_dom - 1)
    peers = ((d, o), (left, 0), (left, 1), (right, 0), (right, 1))
    there = (None, has_left, has_left, has_right, has_right)

    def if_there(cond, act):
        if cond is None:
            act()
        else:
            pl.when(cond)(act)

    barrier = pltpu.get_barrier_semaphore()
    for peer, cond in zip(peers, there):
        if_there(
            cond,
            functools.partial(
                pl.semaphore_signal,
                barrier,
                inc=1,
                device_id=peer,
                device_id_type=MESH,
            ),
        )

    loads = {}
    for at, (src, dst) in enumerate(
        (
            (fdisp_in, fdisp),
            (coord_in, coord),
            (modulus_in, modulus),
            (disp_in, disp),
            (pnodes_in, pnodes),
            (pmat_in.at[0], pm.at[b]),
            (fvel_in, fvel),
            (fstep_in, fstep),
            (enodes_in, enodes),
            (vel_in, vel),
            (step_in, step),
            (family_in, family),
            (live_in, live),
            (ptile_in, ptile),
            (pblend_in, pblend),
            (fmod_in, fmod),
            (sgrad_in, sgrad),
            (qweight_in, qweight),
            (sleft_in, sleft),
            (sright_in, sright),
        )
    ):
        loads[at] = pltpu.make_async_copy(src, dst, lsem.at[at])
        loads[at].start()

    def loaded(*which):
        for at in which:
            loads[at].wait()

    started = []

    def send(src, dst, ssem_at, rsem_at, peer, cond):
        copy = pltpu.make_async_remote_copy(
            src_ref=src,
            dst_ref=dst,
            send_sem=ssem.at[ssem_at],
            recv_sem=rsem.at[rsem_at],
            device_id=peer,
            device_id_type=MESH,
        )
        if_there(cond, copy.start)
        started.append((copy, cond))

    def arrived(dst, rsem_at, cond):
        copy = pltpu.make_async_remote_copy(
            src_ref=dst,
            dst_ref=dst,
            send_sem=ssem.at[0],
            recv_sem=rsem.at[rsem_at],
            device_id=(d, o),
            device_id_type=MESH,
        )
        if_there(cond, copy.wait_recv)

    own = 4 + 2 * b
    theirs = 4 + 2 * o

    loaded(1, 2, 3, 4)
    for t in range(2):
        pdx[own + t] = jnp.concatenate(
            [
                coord[t],
                modulus[t : t + 1, :],
                disp[t],
                pnodes[...].astype(F32),
                jnp.zeros((2, 128), F32),
            ],
            axis=0,
        )
    loaded(0)
    table[b, 24:32, :] = jnp.zeros((8, LO), F32)
    table[b, 56:64, :] = jnp.zeros((8, LO), F32)
    for r in range(HALF_ROWS):
        for c in range(2):
            at = PAD_ROWS * c + r
            table[b, at : at + 1, :] = fdisp[c : c + 1, r * LO : (r + 1) * LO]
    loaded(6, 7)
    speed[b, 24:32, :] = jnp.zeros((8, LO), F32)
    speed[b, 56:64, :] = jnp.zeros((8, LO), F32)
    speed[b, 88:96, :] = jnp.zeros((8, LO), F32)
    for r in range(HALF_ROWS):
        for c in range(2):
            at = PAD_ROWS * c + r
            speed[b, at : at + 1, :] = fvel[c : c + 1, r * LO : (r + 1) * LO]
    for p in range(2):
        lanes = slice(p * 128, (p + 1) * 128)
        speed[b, 2 * PAD_ROWS : 2 * PAD_ROWS + HALF_ROWS, lanes] = fstep[
            pl.ds(p, HALF_ROWS, stride=2), :
        ]
    loaded(*range(8, 20))

    lo_iota = lax.broadcasted_iota(I32, (LO, 128), 0)

    def table_row(node):
        hi = lax.shift_right_arithmetic(node, 8)
        return jnp.where(hi >= HALF_ROWS, hi + (PAD_ROWS - HALF_ROWS), hi)

    def onehot_of(lo_row):
        return jnp.where(
            lo_iota == jnp.broadcast_to(lo_row, (LO, 128)), 1.0, 0.0
        ).astype(BF16)

    @pl.loop(0, 64 // CHUNK)
    def _(i):
        node = enodes[pl.ds(pl.multiple_of(i * CHUNK, CHUNK), CHUNK), :]
        hrow[pl.ds(pl.multiple_of(i * CHUNK, CHUNK), CHUNK), :] = table_row(node)
        lo = lax.bitwise_and(node, LO - 1)
        base = pl.multiple_of(i * (CHUNK * 128), CHUNK * 128)
        for g in range(CHUNK):
            onehot[:, pl.ds(base + g * 128, 128)] = onehot_of(lo[g : g + 1, :])

    sgt[...] = sgrad[...].T
    eye = lax.broadcasted_iota(I32, (64, 64), 0) == lax.broadcasted_iota(
        I32, (64, 64), 1
    )
    weight = jnp.sum(
        jnp.where(eye, jnp.broadcast_to(qweight[...], (64, 64)), 0.0),
        axis=1,
        keepdims=True,
    )
    scale = weight * fmod[...]


    ids[...] = jnp.full((8, 128), -1, I32)
    ids[pl.ds(b, 1), :] = pnodes[...]
    ids[2:3, 0:113] = sleft[...]
    ids[3:4, 0:113] = sright[...]
    few_lo = lax.bitwise_and(ids[...], LO - 1)
    for g in (2, 3):
        onehot[:, 8192 + g * 128 : 8320 + g * 128] = onehot_of(few_lo[g : g + 1, :])

    pl.semaphore_wait(
        barrier, 1 + 2 * has_left.astype(I32) + 2 * has_right.astype(I32)
    )

    send(table.at[b], table.at[b], 0, 0, (d, o), None)
    slots = (own, 8 + 2 * b, 8 + 2 * b, 2 * b, 2 * b)
    marks = (0, 3 + b, 3 + b, 1 + b, 1 + b)
    for j in range(5):
        send(
            pdx.at[pl.ds(own, 2)],
            pdx.at[pl.ds(slots[j], 2)],
            3 + j,
            3 + marks[j],
            peers[j],
            there[j],
        )
    loaded(5)
    send(pm.at[b], pm.at[b], 1, 1, (d, o), None)
    sources = (theirs, 0, 2, 8, 10)
    send(speed.at[b], speed.at[b], 2, 2, (d, o), None)
    states = (started[0][0], started.pop()[0])
    del started[0]

    arrived(pdx.at[pl.ds(theirs, 2)], 3, None)
    ids[pl.ds(o, 1), :] = pdx[theirs, 5:6, :].astype(I32)
    few = ids[...]
    hrow[64:72, :] = table_row(few)
    few_lo = lax.bitwise_and(few, LO - 1)
    for g in range(2):
        onehot[:, 8192 + g * 128 : 8320 + g * 128] = onehot_of(few_lo[g : g + 1, :])

    OX, OY, REST, INFL0, NX, NY, STR, INFL = range(8)
    cur[...] = vel[...]

    def pair(p):
        return p // 3, p % 3

    def keep_bonds():
        for p in range(6):
            t, k = pair(p)
            far_t = pdx[family[t, k]].T
            me = pdx[own + t]
            for q in range(0, 128, 32):
                rows = slice(q, q + 32)
                ox = far_t[rows, 0:1] - me[0:1, :]
                oy = far_t[rows, 1:2] - me[1:2, :]
                r2 = ox * ox + oy * oy
                bonds[OX, p, rows] = ox
                bonds[OY, p, rows] = oy
                bonds[REST, p, rows] = jnp.sqrt(r2 + CORE_SQ)
                bonds[INFL0, p, rows] = jnp.exp(-0.5 * r2)

    row_iota = lax.broadcasted_iota(I32, (64, 128), 0)

    def masked_rows(product, row):
        both = product[0:128] + product[128:256]
        hit = row_iota == jnp.broadcast_to(row, (64, 128))
        out = []
        for c in range(2):
            x = jnp.where(hit[0:32], both[c * 32 : c * 32 + 32], 0.0)
            x = x + jnp.where(hit[32:64], both[64 + c * 32 : 96 + c * 32], 0.0)
            out.append(jnp.sum(x, axis=0, keepdims=True))
        return out

    def spread(values, row):
        hit = row_iota == jnp.broadcast_to(row, (64, 128))
        blocks = []
        for part in range(2):
            wide = [
                jnp.where(hit, jnp.broadcast_to(values[part][c], (64, 128)), 0.0)
                for c in range(2)
            ]
            for half in range(2):
                for c in range(2):
                    blocks.append(wide[c][half * 32 : half * 32 + 32])
        return jnp.concatenate(blocks, axis=0).astype(BF16)

    for s in range(2):
        ub, st = (ub0, ub1)[s], (st0, st1)[s]
        base = 8 + 13 * s
        if s == 0:
            arrived(table.at[o], 0, None)
            arrived(pm.at[o], 1, None)

        top, low = split2(table[...].reshape(128, LO))
        split_table[0:128, :] = top
        split_table[128:256, :] = low
        product = jnp.dot(
            split_table[...], onehot[:, 8192:8448], preferred_element_type=F32
        )
        targets = []
        for q in range(2):
            picked = masked_rows(
                product[:, q * 128 : (q + 1) * 128], hrow[64 + q : 65 + q, :]
            )
            picked = jnp.concatenate(picked + [jnp.zeros((6, 128), F32)], axis=0)
            targets.append(nt(picked, pm[q], precision=EXACT)[0:2, :])
        for k in range(4):
            if s == 0:
                u = pdx[4 + k, 3:5, :]
            else:
                t = k % 2
                mine = ub[4 + k]
                u = mine
            new = u
            for q in range(2):
                hit = jnp.full((2, 128), ptile[q], I32) == k
                new = jnp.where(
                    hit, u + pblend[q : q + 1, :] * (targets[q] - u), new
                )
            ub[4 + k] = new
        send(ub.at[pl.ds(4, 4)], ub.at[pl.ds(8, 4)], base, base + 1, (left, b), has_left)
        send(ub.at[pl.ds(4, 4)], ub.at[pl.ds(0, 4)], base + 1, base, (right, b), has_right)

        @pl.loop(0, 64 // CHUNK)
        def _(i):
            rows = pl.ds(pl.multiple_of(i * CHUNK, CHUNK), CHUNK)
            lanes = pl.ds(pl.multiple_of(i * (CHUNK * 128), CHUNK * 128), CHUNK * 128)
            product = jnp.dot(
                split_table[...], onehot[:, lanes], preferred_element_type=F32
            )
            row = hrow[rows, :]
            found = [
                masked_rows(product[:, g * 128 : (g + 1) * 128], row[g : g + 1, :])
                for g in range(CHUNK)
            ]
            for c in range(2):
                del_[rows, c * 128 : (c + 1) * 128] = jnp.concatenate(
                    [f[c] for f in found], axis=0
                )

        if s == 0:
            few_f = ids[...].astype(F32)
            few_t = few_f.T
            for q in range(2):
                for side in range(2):
                    link[
                        q * 128 : (q + 1) * 128, side * 128 : (side + 1) * 128
                    ] = jnp.where(
                        few_t[:, q : q + 1] == few_f[2 + side : 3 + side, :], 1.0, 0.0
                    ).astype(BF16)

        if s == 0:
            for j in range(1, 5):
                arrived(pdx.at[pl.ds(sources[j], 2)], 3 + j, there[j])
            keep_bonds()

        arrived(ub.at[pl.ds(0, 4)], base, has_left)
        arrived(ub.at[pl.ds(8, 4)], base + 1, has_right)

        totals = [[jnp.zeros((8, 128), F32)] * 2 for _ in range(2)]
        for p in range(6):
            t, k = pair(p)
            far_t = jnp.concatenate([ub[family[t, k]], jnp.zeros((6, 128), F32)], axis=0).T
            me = ub[own + t]
            for q in range(0, 128, 32):
                rows = slice(q, q + 32)
                yx = bonds[OX, p, rows] + (far_t[rows, 0:1] - me[0:1, :])
                yy = bonds[OY, p, rows] + (far_t[rows, 1:2] - me[1:2, :])
                y2 = yx * yx + yy * yy + CORE_SQ
                inverse = lax.rsqrt(y2)
                length = y2 * inverse
                rest = bonds[REST, p, rows]
                stretch = length - rest
                ratio = stretch * (1.0 / STRETCH)
                influence = bonds[INFL0, p, rows] * inverted(1.0 + ratio * ratio)
                bonds[NX, p, rows] = yx * inverse
                bonds[NY, p, rows] = yy * inverse
                bonds[STR, p, rows] = stretch
                bonds[INFL, p, rows] = influence
                weighted = influence * rest
                totals[t][0] = totals[t][0] + folded(weighted * stretch)
                totals[t][1] = totals[t][1] + folded(weighted * rest)
        totals = [[jnp.sum(x, axis=0, keepdims=True) for x in y] for y in totals]

        for t in range(2):
            dilated, volume = totals[t]
            st[own + t] = jnp.concatenate([2.0 * dilated / volume, volume], axis=0)
        for j in range(5):
            send(
                st.at[pl.ds(own, 2)],
                st.at[pl.ds(slots[j], 2)],
                base + 2 + j,
                base + 2 + marks[j],
                peers[j],
                there[j],
            )

        grad = jnp.dot(sgrad[...], del_[...], precision=EXACT, preferred_element_type=F32)
        exx = grad[0:64, 0:128]
        eyy = grad[64:128, 128:256]
        exy = 0.5 * (grad[64:128, 0:128] + grad[0:64, 128:256])
        scaled = scale * (1.0 + exx * exx + eyy * eyy + 2.0 * exy * exy)
        both = exx + eyy
        sxx = scaled * (both + 2.0 * exx)
        syy = scaled * (both + 2.0 * eyy)
        sxy = scaled * 2.0 * exy
        stress = jnp.concatenate(
            [
                jnp.concatenate([sxx, sxy], axis=1),
                jnp.concatenate([sxy, syy], axis=1),
            ],
            axis=0,
        )
        fel[...] = jnp.dot(sgt[...], stress, precision=EXACT, preferred_element_type=F32)
        acc[...] = jnp.zeros((256, LO), F32)

        @pl.loop(0, 64 // CHUNK)
        def _(i):
            rows = pl.ds(pl.multiple_of(i * CHUNK, CHUNK), CHUNK)
            lanes = pl.ds(pl.multiple_of(i * (CHUNK * 128), CHUNK * 128), CHUNK * 128)
            row = hrow[rows, :]
            f = fel[rows, :]
            f_top = f.astype(BF16).astype(F32)
            f_low = f - f_top
            left_side = jnp.concatenate(
                [
                    spread(
                        [
                            [x[g : g + 1, 0:128], x[g : g + 1, 128:256]]
                            for x in (f_top, f_low)
                        ],
                        row[g : g + 1, :],
                    )
                    for g in range(CHUNK)
                ],
                axis=1,
            )
            acc[...] += nt(left_side, onehot[:, lanes])

        partial = acc[0:128, :] + acc[128:256, :]
        pel_send[s] = partial
        if s == 0:
            send(pel_send.at[s], pel_recv.at[s], base + 7, base + 7, (d, o), None)
        else:
            cut = pl.ds(o * 64, 64)
            send(
                pel_send.at[s, cut],
                pel_recv.at[s, cut],
                base + 7,
                base + 7,
                (d, o),
                None,
            )
        top, low = split2(partial)
        product = jnp.dot(
            jnp.concatenate([top, low], axis=0),
            onehot[:, 8448:8704],
            preferred_element_type=F32,
        )
        border = []
        for side in range(2):
            found = masked_rows(
                product[:, side * 128 : (side + 1) * 128],
                hrow[66 + side : 67 + side, :],
            )
            border.append(jnp.concatenate(found, axis=0))

        for j in range(5):
            arrived(st.at[pl.ds(sources[j], 2)], base + 2 + j, there[j])

        def coefficients(k, state):
            theta, volume = state[0:1, :], state[1:2, :]
            return 2.0 * k * theta / volume, 4.0 * k / volume, 0.5 * theta

        totals = [[jnp.zeros((8, 128), F32)] * 2 for _ in range(2)]
        near = [coefficients(pdx[own + t][2:3, :], st[own + t]) for t in range(2)]
        for p in range(6):
            t, k = pair(p)
            j = family[t, k]
            far = coefficients(pdx[j][2:3, :], st[j])
            far_t = jnp.concatenate(far + (jnp.zeros((5, 128), F32),), axis=0).T
            oa, ob, oc = near[t]
            for q in range(0, 128, 32):
                rows = slice(q, q + 32)
                rest = bonds[REST, p, rows]
                stretch = bonds[STR, p, rows]
                mine = oa * rest + ob * (stretch - oc * rest)
                away = far_t[rows, 0:1] * rest + far_t[rows, 1:2] * (
                    stretch - far_t[rows, 2:3] * rest
                )
                force = bonds[INFL, p, rows] * (mine + away)
                totals[t][0] = totals[t][0] + folded(force * bonds[NX, p, rows])
                totals[t][1] = totals[t][1] + folded(force * bonds[NY, p, rows])

        forces, moved = [], []
        for t in range(2):
            alive = jnp.full((2, 128), 2 * b + t, I32) < live[0]
            total = [jnp.sum(x, axis=0, keepdims=True) for x in totals[t]]
            force = jnp.where(alive, jnp.concatenate(total, axis=0), 0.0)
            forces.append(force)
            v = jnp.where(alive, cur[t] + step[t : t + 1, :] * force, 0.0)
            u = jnp.where(alive, ub[own + t] + TIME_STEP * v, 0.0)
            cur[t] = v
            moved.append(u)

        reaction = []
        for q in range(2):
            w = jnp.zeros((2, 128), F32)
            for t in range(2):
                hit = jnp.full((2, 128), ptile[q], I32) == 2 * b + t
                w = w + jnp.where(hit, pblend[q : q + 1, :] * forces[t], 0.0)
            w = jnp.concatenate([w, jnp.zeros((6, 128), F32)], axis=0)
            reaction.append(
                jnp.dot(w, pm[q], precision=EXACT, preferred_element_type=F32)[0:2, :]
            )
        late = jnp.concatenate(reaction + moved, axis=0)
        late_send[s] = late
        send(late_send.at[s], late_recv.at[s], base + 8, base + 8, (d, o), None)
        wide = jnp.concatenate(reaction, axis=1)
        top, low = split2(wide)
        met = jnp.dot(
            jnp.concatenate([top, low, jnp.zeros((12, 256), BF16)], axis=0),
            link[...],
            preferred_element_type=F32,
        )
        met = met[0:2, :] + met[2:4, :]
        for side in range(2):
            bd_send[s, side] = met[:, side * 128 : (side + 1) * 128] - border[side]
        for j in range(4):
            side = j // 2
            send(
                bd_send.at[s, side],
                bd_recv.at[s, 2 * (1 - side) + b],
                base + 9 + j,
                base + 9 + 2 * (1 - side) + b,
                peers[1 + j],
                there[1 + j],
            )
        if s == 0:
            for t in range(2):
                ub1[own + t] = moved[t]
        else:
            for t in range(2):
                disp_out[t] = moved[t]
                vel_out[t] = cur[t]

        arrived(late_recv.at[s], base + 8, None)
        other = late_recv[s]
        if s == 0:
            for t in range(2):
                ub1[theirs + t] = other[4 + 2 * t : 6 + 2 * t, :]
        for j in range(4):
            arrived(bd_recv.at[s, j], base + 9 + j, there[1 + j])
        shared = [
            jnp.where(
                jnp.full((2, 128), d, I32) > 0, bd_recv[s, 0] + bd_recv[s, 1], 0.0
            ),
            jnp.where(
                jnp.full((2, 128), d, I32) < n_dom - 1,
                bd_recv[s, 2] + bd_recv[s, 3],
                0.0,
            ),
        ]
        sides = []
        for g, x in enumerate(
            [late[0:2, :] + other[0:2, :], late[2:4, :] + other[2:4, :]] + shared
        ):
            x_top = x.astype(BF16).astype(F32)
            x_low = x - x_top
            sides.append(
                spread(
                    [[y[0:1, :], y[1:2, :]] for y in (x_top, x_low)],
                    hrow[64 + g : 65 + g, :],
                )
            )
        extra = nt(jnp.concatenate(sides, axis=1), onehot[:, 8192:8704])
        acc[0:128, :] = extra[0:128, :] + extra[128:256, :]
        if s == 0:
            arrived(speed.at[o], 2, None)
            arrived(pel_recv.at[s], base + 7, None)
            for copy in states:
                copy.wait_send()
        else:
            arrived(pel_recv.at[s, pl.ds(b * 64, 64)], base + 7, None)
        for h in range(2) if s == 0 else (b,):
            for c in range(2):
                cut = pl.ds(h * 64 + c * 32, 32)
                rows = slice(c * 32, c * 32 + 32)
                nodal = acc[cut, :] - (pel_send[s, cut, :] + pel_recv[s, cut, :])
                v = speed[h, rows, :] + speed[h, 64:96, :] * nodal
                speed[h, rows, :] = v
                table[h, rows, :] = table[h, rows, :] + TIME_STEP * v

    for r in range(HALF_ROWS):
        lanes = slice(r * LO, (r + 1) * LO)
        for c in range(2):
            at = PAD_ROWS * c + r
            fdisp_out[c : c + 1, lanes] = table[b, at : at + 1, :]
            fvel_out[c : c + 1, lanes] = speed[b, at : at + 1, :]
    for copy, cond in started:
        if_there(cond, copy.wait_send)


def hand_over(*refs):
    ins, outs, sems = refs[:4], refs[4:8], refs[8]
    copies = [
        pltpu.make_async_copy(src, dst, sems.at[at])
        for at, (src, dst) in enumerate(zip(ins, outs))
    ]
    for copy in copies:
        copy.start()
    for copy in copies:
        copy.wait()


def shards(n_dom, *args):
    (
        pd_disp,
        pd_vel,
        pd_coord,
        pd_modulus,
        pd_step,
        family,
        live,
        patch_tile,
        patch_blend,
        patch_nodes,
        patch_matrix,
        fe_disp,
        fe_vel,
        fe_step,
        fe_modulus,
        element_nodes,
        shape_grad,
        quad_weight,
        shared_left,
        shared_right,
    ) = args
    vmem = pl.BlockSpec(memory_space=pltpu.VMEM)
    hbm = pl.BlockSpec(memory_space=pltpu.HBM)
    rows = fe_step.shape[0] // 128

    def f32(*shape):
        return pltpu.VMEM(shape, F32)

    results = pl.pallas_call(
        functools.partial(kernel, n_dom),
        out_shape=[
            pltpu.VMEM(pd_disp.shape, F32),
            pltpu.VMEM(pd_vel.shape, F32),
            pltpu.VMEM(fe_disp.shape, F32),
            pltpu.VMEM(fe_vel.shape, F32),
        ],
        in_specs=[hbm] * 20,
        out_specs=[vmem] * 4,
        scratch_shapes=[
            f32(2, 2, 128),
            f32(2, 2, 128),
            f32(2, 2, 128),
            f32(2, 128),
            f32(2, 128),
            pltpu.SMEM((2, 3), I32),
            pltpu.SMEM((1,), I32),
            pltpu.SMEM((2,), I32),
            f32(2, 128),
            pltpu.VMEM((1, 128), I32),
            f32(*fe_disp.shape),
            f32(*fe_vel.shape),
            f32(rows, 128),
            f32(1, 128),
            pltpu.VMEM((64, 128), I32),
            f32(128, 64),
            f32(1, 64),
            pltpu.VMEM((1, 113), I32),
            pltpu.VMEM((1, 113), I32),
            f32(12, 8, 128),
            f32(12, 2, 128),
            f32(12, 2, 128),
            f32(12, 2, 128),
            f32(12, 2, 128),
            f32(2, 128, 128),
            f32(2, 64, LO),
            f32(2, 96, LO),
            pltpu.VMEM((256, LO), BF16),
            pltpu.VMEM((LO, 8704), BF16),
            pltpu.VMEM((72, 128), I32),
            pltpu.VMEM((8, 128), I32),
            pltpu.VMEM((256, 256), BF16),
            f32(64, 256),
            f32(64, 256),
            f32(64, 128),
            f32(256, LO),
            f32(8, 6, 128, 128),
            f32(2, 2, 128),
            f32(2, 128, LO),
            f32(2, 128, LO),
            f32(2, 8, 128),
            f32(2, 8, 128),
            f32(2, 2, 2, 128),
            f32(2, 4, 2, 128),
            pltpu.SemaphoreType.DMA((N_COPIES,)),
            pltpu.SemaphoreType.DMA((N_COPIES,)),
            pltpu.SemaphoreType.DMA((20,)),
        ],
        compiler_params=pltpu.CompilerParams(
            collective_id=0, has_side_effects=True, vmem_limit_bytes=VMEM_BYTES
        ),
    )(
        pd_disp,
        pd_vel,
        pd_coord,
        pd_modulus,
        pd_step,
        family,
        live,
        patch_tile,
        patch_blend,
        patch_nodes,
        patch_matrix,
        fe_disp,
        fe_vel,
        fe_step.reshape(-1, 128),
        fe_modulus.reshape(1, -1),
        element_nodes,
        shape_grad.reshape(-1, shape_grad.shape[2]),
        quad_weight.reshape(1, -1),
        shared_left,
        shared_right,
    )
    return pl.pallas_call(
        hand_over,
        out_shape=[jax.ShapeDtypeStruct(x.shape, F32) for x in results],
        in_specs=[vmem] * 4,
        out_specs=[hbm] * 4,
        scratch_shapes=[pltpu.SemaphoreType.DMA((4,))],
        compiler_params=pltpu.CompilerParams(vmem_limit_bytes=2**20),
    )(*results)


def solution(mesh):
    both = ("dom", "blk")
    return jax.shard_map(
        functools.partial(shards, mesh.shape["dom"]),
        mesh=mesh,
        in_specs=(
            P(both, None, None),
            P(both, None, None),
            P(both, None, None),
            P(both, None),
            P(both, None),
            P(both, None),
            P("dom"),
            P("dom"),
            P("dom", None),
            P(both, None),
            P(both, None, None),
            P(None, both),
            P(None, both),
            P(both),
            P(both),
            P(None, both),
            P(),
            P(),
            P("dom", None),
            P("dom", None),
        ),
        out_specs=(
            P(both, None, None),
            P(both, None, None),
            P(None, both),
            P(None, both),
        ),
        check_vma=False,
    )
```

```python
import functools

import jax
import jax.numpy as jnp
from jax import lax
from jax.experimental import pallas as pl
from jax.experimental.pallas import tpu as pltpu
from jax.sharding import PartitionSpec as P

MESH = pl.DeviceIdType.MESH
F32 = jnp.float32
BF16 = jnp.bfloat16
I32 = jnp.int32
EXACT = lax.Precision.HIGHEST

TIME_STEP = 0.5
CORE_SQ = 0.01
STRETCH = 0.3

LO = 256
HALF_ROWS = 25
PAD_ROWS = 32
CHUNK = 8
N_COPIES = 37
VMEM_BYTES = 60 * 2**20


def split2(x):
    top = x.astype(BF16)
    return top, (x - top.astype(F32)).astype(BF16)


def folded(x):
    return jnp.sum(x.reshape(-1, 8, x.shape[1]), axis=0)


def inverted(x):
    y = pl.reciprocal(x, approx=True)
    return y * (2.0 - x * y)


def nt(a, b, **kw):
    return lax.dot_general(
        a, b, (((1,), (1,)), ((), ())), preferred_element_type=F32, **kw
    )


def kernel(
    n_dom,
    disp_in,
    vel_in,
    coord_in,
    modulus_in,
    step_in,
    family_in,
    live_in,
    ptile_in,
    pblend_in,
    pnodes_in,
    pmat_in,
    fdisp_in,
    fvel_in,
    fstep_in,
    fmod_in,
    enodes_in,
    sgrad_in,
    qweight_in,
    sleft_in,
    sright_in,
    disp_out,
    vel_out,
    fdisp_out,
    fvel_out,
    disp,
    vel,
    coord,
    modulus,
    step,
    family,
    live,
    ptile,
    pblend,
    pnodes,
    fdisp,
    fvel,
    fstep,
    fmod,
    enodes,
    sgrad,
    qweight,
    sleft,
    sright,
    pdx,
    ub0,
    ub1,
    lists_in,
    lists_sent,
    lists,
    pm,
    table,
    speed,
    split_table,
    onehot,
    hrow,
    ids,
    link,
    del_,
    fel,
    sgt,
    acc,
    bonds,
    far_bonds,
    far_state,
    cur,
    pel_send,
    pel_recv,
    late_send,
    late_recv,
    bd_send,
    bd_recv,
    ssem,
    rsem,
    lsem,
):
    d = lax.axis_index("dom")
    b = lax.axis_index("blk")
    o = 1 - b
    has_left = d > 0
    has_right = d < n_dom - 1
    has_left2 = d > 1
    has_right2 = d < n_dom - 2
    left = jnp.maximum(d - 1, 0)
    right = jnp.minimum(d + 1, n_dom - 1)
    left2 = jnp.maximum(d - 2, 0)
    right2 = jnp.minimum(d + 2, n_dom - 1)
    peers = ((d, o),) + tuple(
        (x, j) for x in (left, right, left2, right2) for j in range(2)
    )
    there = (None,) + tuple(
        x for x in (has_left, has_right, has_left2, has_right2) for j in range(2)
    )

    def if_there(cond, act):
        if cond is None:
            act()
        else:
            pl.when(cond)(act)

    barrier = pltpu.get_barrier_semaphore()
    for peer, cond in zip(peers, there):
        if_there(
            cond,
            functools.partial(
                pl.semaphore_signal,
                barrier,
                inc=1,
                device_id=peer,
                device_id_type=MESH,
            ),
        )

    loads = {}
    for at, (src, dst) in enumerate(
        (
            (fdisp_in, fdisp),
            (coord_in, coord),
            (modulus_in, modulus),
            (disp_in, disp),
            (pnodes_in, pnodes),
            (pmat_in.at[0], pm.at[b]),
            (fvel_in, fvel),
            (fstep_in, fstep),
            (enodes_in, enodes),
            (vel_in, vel),
            (step_in, step),
            (family_in, family),
            (family_in, lists_in),
            (live_in, live),
            (ptile_in, ptile),
            (pblend_in, pblend),
            (fmod_in, fmod),
            (sgrad_in, sgrad),
            (qweight_in, qweight),
            (sleft_in, sleft),
            (sright_in, sright),
        )
    ):
        loads[at] = pltpu.make_async_copy(src, dst, lsem.at[at])
        loads[at].start()

    def loaded(*which):
        for at in which:
            loads[at].wait()

    started = []

    def send(src, dst, ssem_at, rsem_at, peer, cond):
        copy = pltpu.make_async_remote_copy(
            src_ref=src,
            dst_ref=dst,
            send_sem=ssem.at[ssem_at],
            recv_sem=rsem.at[rsem_at],
            device_id=peer,
            device_id_type=MESH,
        )
        if_there(cond, copy.start)
        started.append((copy, cond))

    def arrived(dst, rsem_at, cond):
        copy = pltpu.make_async_remote_copy(
            src_ref=dst,
            dst_ref=dst,
            send_sem=ssem.at[0],
            recv_sem=rsem.at[rsem_at],
            device_id=(d, o),
            device_id_type=MESH,
        )
        if_there(cond, copy.wait_recv)

    own = 8 + 2 * b
    theirs = 8 + 2 * o

    loaded(1, 2, 3, 4)
    for t in range(2):
        pdx[own + t] = jnp.concatenate(
            [
                coord[t],
                modulus[t : t + 1, :],
                disp[t],
                pnodes[...].astype(F32),
                jnp.zeros((2, 128), F32),
            ],
            axis=0,
        )
    loaded(0)
    table[b, 24:32, :] = jnp.zeros((8, LO), F32)
    table[b, 56:64, :] = jnp.zeros((8, LO), F32)
    for r in range(HALF_ROWS):
        for c in range(2):
            at = PAD_ROWS * c + r
            table[b, at : at + 1, :] = fdisp[c : c + 1, r * LO : (r + 1) * LO]
    loaded(6, 7)
    speed[b, 24:32, :] = jnp.zeros((8, LO), F32)
    speed[b, 56:64, :] = jnp.zeros((8, LO), F32)
    speed[b, 88:96, :] = jnp.zeros((8, LO), F32)
    for r in range(HALF_ROWS):
        for c in range(2):
            at = PAD_ROWS * c + r
            speed[b, at : at + 1, :] = fvel[c : c + 1, r * LO : (r + 1) * LO]
    for p in range(2):
        lanes = slice(p * 128, (p + 1) * 128)
        speed[b, 2 * PAD_ROWS : 2 * PAD_ROWS + HALF_ROWS, lanes] = fstep[
            pl.ds(p, HALF_ROWS, stride=2), :
        ]
    loaded(*range(8, 21))

    lo_iota = lax.broadcasted_iota(I32, (LO, 128), 0)

    def table_row(node):
        hi = lax.shift_right_arithmetic(node, 8)
        return jnp.where(hi >= HALF_ROWS, hi + (PAD_ROWS - HALF_ROWS), hi)

    def onehot_of(lo_row):
        return jnp.where(
            lo_iota == jnp.broadcast_to(lo_row, (LO, 128)), 1.0, 0.0
        ).astype(BF16)

    @pl.loop(0, 64 // CHUNK)
    def _(i):
        node = enodes[pl.ds(pl.multiple_of(i * CHUNK, CHUNK), CHUNK), :]
        hrow[pl.ds(pl.multiple_of(i * CHUNK, CHUNK), CHUNK), :] = table_row(node)
        lo = lax.bitwise_and(node, LO - 1)
        base = pl.multiple_of(i * (CHUNK * 128), CHUNK * 128)
        for g in range(CHUNK):
            onehot[:, pl.ds(base + g * 128, 128)] = onehot_of(lo[g : g + 1, :])

    sgt[...] = sgrad[...].T
    eye = lax.broadcasted_iota(I32, (64, 64), 0) == lax.broadcasted_iota(
        I32, (64, 64), 1
    )
    weight = jnp.sum(
        jnp.where(eye, jnp.broadcast_to(qweight[...], (64, 64)), 0.0),
        axis=1,
        keepdims=True,
    )
    scale = weight * fmod[...]


    lists_sent[2 + b] = jnp.zeros((8, 128), I32)
    lists_sent[2 + b, 0:2, 0:3] = lists_in[...]

    @pl.when(jnp.logical_not(has_left))
    def _():
        lists_sent[0:2] = jnp.zeros((2, 8, 128), I32)

    @pl.when(jnp.logical_not(has_right))
    def _():
        lists_sent[4:6] = jnp.zeros((2, 8, 128), I32)

    ids[...] = jnp.full((8, 128), -1, I32)
    ids[pl.ds(b, 1), :] = pnodes[...]
    ids[2:3, 0:113] = sleft[...]
    ids[3:4, 0:113] = sright[...]
    few_lo = lax.bitwise_and(ids[...], LO - 1)
    for g in (2, 3):
        onehot[:, 8192 + g * 128 : 8320 + g * 128] = onehot_of(few_lo[g : g + 1, :])

    pl.semaphore_wait(
        barrier, 1 + 2 * sum(x.astype(I32) for x in (has_left, has_right, has_left2, has_right2))
    )

    send(table.at[b], table.at[b], 0, 0, (d, o), None)
    slots = (own,) + tuple(x + 2 * b for x in (12, 12, 4, 4, 16, 16, 0, 0))
    marks = (0,) + tuple(x + b for x in (3, 3, 1, 1, 7, 7, 5, 5))
    homes = (2 + b,) + tuple(x + b for x in (4, 4, 0, 0))
    loaded(5)
    send(pm.at[b], pm.at[b], 1, 1, (d, o), None)
    for j in range(9):
        send(
            pdx.at[pl.ds(own, 2)],
            pdx.at[pl.ds(slots[j], 2)],
            3 + j,
            3 + marks[j],
            peers[j],
            there[j],
        )
    sources = (theirs, 4, 6, 12, 14, 0, 2, 16, 18)
    sources_lists = (2 + o, 0, 1, 4, 5)
    send(speed.at[b], speed.at[b], 2, 2, (d, o), None)
    states = (started[0][0], started.pop()[0])
    del started[0]
    for j in range(5):
        send(
            lists_sent.at[2 + b],
            lists_sent.at[homes[j]],
            12 + j,
            12 + marks[j],
            peers[j],
            there[j],
        )

    arrived(pdx.at[pl.ds(theirs, 2)], 3, None)
    ids[pl.ds(o, 1), :] = pdx[theirs, 5:6, :].astype(I32)
    few = ids[...]
    hrow[64:72, :] = table_row(few)
    few_lo = lax.bitwise_and(few, LO - 1)
    for g in range(2):
        onehot[:, 8192 + g * 128 : 8320 + g * 128] = onehot_of(few_lo[g : g + 1, :])

    OX, OY, REST, INFL0, NX, NY, STR, INFL = range(8)
    cur[...] = vel[...]

    def keep_pair(into, p, far, me):
        far_t = pdx[far].T
        for q in range(0, 128, 32):
            rows = slice(q, q + 32)
            ox = far_t[rows, 0:1] - me[0:1, :]
            oy = far_t[rows, 1:2] - me[1:2, :]
            r2 = ox * ox + oy * oy
            into[OX, p, rows] = ox
            into[OY, p, rows] = oy
            into[REST, p, rows] = jnp.sqrt(r2 + CORE_SQ)
            into[INFL0, p, rows] = jnp.exp(-0.5 * r2)

    def named(p):
        return family[p // 3, p % 3]

    def named_far(f, k):
        listed = lists[lax.shift_right_arithmetic(f, 1), lax.bitwise_and(f, 1), k]
        return listed + lax.shift_left(lax.shift_right_arithmetic(f, 2), 2)

    def keep_bonds():
        for p in range(6):
            keep_pair(bonds, p, named(p) + 4, pdx[own + p // 3])

        @pl.loop(0, 6)
        def _(p):
            t = p // 3
            f = family[t, p - 3 * t]
            me = pdx[f + 4]
            for k in range(3):
                keep_pair(far_bonds, 3 * p + k, named_far(f, k), me)

    def stretched(kept, p, rows, ub, far_t, me):
        yx = kept[OX, p, rows] + (far_t[rows, 0:1] - me[0:1, :])
        yy = kept[OY, p, rows] + (far_t[rows, 1:2] - me[1:2, :])
        y2 = yx * yx + yy * yy + CORE_SQ
        inverse = lax.rsqrt(y2)
        rest = kept[REST, p, rows]
        stretch = y2 * inverse - rest
        ratio = stretch * (1.0 / STRETCH)
        influence = kept[INFL0, p, rows] * inverted(1.0 + ratio * ratio)
        return yx, yy, inverse, rest, stretch, influence

    def columns(ub, far):
        return jnp.concatenate([ub[far], jnp.zeros((6, 128), F32)], axis=0).T

    def state_of(total):
        dilated, volume = [jnp.sum(x, axis=0, keepdims=True) for x in total]
        return jnp.concatenate([2.0 * dilated / volume, volume], axis=0)

    row_iota = lax.broadcasted_iota(I32, (64, 128), 0)

    def masked_rows(product, row):
        both = product[0:128] + product[128:256]
        hit = row_iota == jnp.broadcast_to(row, (64, 128))
        out = []
        for c in range(2):
            x = jnp.where(hit[0:32], both[c * 32 : c * 32 + 32], 0.0)
            x = x + jnp.where(hit[32:64], both[64 + c * 32 : 96 + c * 32], 0.0)
            out.append(jnp.sum(x, axis=0, keepdims=True))
        return out

    def spread(values, row):
        hit = row_iota == jnp.broadcast_to(row, (64, 128))
        blocks = []
        for part in range(2):
            wide = [
                jnp.where(hit, jnp.broadcast_to(values[part][c], (64, 128)), 0.0)
                for c in range(2)
            ]
            for half in range(2):
                for c in range(2):
                    blocks.append(wide[c][half * 32 : half * 32 + 32])
        return jnp.concatenate(blocks, axis=0).astype(BF16)

    for s in range(2):
        ub = (ub0, ub1)[s]
        base = 17 + 10 * s
        if s == 0:
            arrived(table.at[o], 0, None)
            arrived(pm.at[o], 1, None)

        top, low = split2(table[...].reshape(128, LO))
        split_table[0:128, :] = top
        split_table[128:256, :] = low
        product = jnp.dot(
            split_table[...], onehot[:, 8192:8448], preferred_element_type=F32
        )
        targets = []
        for q in range(2):
            picked = masked_rows(
                product[:, q * 128 : (q + 1) * 128], hrow[64 + q : 65 + q, :]
            )
            picked = jnp.concatenate(picked + [jnp.zeros((6, 128), F32)], axis=0)
            targets.append(nt(picked, pm[q], precision=EXACT)[0:2, :])
        for k in range(4):
            if s == 0:
                u = pdx[8 + k, 3:5, :]
            else:
                u = ub[8 + k]
            new = u
            for q in range(2):
                hit = jnp.full((2, 128), ptile[q], I32) == k
                new = jnp.where(
                    hit, u + pblend[q : q + 1, :] * (targets[q] - u), new
                )
            ub[8 + k] = new
        mine = ub.at[pl.ds(8, 4)]
        for j, (to, at, peer, cond) in enumerate(
            (
                (16, 3, left2, has_left2),
                (0, 2, right2, has_right2),
                (12, 1, left, has_left),
                (4, 0, right, has_right),
            )
        ):
            send(mine, ub.at[pl.ds(to, 4)], base + j, base + at, (peer, b), cond)

        @pl.loop(0, 64 // CHUNK)
        def _(i):
            rows = pl.ds(pl.multiple_of(i * CHUNK, CHUNK), CHUNK)
            lanes = pl.ds(pl.multiple_of(i * (CHUNK * 128), CHUNK * 128), CHUNK * 128)
            product = jnp.dot(
                split_table[...], onehot[:, lanes], preferred_element_type=F32
            )
            row = hrow[rows, :]
            found = [
                masked_rows(product[:, g * 128 : (g + 1) * 128], row[g : g + 1, :])
                for g in range(CHUNK)
            ]
            for c in range(2):
                del_[rows, c * 128 : (c + 1) * 128] = jnp.concatenate(
                    [f[c] for f in found], axis=0
                )

        if s == 0:
            few_f = ids[...].astype(F32)
            few_t = few_f.T
            for q in range(2):
                for side in range(2):
                    link[
                        q * 128 : (q + 1) * 128, side * 128 : (side + 1) * 128
                    ] = jnp.where(
                        few_t[:, q : q + 1] == few_f[2 + side : 3 + side, :], 1.0, 0.0
                    ).astype(BF16)

        grad = jnp.dot(sgrad[...], del_[...], precision=EXACT, preferred_element_type=F32)
        exx = grad[0:64, 0:128]
        eyy = grad[64:128, 128:256]
        exy = 0.5 * (grad[64:128, 0:128] + grad[0:64, 128:256])
        scaled = scale * (1.0 + exx * exx + eyy * eyy + 2.0 * exy * exy)
        both = exx + eyy
        sxx = scaled * (both + 2.0 * exx)
        syy = scaled * (both + 2.0 * eyy)
        sxy = scaled * 2.0 * exy
        stress = jnp.concatenate(
            [
                jnp.concatenate([sxx, sxy], axis=1),
                jnp.concatenate([sxy, syy], axis=1),
            ],
            axis=0,
        )
        fel[...] = jnp.dot(sgt[...], stress, precision=EXACT, preferred_element_type=F32)
        acc[...] = jnp.zeros((256, LO), F32)

        @pl.loop(0, 64 // CHUNK)
        def _(i):
            rows = pl.ds(pl.multiple_of(i * CHUNK, CHUNK), CHUNK)
            lanes = pl.ds(pl.multiple_of(i * (CHUNK * 128), CHUNK * 128), CHUNK * 128)
            row = hrow[rows, :]
            f = fel[rows, :]
            f_top = f.astype(BF16).astype(F32)
            f_low = f - f_top
            left_side = jnp.concatenate(
                [
                    spread(
                        [
                            [x[g : g + 1, 0:128], x[g : g + 1, 128:256]]
                            for x in (f_top, f_low)
                        ],
                        row[g : g + 1, :],
                    )
                    for g in range(CHUNK)
                ],
                axis=1,
            )
            acc[...] += nt(left_side, onehot[:, lanes])

        partial = acc[0:128, :] + acc[128:256, :]
        pel_send[s] = partial
        if s == 0:
            send(pel_send.at[s], pel_recv.at[s], base + 4, base + 4, (d, o), None)
        else:
            cut = pl.ds(o * 64, 64)
            send(
                pel_send.at[s, cut],
                pel_recv.at[s, cut],
                base + 4,
                base + 4,
                (d, o),
                None,
            )
        top, low = split2(partial)
        product = jnp.dot(
            jnp.concatenate([top, low], axis=0),
            onehot[:, 8448:8704],
            preferred_element_type=F32,
        )
        border = []
        for side in range(2):
            found = masked_rows(
                product[:, side * 128 : (side + 1) * 128],
                hrow[66 + side : 67 + side, :],
            )
            border.append(jnp.concatenate(found, axis=0))

        if s == 0:
            for j in range(1, 9):
                arrived(pdx.at[pl.ds(sources[j], 2)], 3 + j, there[j])
            for j in range(5):
                arrived(lists_sent.at[sources_lists[j]], 12 + j, there[j])
            scalars = pltpu.make_async_copy(lists_sent, lists, lsem.at[21])
            scalars.start()
            scalars.wait()
            keep_bonds()

        for at, (frm, cond) in enumerate(
            ((4, has_left), (12, has_right), (0, has_left2), (16, has_right2))
        ):
            arrived(ub.at[pl.ds(frm, 4)], base + at, cond)

        @pl.loop(0, 3)
        def _(i):
            for j in range(2):
                p = 2 * i + j
                t = p // 3
                f = family[t, p - 3 * t]
                me = ub[f + 4]
                total = [jnp.zeros((8, 128), F32)] * 2
                for k in range(3):
                    far_t = columns(ub, named_far(f, k))
                    for q in range(0, 128, 32):
                        *_, rest, stretch, influence = stretched(
                            far_bonds, 3 * p + k, slice(q, q + 32), ub, far_t, me
                        )
                        weighted = influence * rest
                        total[0] = total[0] + folded(weighted * stretch)
                        total[1] = total[1] + folded(weighted * rest)
                far_state[p] = state_of(total)

        totals = [[jnp.zeros((8, 128), F32)] * 2 for _ in range(2)]
        for p in range(6):
            t = p // 3
            far_t = columns(ub, named(p) + 4)
            me = ub[own + t]
            for q in range(0, 128, 32):
                rows = slice(q, q + 32)
                yx, yy, inverse, rest, stretch, influence = stretched(
                    bonds, p, rows, ub, far_t, me
                )
                bonds[NX, p, rows] = yx * inverse
                bonds[NY, p, rows] = yy * inverse
                bonds[STR, p, rows] = stretch
                bonds[INFL, p, rows] = influence
                weighted = influence * rest
                totals[t][0] = totals[t][0] + folded(weighted * stretch)
                totals[t][1] = totals[t][1] + folded(weighted * rest)
        states_own = [state_of(x) for x in totals]

        def coefficients(k, state):
            theta, volume = state[0:1, :], state[1:2, :]
            return 2.0 * k * theta / volume, 4.0 * k / volume, 0.5 * theta

        totals = [[jnp.zeros((8, 128), F32)] * 2 for _ in range(2)]
        near = [coefficients(pdx[own + t][2:3, :], states_own[t]) for t in range(2)]
        for p in range(6):
            t = p // 3
            far = coefficients(pdx[named(p) + 4][2:3, :], far_state[p])
            far_t = jnp.concatenate(far + (jnp.zeros((5, 128), F32),), axis=0).T
            oa, ob, oc = near[t]
            for q in range(0, 128, 32):
                rows = slice(q, q + 32)
                rest = bonds[REST, p, rows]
                stretch = bonds[STR, p, rows]
                mine = oa * rest + ob * (stretch - oc * rest)
                away = far_t[rows, 0:1] * rest + far_t[rows, 1:2] * (
                    stretch - far_t[rows, 2:3] * rest
                )
                force = bonds[INFL, p, rows] * (mine + away)
                totals[t][0] = totals[t][0] + folded(force * bonds[NX, p, rows])
                totals[t][1] = totals[t][1] + folded(force * bonds[NY, p, rows])

        forces, moved = [], []
        for t in range(2):
            alive = jnp.full((2, 128), 2 * b + t, I32) < live[0]
            total = [jnp.sum(x, axis=0, keepdims=True) for x in totals[t]]
            force = jnp.where(alive, jnp.concatenate(total, axis=0), 0.0)
            forces.append(force)
            v = jnp.where(alive, cur[t] + step[t : t + 1, :] * force, 0.0)
            u = jnp.where(alive, ub[own + t] + TIME_STEP * v, 0.0)
            cur[t] = v
            moved.append(u)

        reaction = []
        for q in range(2):
            w = jnp.zeros((2, 128), F32)
            for t in range(2):
                hit = jnp.full((2, 128), ptile[q], I32) == 2 * b + t
                w = w + jnp.where(hit, pblend[q : q + 1, :] * forces[t], 0.0)
            w = jnp.concatenate([w, jnp.zeros((6, 128), F32)], axis=0)
            reaction.append(
                jnp.dot(w, pm[q], precision=EXACT, preferred_element_type=F32)[0:2, :]
            )
        late = jnp.concatenate(reaction + moved, axis=0)
        late_send[s] = late
        send(late_send.at[s], late_recv.at[s], base + 5, base + 5, (d, o), None)
        wide = jnp.concatenate(reaction, axis=1)
        top, low = split2(wide)
        met = jnp.dot(
            jnp.concatenate([top, low, jnp.zeros((12, 256), BF16)], axis=0),
            link[...],
            preferred_element_type=F32,
        )
        met = met[0:2, :] + met[2:4, :]
        for side in range(2):
            bd_send[s, side] = met[:, side * 128 : (side + 1) * 128] - border[side]
        for j in range(4):
            side = j // 2
            send(
                bd_send.at[s, side],
                bd_recv.at[s, 2 * (1 - side) + b],
                base + 6 + j,
                base + 6 + 2 * (1 - side) + b,
                peers[1 + j],
                there[1 + j],
            )
        if s == 0:
            for t in range(2):
                ub1[own + t] = moved[t]
        else:
            for t in range(2):
                disp_out[t] = moved[t]
                vel_out[t] = cur[t]

        halves = range(2) if s == 0 else (b,)
        if s == 0:
            arrived(speed.at[o], 2, None)
            arrived(pel_recv.at[s], base + 4, None)
            for copy in states:
                copy.wait_send()
        else:
            arrived(pel_recv.at[s, pl.ds(b * 64, 64)], base + 4, None)
        for h in halves:
            for c in range(2):
                cut = pl.ds(h * 64 + c * 32, 32)
                rows = slice(c * 32, c * 32 + 32)
                speed[h, rows, :] = speed[h, rows, :] - speed[h, 64:96, :] * (
                    pel_send[s, cut, :] + pel_recv[s, cut, :]
                )
        arrived(late_recv.at[s], base + 5, None)
        other = late_recv[s]
        if s == 0:
            for t in range(2):
                ub1[theirs + t] = other[4 + 2 * t : 6 + 2 * t, :]
        for j in range(4):
            arrived(bd_recv.at[s, j], base + 6 + j, there[1 + j])
        shared = [
            jnp.where(
                jnp.full((2, 128), d, I32) > 0, bd_recv[s, 0] + bd_recv[s, 1], 0.0
            ),
            jnp.where(
                jnp.full((2, 128), d, I32) < n_dom - 1,
                bd_recv[s, 2] + bd_recv[s, 3],
                0.0,
            ),
        ]
        sides = []
        for g, x in enumerate(
            [late[0:2, :] + other[0:2, :], late[2:4, :] + other[2:4, :]] + shared
        ):
            x_top = x.astype(BF16).astype(F32)
            x_low = x - x_top
            sides.append(
                spread(
                    [[y[0:1, :], y[1:2, :]] for y in (x_top, x_low)],
                    hrow[64 + g : 65 + g, :],
                )
            )
        extra = nt(jnp.concatenate(sides, axis=1), onehot[:, 8192:8704])
        acc[0:128, :] = extra[0:128, :] + extra[128:256, :]
        for h in halves:
            for c in range(2):
                cut = pl.ds(h * 64 + c * 32, 32)
                rows = slice(c * 32, c * 32 + 32)
                v = speed[h, rows, :] + speed[h, 64:96, :] * acc[cut, :]
                speed[h, rows, :] = v
                table[h, rows, :] = table[h, rows, :] + TIME_STEP * v

    for r in range(HALF_ROWS):
        lanes = slice(r * LO, (r + 1) * LO)
        for c in range(2):
            at = PAD_ROWS * c + r
            fdisp_out[c : c + 1, lanes] = table[b, at : at + 1, :]
            fvel_out[c : c + 1, lanes] = speed[b, at : at + 1, :]
    for copy, cond in started:
        if_there(cond, copy.wait_send)


def hand_over(*refs):
    ins, outs, sems = refs[:4], refs[4:8], refs[8]
    copies = [
        pltpu.make_async_copy(src, dst, sems.at[at])
        for at, (src, dst) in enumerate(zip(ins, outs))
    ]
    for copy in copies:
        copy.start()
    for copy in copies:
        copy.wait()


def shards(n_dom, *args):
    (
        pd_disp,
        pd_vel,
        pd_coord,
        pd_modulus,
        pd_step,
        family,
        live,
        patch_tile,
        patch_blend,
        patch_nodes,
        patch_matrix,
        fe_disp,
        fe_vel,
        fe_step,
        fe_modulus,
        element_nodes,
        shape_grad,
        quad_weight,
        shared_left,
        shared_right,
    ) = args
    vmem = pl.BlockSpec(memory_space=pltpu.VMEM)
    hbm = pl.BlockSpec(memory_space=pltpu.HBM)
    rows = fe_step.shape[0] // 128

    def f32(*shape):
        return pltpu.VMEM(shape, F32)

    results = pl.pallas_call(
        functools.partial(kernel, n_dom),
        out_shape=[
            pltpu.VMEM(pd_disp.shape, F32),
            pltpu.VMEM(pd_vel.shape, F32),
            pltpu.VMEM(fe_disp.shape, F32),
            pltpu.VMEM(fe_vel.shape, F32),
        ],
        in_specs=[hbm] * 20,
        out_specs=[vmem] * 4,
        scratch_shapes=[
            f32(2, 2, 128),
            f32(2, 2, 128),
            f32(2, 2, 128),
            f32(2, 128),
            f32(2, 128),
            pltpu.SMEM((2, 3), I32),
            pltpu.SMEM((1,), I32),
            pltpu.SMEM((2,), I32),
            f32(2, 128),
            pltpu.VMEM((1, 128), I32),
            f32(*fe_disp.shape),
            f32(*fe_vel.shape),
            f32(rows, 128),
            f32(1, 128),
            pltpu.VMEM((64, 128), I32),
            f32(128, 64),
            f32(1, 64),
            pltpu.VMEM((1, 113), I32),
            pltpu.VMEM((1, 113), I32),
            f32(20, 8, 128),
            f32(20, 2, 128),
            f32(20, 2, 128),
            pltpu.VMEM((2, 3), I32),
            pltpu.VMEM((6, 8, 128), I32),
            pltpu.SMEM((6, 8, 128), I32),
            f32(2, 128, 128),
            f32(2, 64, LO),
            f32(2, 96, LO),
            pltpu.VMEM((256, LO), BF16),
            pltpu.VMEM((LO, 8704), BF16),
            pltpu.VMEM((72, 128), I32),
            pltpu.VMEM((8, 128), I32),
            pltpu.VMEM((256, 256), BF16),
            f32(64, 256),
            f32(64, 256),
            f32(64, 128),
            f32(256, LO),
            f32(8, 6, 128, 128),
            f32(4, 18, 128, 128),
            f32(6, 2, 128),
            f32(2, 2, 128),
            f32(2, 128, LO),
            f32(2, 128, LO),
            f32(2, 8, 128),
            f32(2, 8, 128),
            f32(2, 2, 2, 128),
            f32(2, 4, 2, 128),
            pltpu.SemaphoreType.DMA((N_COPIES,)),
            pltpu.SemaphoreType.DMA((N_COPIES,)),
            pltpu.SemaphoreType.DMA((22,)),
        ],
        compiler_params=pltpu.CompilerParams(
            collective_id=0, has_side_effects=True, vmem_limit_bytes=VMEM_BYTES
        ),
    )(
        pd_disp,
        pd_vel,
        pd_coord,
        pd_modulus,
        pd_step,
        family,
        live,
        patch_tile,
        patch_blend,
        patch_nodes,
        patch_matrix,
        fe_disp,
        fe_vel,
        fe_step.reshape(-1, 128),
        fe_modulus.reshape(1, -1),
        element_nodes,
        shape_grad.reshape(-1, shape_grad.shape[2]),
        quad_weight.reshape(1, -1),
        shared_left,
        shared_right,
    )
    return pl.pallas_call(
        hand_over,
        out_shape=[jax.ShapeDtypeStruct(x.shape, F32) for x in results],
        in_specs=[vmem] * 4,
        out_specs=[hbm] * 4,
        scratch_shapes=[pltpu.SemaphoreType.DMA((4,))],
        compiler_params=pltpu.CompilerParams(vmem_limit_bytes=2**20),
    )(*results)


def solution(mesh):
    both = ("dom", "blk")
    return jax.shard_map(
        functools.partial(shards, mesh.shape["dom"]),
        mesh=mesh,
        in_specs=(
            P(both, None, None),
            P(both, None, None),
            P(both, None, None),
            P(both, None),
            P(both, None),
            P(both, None),
            P("dom"),
            P("dom"),
            P("dom", None),
            P(both, None),
            P(both, None, None),
            P(None, both),
            P(None, both),
            P(both),
            P(both),
            P(None, both),
            P(),
            P(),
            P("dom", None),
            P("dom", None),
        ),
        out_specs=(
            P(both, None, None),
            P(both, None, None),
            P(None, both),
            P(None, both),
        ),
        check_vma=False,
    )
```

```python
import functools

import jax
import jax.numpy as jnp
from jax import lax
from jax.experimental import pallas as pl
from jax.experimental.pallas import tpu as pltpu
from jax.sharding import PartitionSpec as P

MESH = pl.DeviceIdType.MESH
F32 = jnp.float32
BF16 = jnp.bfloat16
I32 = jnp.int32
EXACT = lax.Precision.HIGHEST

TIME_STEP = 0.5
CORE_SQ = 0.01
STRETCH = 0.3

LO = 256
HALF_ROWS = 25
PAD_ROWS = 32
CHUNK = 8
N_COPIES = 37
VMEM_BYTES = 60 * 2**20


def split2(x):
    top = x.astype(BF16)
    return top, (x - top.astype(F32)).astype(BF16)


def folded(x):
    return jnp.sum(x.reshape(-1, 8, x.shape[1]), axis=0)


def inverted(x):
    y = pl.reciprocal(x, approx=True)
    return y * (2.0 - x * y)


def nt(a, b, **kw):
    return lax.dot_general(
        a, b, (((1,), (1,)), ((), ())), preferred_element_type=F32, **kw
    )


def kernel(
    n_dom,
    disp_in,
    vel_in,
    coord_in,
    modulus_in,
    step_in,
    family_in,
    live_in,
    ptile_in,
    pblend_in,
    pnodes_in,
    pmat_in,
    fdisp_in,
    fvel_in,
    fstep_in,
    fmod_in,
    enodes_in,
    sgrad_in,
    qweight_in,
    sleft_in,
    sright_in,
    disp_out,
    vel_out,
    fdisp_out,
    fvel_out,
    disp,
    vel,
    coord,
    modulus,
    step,
    family,
    live,
    ptile,
    pblend,
    pnodes,
    fdisp,
    fvel,
    fstep,
    fmod,
    enodes,
    sgrad,
    qweight,
    sleft,
    sright,
    pdx,
    ub0,
    ub1,
    place,
    lists_in,
    lists_sent,
    lists,
    pm,
    table,
    speed,
    split_table,
    onehot,
    hrow,
    ids,
    link,
    del_,
    fel,
    sgt,
    acc,
    bonds,
    far_bonds,
    far_state,
    cur,
    pel_send,
    pel_recv,
    late_send,
    late_recv,
    bd_send,
    bd_recv,
    ssem,
    rsem,
    lsem,
):
    d = lax.axis_index("dom")
    b = lax.axis_index("blk")
    o = 1 - b
    has_left = d > 0
    has_right = d < n_dom - 1
    has_left2 = d > 1
    has_right2 = d < n_dom - 2
    left = jnp.maximum(d - 1, 0)
    right = jnp.minimum(d + 1, n_dom - 1)
    left2 = jnp.maximum(d - 2, 0)
    right2 = jnp.minimum(d + 2, n_dom - 1)
    peers = ((d, o),) + tuple(
        (x, j) for x in (left, right, left2, right2) for j in range(2)
    )
    there = (None,) + tuple(
        x for x in (has_left, has_right, has_left2, has_right2) for j in range(2)
    )

    def if_there(cond, act):
        if cond is None:
            act()
        else:
            pl.when(cond)(act)

    barrier = pltpu.get_barrier_semaphore()
    for peer, cond in zip(peers, there):
        if_there(
            cond,
            functools.partial(
                pl.semaphore_signal,
                barrier,
                inc=1,
                device_id=peer,
                device_id_type=MESH,
            ),
        )

    loads = {}
    for at, (src, dst) in enumerate(
        (
            (fdisp_in, fdisp),
            (coord_in, coord),
            (modulus_in, modulus),
            (disp_in, disp),
            (pnodes_in, pnodes),
            (pmat_in.at[0], pm.at[b]),
            (fvel_in, fvel),
            (fstep_in, fstep),
            (enodes_in, enodes),
            (vel_in, vel),
            (step_in, step),
            (family_in, family),
            (family_in, lists_in),
            (live_in, live),
            (ptile_in, ptile),
            (pblend_in, pblend),
            (fmod_in, fmod),
            (sgrad_in, sgrad),
            (qweight_in, qweight),
            (sleft_in, sleft),
            (sright_in, sright),
        )
    ):
        loads[at] = pltpu.make_async_copy(src, dst, lsem.at[at])
        loads[at].start()

    def loaded(*which):
        for at in which:
            loads[at].wait()

    started = []

    def send(src, dst, ssem_at, rsem_at, peer, cond):
        copy = pltpu.make_async_remote_copy(
            src_ref=src,
            dst_ref=dst,
            send_sem=ssem.at[ssem_at],
            recv_sem=rsem.at[rsem_at],
            device_id=peer,
            device_id_type=MESH,
        )
        if_there(cond, copy.start)
        started.append((copy, cond))

    def arrived(dst, rsem_at, cond):
        copy = pltpu.make_async_remote_copy(
            src_ref=dst,
            dst_ref=dst,
            send_sem=ssem.at[0],
            recv_sem=rsem.at[rsem_at],
            device_id=(d, o),
            device_id_type=MESH,
        )
        if_there(cond, copy.wait_recv)

    own = 8 + 2 * b
    theirs = 8 + 2 * o

    loaded(1, 2, 3, 4)
    for t in range(2):
        pdx[own + t] = jnp.concatenate(
            [
                coord[t],
                modulus[t : t + 1, :],
                disp[t],
                pnodes[...].astype(F32),
                jnp.zeros((2, 128), F32),
            ],
            axis=0,
        )
    loaded(0)
    table[b, 24:32, :] = jnp.zeros((8, LO), F32)
    table[b, 56:64, :] = jnp.zeros((8, LO), F32)
    for r in range(HALF_ROWS):
        for c in range(2):
            at = PAD_ROWS * c + r
            table[b, at : at + 1, :] = fdisp[c : c + 1, r * LO : (r + 1) * LO]
    loaded(6, 7)
    speed[b, 24:32, :] = jnp.zeros((8, LO), F32)
    speed[b, 56:64, :] = jnp.zeros((8, LO), F32)
    speed[b, 88:96, :] = jnp.zeros((8, LO), F32)
    for r in range(HALF_ROWS):
        for c in range(2):
            at = PAD_ROWS * c + r
            speed[b, at : at + 1, :] = fvel[c : c + 1, r * LO : (r + 1) * LO]
    for p in range(2):
        lanes = slice(p * 128, (p + 1) * 128)
        speed[b, 2 * PAD_ROWS : 2 * PAD_ROWS + HALF_ROWS, lanes] = fstep[
            pl.ds(p, HALF_ROWS, stride=2), :
        ]
    loaded(*range(8, 21))

    lo_iota = lax.broadcasted_iota(I32, (LO, 128), 0)

    def table_row(node):
        hi = lax.shift_right_arithmetic(node, 8)
        return jnp.where(hi >= HALF_ROWS, hi + (PAD_ROWS - HALF_ROWS), hi)

    def onehot_of(lo_row):
        return jnp.where(
            lo_iota == jnp.broadcast_to(lo_row, (LO, 128)), 1.0, 0.0
        ).astype(BF16)

    @pl.loop(0, 64 // CHUNK, unroll=2)
    def _(i):
        node = enodes[pl.ds(pl.multiple_of(i * CHUNK, CHUNK), CHUNK), :]
        hrow[pl.ds(pl.multiple_of(i * CHUNK, CHUNK), CHUNK), :] = table_row(node)
        lo = lax.bitwise_and(node, LO - 1)
        base = pl.multiple_of(i * (CHUNK * 128), CHUNK * 128)
        for g in range(CHUNK):
            onehot[:, pl.ds(base + g * 128, 128)] = onehot_of(lo[g : g + 1, :])

    sgt[...] = sgrad[...].T
    eye = lax.broadcasted_iota(I32, (64, 64), 0) == lax.broadcasted_iota(
        I32, (64, 64), 1
    )
    weight = jnp.sum(
        jnp.where(eye, jnp.broadcast_to(qweight[...], (64, 64)), 0.0),
        axis=1,
        keepdims=True,
    )
    scale = weight * fmod[...]


    lists_sent[2 + b] = jnp.zeros((8, 128), I32)
    lists_sent[2 + b, 0:2, 0:3] = lists_in[...]

    @pl.when(jnp.logical_not(has_left))
    def _():
        lists_sent[0:2] = jnp.zeros((2, 8, 128), I32)

    @pl.when(jnp.logical_not(has_right))
    def _():
        lists_sent[4:6] = jnp.zeros((2, 8, 128), I32)

    ids[...] = jnp.full((8, 128), -1, I32)
    ids[pl.ds(b, 1), :] = pnodes[...]
    ids[2:3, 0:113] = sleft[...]
    ids[3:4, 0:113] = sright[...]
    few_lo = lax.bitwise_and(ids[...], LO - 1)
    for g in (2, 3):
        onehot[:, 8192 + g * 128 : 8320 + g * 128] = onehot_of(few_lo[g : g + 1, :])

    pl.semaphore_wait(
        barrier, 1 + 2 * sum(x.astype(I32) for x in (has_left, has_right, has_left2, has_right2))
    )

    send(table.at[b], table.at[b], 0, 0, (d, o), None)
    slots = (own,) + tuple(x + 2 * b for x in (12, 12, 4, 4, 16, 16, 0, 0))
    marks = (0,) + tuple(x + b for x in (3, 3, 1, 1, 7, 7, 5, 5))
    homes = (2 + b,) + tuple(x + b for x in (4, 4, 0, 0))
    loaded(5)
    send(pm.at[b], pm.at[b], 1, 1, (d, o), None)
    for j in range(9):
        send(
            pdx.at[pl.ds(own, 2)],
            pdx.at[pl.ds(slots[j], 2)],
            3 + j,
            3 + marks[j],
            peers[j],
            there[j],
        )
    sources = (theirs, 4, 6, 12, 14, 0, 2, 16, 18)
    sources_lists = (2 + o, 0, 1, 4, 5)
    send(speed.at[b], speed.at[b], 2, 2, (d, o), None)
    states = (started[0][0], started.pop()[0])
    del started[0]
    for j in range(5):
        send(
            lists_sent.at[2 + b],
            lists_sent.at[homes[j]],
            12 + j,
            12 + marks[j],
            peers[j],
            there[j],
        )

    arrived(pdx.at[pl.ds(theirs, 2)], 3, None)
    ids[pl.ds(o, 1), :] = pdx[theirs, 5:6, :].astype(I32)
    few = ids[...]
    hrow[64:72, :] = table_row(few)
    few_lo = lax.bitwise_and(few, LO - 1)
    for g in range(2):
        onehot[:, 8192 + g * 128 : 8320 + g * 128] = onehot_of(few_lo[g : g + 1, :])

    REST, INFL0, NX, NY, STR, INFL = range(6)
    cur[...] = vel[...]

    def keep_pair(into, p, far, me):
        far_t = pdx[far].T
        for q in range(0, 128, 32):
            rows = slice(q, q + 32)
            ox = far_t[rows, 0:1] - me[0:1, :]
            oy = far_t[rows, 1:2] - me[1:2, :]
            r2 = ox * ox + oy * oy
            into[REST, p, rows] = jnp.sqrt(r2 + CORE_SQ)
            into[INFL0, p, rows] = jnp.exp(-0.5 * r2)

    def named(p):
        return family[p // 3, p % 3]

    def named_far(f, k):
        listed = lists[lax.shift_right_arithmetic(f, 1), lax.bitwise_and(f, 1), k]
        return listed + lax.shift_left(lax.shift_right_arithmetic(f, 2), 2)

    def keep_bonds():
        for p in range(6):
            keep_pair(bonds, p, named(p) + 4, pdx[own + p // 3])

        @pl.loop(0, 6, unroll=2)
        def _(p):
            t = p // 3
            f = family[t, p - 3 * t]
            me = pdx[f + 4]
            for k in range(3):
                keep_pair(far_bonds, 3 * p + k, named_far(f, k), me)

    def stretched(kept, p, rows, far_t, me):
        yx = far_t[rows, 0:1] - me[0:1, :]
        yy = far_t[rows, 1:2] - me[1:2, :]
        y2 = yx * yx + yy * yy + CORE_SQ
        inverse = lax.rsqrt(y2)
        rest = kept[REST, p, rows]
        stretch = y2 * inverse - rest
        ratio = stretch * (1.0 / STRETCH)
        influence = kept[INFL0, p, rows] * inverted(1.0 + ratio * ratio)
        return yx, yy, inverse, rest, stretch, influence

    def columns(far):
        return jnp.concatenate([place[far], jnp.zeros((6, 128), F32)], axis=0).T

    def state_of(total):
        dilated, volume = [jnp.sum(x, axis=0, keepdims=True) for x in total]
        return jnp.concatenate([2.0 * dilated / volume, volume], axis=0)

    row_iota = lax.broadcasted_iota(I32, (64, 128), 0)

    def masked_rows(product, row):
        both = product[0:128] + product[128:256]
        hit = row_iota == jnp.broadcast_to(row, (64, 128))
        out = []
        for c in range(2):
            x = jnp.where(hit[0:32], both[c * 32 : c * 32 + 32], 0.0)
            x = x + jnp.where(hit[32:64], both[64 + c * 32 : 96 + c * 32], 0.0)
            out.append(jnp.sum(x, axis=0, keepdims=True))
        return out

    def spread(values, row):
        hit = row_iota == jnp.broadcast_to(row, (64, 128))
        blocks = []
        for part in range(2):
            wide = [
                jnp.where(hit, jnp.broadcast_to(values[part][c], (64, 128)), 0.0)
                for c in range(2)
            ]
            for half in range(2):
                for c in range(2):
                    blocks.append(wide[c][half * 32 : half * 32 + 32])
        return jnp.concatenate(blocks, axis=0).astype(BF16)

    for s in range(2):
        ub = (ub0, ub1)[s]
        base = 17 + 10 * s
        if s == 0:
            arrived(table.at[o], 0, None)
            arrived(pm.at[o], 1, None)

        top, low = split2(table[...].reshape(128, LO))
        split_table[0:128, :] = top
        split_table[128:256, :] = low
        product = jnp.dot(
            split_table[...], onehot[:, 8192:8448], preferred_element_type=F32
        )
        targets = []
        for q in range(2):
            picked = masked_rows(
                product[:, q * 128 : (q + 1) * 128], hrow[64 + q : 65 + q, :]
            )
            picked = jnp.concatenate(picked + [jnp.zeros((6, 128), F32)], axis=0)
            targets.append(nt(picked, pm[q], precision=EXACT)[0:2, :])
        for k in range(4):
            if s == 0:
                u = pdx[8 + k, 3:5, :]
            else:
                u = ub[8 + k]
            new = u
            for q in range(2):
                hit = jnp.full((2, 128), ptile[q], I32) == k
                new = jnp.where(
                    hit, u + pblend[q : q + 1, :] * (targets[q] - u), new
                )
            ub[8 + k] = new
        mine = ub.at[pl.ds(8, 4)]
        for j, (to, at, peer, cond) in enumerate(
            (
                (16, 3, left2, has_left2),
                (0, 2, right2, has_right2),
                (12, 1, left, has_left),
                (4, 0, right, has_right),
            )
        ):
            send(mine, ub.at[pl.ds(to, 4)], base + j, base + at, (peer, b), cond)

        @pl.loop(0, 64 // CHUNK, unroll=2)
        def _(i):
            rows = pl.ds(pl.multiple_of(i * CHUNK, CHUNK), CHUNK)
            lanes = pl.ds(pl.multiple_of(i * (CHUNK * 128), CHUNK * 128), CHUNK * 128)
            product = jnp.dot(
                split_table[...], onehot[:, lanes], preferred_element_type=F32
            )
            row = hrow[rows, :]
            found = [
                masked_rows(product[:, g * 128 : (g + 1) * 128], row[g : g + 1, :])
                for g in range(CHUNK)
            ]
            for c in range(2):
                del_[rows, c * 128 : (c + 1) * 128] = jnp.concatenate(
                    [f[c] for f in found], axis=0
                )

        if s == 0:
            few_f = ids[...].astype(F32)
            few_t = few_f.T
            for q in range(2):
                for side in range(2):
                    link[
                        q * 128 : (q + 1) * 128, side * 128 : (side + 1) * 128
                    ] = jnp.where(
                        few_t[:, q : q + 1] == few_f[2 + side : 3 + side, :], 1.0, 0.0
                    ).astype(BF16)

        grad = jnp.dot(sgrad[...], del_[...], precision=EXACT, preferred_element_type=F32)
        exx = grad[0:64, 0:128]
        eyy = grad[64:128, 128:256]
        exy = 0.5 * (grad[64:128, 0:128] + grad[0:64, 128:256])
        scaled = scale * (1.0 + exx * exx + eyy * eyy + 2.0 * exy * exy)
        both = exx + eyy
        sxx = scaled * (both + 2.0 * exx)
        syy = scaled * (both + 2.0 * eyy)
        sxy = scaled * 2.0 * exy
        stress = jnp.concatenate(
            [
                jnp.concatenate([sxx, sxy], axis=1),
                jnp.concatenate([sxy, syy], axis=1),
            ],
            axis=0,
        )
        fel[...] = jnp.dot(sgt[...], stress, precision=EXACT, preferred_element_type=F32)
        acc[...] = jnp.zeros((256, LO), F32)

        @pl.loop(0, 64 // CHUNK, unroll=2)
        def _(i):
            rows = pl.ds(pl.multiple_of(i * CHUNK, CHUNK), CHUNK)
            lanes = pl.ds(pl.multiple_of(i * (CHUNK * 128), CHUNK * 128), CHUNK * 128)
            row = hrow[rows, :]
            f = fel[rows, :]
            f_top = f.astype(BF16).astype(F32)
            f_low = f - f_top
            left_side = jnp.concatenate(
                [
                    spread(
                        [
                            [x[g : g + 1, 0:128], x[g : g + 1, 128:256]]
                            for x in (f_top, f_low)
                        ],
                        row[g : g + 1, :],
                    )
                    for g in range(CHUNK)
                ],
                axis=1,
            )
            acc[...] += nt(left_side, onehot[:, lanes])

        partial = acc[0:128, :] + acc[128:256, :]
        pel_send[s] = partial
        if s == 0:
            send(pel_send.at[s], pel_recv.at[s], base + 4, base + 4, (d, o), None)
        else:
            cut = pl.ds(o * 64, 64)
            send(
                pel_send.at[s, cut],
                pel_recv.at[s, cut],
                base + 4,
                base + 4,
                (d, o),
                None,
            )
        top, low = split2(partial)
        product = jnp.dot(
            jnp.concatenate([top, low], axis=0),
            onehot[:, 8448:8704],
            preferred_element_type=F32,
        )
        border = []
        for side in range(2):
            found = masked_rows(
                product[:, side * 128 : (side + 1) * 128],
                hrow[66 + side : 67 + side, :],
            )
            border.append(jnp.concatenate(found, axis=0))

        if s == 0:
            for j in range(1, 9):
                arrived(pdx.at[pl.ds(sources[j], 2)], 3 + j, there[j])
            for j in range(5):
                arrived(lists_sent.at[sources_lists[j]], 12 + j, there[j])
            scalars = pltpu.make_async_copy(lists_sent, lists, lsem.at[21])
            scalars.start()
            scalars.wait()
            keep_bonds()

        for at, (frm, cond) in enumerate(
            ((4, has_left), (12, has_right), (0, has_left2), (16, has_right2))
        ):
            arrived(ub.at[pl.ds(frm, 4)], base + at, cond)
        place[...] = pdx[:, 0:2, :] + ub[...]

        @pl.loop(0, 3)
        def _(i):
            for j in range(2):
                p = 2 * i + j
                t = p // 3
                f = family[t, p - 3 * t]
                me = place[f + 4]
                total = [jnp.zeros((8, 128), F32)] * 2
                for k in range(3):
                    far_t = columns(named_far(f, k))
                    for q in range(0, 128, 32):
                        *_, rest, stretch, influence = stretched(
                            far_bonds, 3 * p + k, slice(q, q + 32), far_t, me
                        )
                        weighted = influence * rest
                        total[0] = total[0] + folded(weighted * stretch)
                        total[1] = total[1] + folded(weighted * rest)
                far_state[p] = state_of(total)

        totals = [[jnp.zeros((8, 128), F32)] * 2 for _ in range(2)]
        for p in range(6):
            t = p // 3
            far_t = columns(named(p) + 4)
            me = place[own + t]
            for q in range(0, 128, 32):
                rows = slice(q, q + 32)
                yx, yy, inverse, rest, stretch, influence = stretched(
                    bonds, p, rows, far_t, me
                )
                bonds[NX, p, rows] = yx * inverse
                bonds[NY, p, rows] = yy * inverse
                bonds[STR, p, rows] = stretch
                bonds[INFL, p, rows] = influence
                weighted = influence * rest
                totals[t][0] = totals[t][0] + folded(weighted * stretch)
                totals[t][1] = totals[t][1] + folded(weighted * rest)
        states_own = [state_of(x) for x in totals]

        def coefficients(k, state):
            theta, volume = state[0:1, :], state[1:2, :]
            return 2.0 * k * theta / volume, 4.0 * k / volume, 0.5 * theta

        totals = [[jnp.zeros((8, 128), F32)] * 2 for _ in range(2)]
        near = [coefficients(pdx[own + t][2:3, :], states_own[t]) for t in range(2)]
        for p in range(6):
            t = p // 3
            far = coefficients(pdx[named(p) + 4][2:3, :], far_state[p])
            far_t = jnp.concatenate(far + (jnp.zeros((5, 128), F32),), axis=0).T
            oa, ob, oc = near[t]
            for q in range(0, 128, 32):
                rows = slice(q, q + 32)
                rest = bonds[REST, p, rows]
                stretch = bonds[STR, p, rows]
                mine = oa * rest + ob * (stretch - oc * rest)
                away = far_t[rows, 0:1] * rest + far_t[rows, 1:2] * (
                    stretch - far_t[rows, 2:3] * rest
                )
                force = bonds[INFL, p, rows] * (mine + away)
                totals[t][0] = totals[t][0] + folded(force * bonds[NX, p, rows])
                totals[t][1] = totals[t][1] + folded(force * bonds[NY, p, rows])

        forces, moved = [], []
        for t in range(2):
            alive = jnp.full((2, 128), 2 * b + t, I32) < live[0]
            total = [jnp.sum(x, axis=0, keepdims=True) for x in totals[t]]
            force = jnp.where(alive, jnp.concatenate(total, axis=0), 0.0)
            forces.append(force)
            v = jnp.where(alive, cur[t] + step[t : t + 1, :] * force, 0.0)
            u = jnp.where(alive, ub[own + t] + TIME_STEP * v, 0.0)
            cur[t] = v
            moved.append(u)

        reaction = []
        for q in range(2):
            w = jnp.zeros((2, 128), F32)
            for t in range(2):
                hit = jnp.full((2, 128), ptile[q], I32) == 2 * b + t
                w = w + jnp.where(hit, pblend[q : q + 1, :] * forces[t], 0.0)
            w = jnp.concatenate([w, jnp.zeros((6, 128), F32)], axis=0)
            reaction.append(
                jnp.dot(w, pm[q], precision=EXACT, preferred_element_type=F32)[0:2, :]
            )
        late = jnp.concatenate(reaction + moved, axis=0)
        late_send[s] = late
        send(late_send.at[s], late_recv.at[s], base + 5, base + 5, (d, o), None)
        wide = jnp.concatenate(reaction, axis=1)
        top, low = split2(wide)
        met = jnp.dot(
            jnp.concatenate([top, low, jnp.zeros((12, 256), BF16)], axis=0),
            link[...],
            preferred_element_type=F32,
        )
        met = met[0:2, :] + met[2:4, :]
        for side in range(2):
            bd_send[s, side] = met[:, side * 128 : (side + 1) * 128] - border[side]
        for j in range(4):
            side = j // 2
            send(
                bd_send.at[s, side],
                bd_recv.at[s, 2 * (1 - side) + b],
                base + 6 + j,
                base + 6 + 2 * (1 - side) + b,
                peers[1 + j],
                there[1 + j],
            )
        if s == 0:
            for t in range(2):
                ub1[own + t] = moved[t]
        else:
            for t in range(2):
                disp_out[t] = moved[t]
                vel_out[t] = cur[t]

        halves = range(2) if s == 0 else (b,)
        if s == 0:
            arrived(speed.at[o], 2, None)
            arrived(pel_recv.at[s], base + 4, None)
            for copy in states:
                copy.wait_send()
        else:
            arrived(pel_recv.at[s, pl.ds(b * 64, 64)], base + 4, None)
        for h in halves:
            for c in range(2):
                cut = pl.ds(h * 64 + c * 32, 32)
                rows = slice(c * 32, c * 32 + 32)
                speed[h, rows, :] = speed[h, rows, :] - speed[h, 64:96, :] * (
                    pel_send[s, cut, :] + pel_recv[s, cut, :]
                )
        arrived(late_recv.at[s], base + 5, None)
        other = late_recv[s]
        if s == 0:
            for t in range(2):
                ub1[theirs + t] = other[4 + 2 * t : 6 + 2 * t, :]
        for j in range(4):
            arrived(bd_recv.at[s, j], base + 6 + j, there[1 + j])
        shared = [
            jnp.where(
                jnp.full((2, 128), d, I32) > 0, bd_recv[s, 0] + bd_recv[s, 1], 0.0
            ),
            jnp.where(
                jnp.full((2, 128), d, I32) < n_dom - 1,
                bd_recv[s, 2] + bd_recv[s, 3],
                0.0,
            ),
        ]
        sides = []
        for g, x in enumerate(
            [late[0:2, :] + other[0:2, :], late[2:4, :] + other[2:4, :]] + shared
        ):
            x_top = x.astype(BF16).astype(F32)
            x_low = x - x_top
            sides.append(
                spread(
                    [[y[0:1, :], y[1:2, :]] for y in (x_top, x_low)],
                    hrow[64 + g : 65 + g, :],
                )
            )
        extra = nt(jnp.concatenate(sides, axis=1), onehot[:, 8192:8704])
        acc[0:128, :] = extra[0:128, :] + extra[128:256, :]
        for h in halves:
            for c in range(2):
                cut = pl.ds(h * 64 + c * 32, 32)
                rows = slice(c * 32, c * 32 + 32)
                v = speed[h, rows, :] + speed[h, 64:96, :] * acc[cut, :]
                speed[h, rows, :] = v
                table[h, rows, :] = table[h, rows, :] + TIME_STEP * v

    for r in range(HALF_ROWS):
        lanes = slice(r * LO, (r + 1) * LO)
        for c in range(2):
            at = PAD_ROWS * c + r
            fdisp_out[c : c + 1, lanes] = table[b, at : at + 1, :]
            fvel_out[c : c + 1, lanes] = speed[b, at : at + 1, :]
    for copy, cond in started:
        if_there(cond, copy.wait_send)


def hand_over(*refs):
    ins, outs, sems = refs[:4], refs[4:8], refs[8]
    copies = [
        pltpu.make_async_copy(src, dst, sems.at[at])
        for at, (src, dst) in enumerate(zip(ins, outs))
    ]
    for copy in copies:
        copy.start()
    for copy in copies:
        copy.wait()


def shards(n_dom, *args):
    (
        pd_disp,
        pd_vel,
        pd_coord,
        pd_modulus,
        pd_step,
        family,
        live,
        patch_tile,
        patch_blend,
        patch_nodes,
        patch_matrix,
        fe_disp,
        fe_vel,
        fe_step,
        fe_modulus,
        element_nodes,
        shape_grad,
        quad_weight,
        shared_left,
        shared_right,
    ) = args
    vmem = pl.BlockSpec(memory_space=pltpu.VMEM)
    hbm = pl.BlockSpec(memory_space=pltpu.HBM)
    rows = fe_step.shape[0] // 128

    def f32(*shape):
        return pltpu.VMEM(shape, F32)

    results = pl.pallas_call(
        functools.partial(kernel, n_dom),
        out_shape=[
            pltpu.VMEM(pd_disp.shape, F32),
            pltpu.VMEM(pd_vel.shape, F32),
            pltpu.VMEM(fe_disp.shape, F32),
            pltpu.VMEM(fe_vel.shape, F32),
        ],
        in_specs=[hbm] * 20,
        out_specs=[vmem] * 4,
        scratch_shapes=[
            f32(2, 2, 128),
            f32(2, 2, 128),
            f32(2, 2, 128),
            f32(2, 128),
            f32(2, 128),
            pltpu.SMEM((2, 3), I32),
            pltpu.SMEM((1,), I32),
            pltpu.SMEM((2,), I32),
            f32(2, 128),
            pltpu.VMEM((1, 128), I32),
            f32(*fe_disp.shape),
            f32(*fe_vel.shape),
            f32(rows, 128),
            f32(1, 128),
            pltpu.VMEM((64, 128), I32),
            f32(128, 64),
            f32(1, 64),
            pltpu.VMEM((1, 113), I32),
            pltpu.VMEM((1, 113), I32),
            f32(20, 8, 128),
            f32(20, 2, 128),
            f32(20, 2, 128),
            f32(20, 2, 128),
            pltpu.VMEM((2, 3), I32),
            pltpu.VMEM((6, 8, 128), I32),
            pltpu.SMEM((6, 8, 128), I32),
            f32(2, 128, 128),
            f32(2, 64, LO),
            f32(2, 96, LO),
            pltpu.VMEM((256, LO), BF16),
            pltpu.VMEM((LO, 8704), BF16),
            pltpu.VMEM((72, 128), I32),
            pltpu.VMEM((8, 128), I32),
            pltpu.VMEM((256, 256), BF16),
            f32(64, 256),
            f32(64, 256),
            f32(64, 128),
            f32(256, LO),
            f32(6, 6, 128, 128),
            f32(2, 18, 128, 128),
            f32(6, 2, 128),
            f32(2, 2, 128),
            f32(2, 128, LO),
            f32(2, 128, LO),
            f32(2, 8, 128),
            f32(2, 8, 128),
            f32(2, 2, 2, 128),
            f32(2, 4, 2, 128),
            pltpu.SemaphoreType.DMA((N_COPIES,)),
            pltpu.SemaphoreType.DMA((N_COPIES,)),
            pltpu.SemaphoreType.DMA((22,)),
        ],
        compiler_params=pltpu.CompilerParams(
            collective_id=0, has_side_effects=True, vmem_limit_bytes=VMEM_BYTES
        ),
    )(
        pd_disp,
        pd_vel,
        pd_coord,
        pd_modulus,
        pd_step,
        family,
        live,
        patch_tile,
        patch_blend,
        patch_nodes,
        patch_matrix,
        fe_disp,
        fe_vel,
        fe_step.reshape(-1, 128),
        fe_modulus.reshape(1, -1),
        element_nodes,
        shape_grad.reshape(-1, shape_grad.shape[2]),
        quad_weight.reshape(1, -1),
        shared_left,
        shared_right,
    )
    return pl.pallas_call(
        hand_over,
        out_shape=[jax.ShapeDtypeStruct(x.shape, F32) for x in results],
        in_specs=[vmem] * 4,
        out_specs=[hbm] * 4,
        scratch_shapes=[pltpu.SemaphoreType.DMA((4,))],
        compiler_params=pltpu.CompilerParams(vmem_limit_bytes=2**20),
    )(*results)


def solution(mesh):
    both = ("dom", "blk")
    return jax.shard_map(
        functools.partial(shards, mesh.shape["dom"]),
        mesh=mesh,
        in_specs=(
            P(both, None, None),
            P(both, None, None),
            P(both, None, None),
            P(both, None),
            P(both, None),
            P(both, None),
            P("dom"),
            P("dom"),
            P("dom", None),
            P(both, None),
            P(both, None, None),
            P(None, both),
            P(None, both),
            P(both),
            P(both),
            P(None, both),
            P(),
            P(),
            P("dom", None),
            P("dom", None),
        ),
        out_specs=(
            P(both, None, None),
            P(both, None, None),
            P(None, both),
            P(None, both),
        ),
        check_vma=False,
    )
```

```python
import functools

import jax
import jax.numpy as jnp
from jax import lax
from jax.experimental import pallas as pl
from jax.experimental.pallas import tpu as pltpu
from jax.sharding import PartitionSpec as P

MESH = pl.DeviceIdType.MESH
F32 = jnp.float32
BF16 = jnp.bfloat16
I32 = jnp.int32
EXACT = lax.Precision.HIGHEST

TIME_STEP = 0.5
CORE_SQ = 0.01
STRETCH = 0.3

LO = 256
HALF_ROWS = 25
PAD_ROWS = 32
CHUNK = 8
N_COPIES = 37
VMEM_BYTES = 60 * 2**20


def split2(x):
    top = x.astype(BF16)
    return top, (x - top.astype(F32)).astype(BF16)


def folded(x):
    return jnp.sum(x.reshape(-1, 8, x.shape[1]), axis=0)


def inverted(x):
    y = pl.reciprocal(x, approx=True)
    return y * (2.0 - x * y)


def two_parts(x):
    top, low = split2(x)
    return jnp.concatenate([top, low, jnp.zeros((12, x.shape[1]), BF16)], axis=0)


def nt(a, b, **kw):
    return lax.dot_general(
        a, b, (((1,), (1,)), ((), ())), preferred_element_type=F32, **kw
    )


def kernel(
    n_dom,
    disp_in,
    vel_in,
    coord_in,
    modulus_in,
    step_in,
    family_in,
    live_in,
    ptile_in,
    pblend_in,
    pnodes_in,
    pmat_in,
    fdisp_in,
    fvel_in,
    fstep_in,
    fmod_in,
    enodes_in,
    sgrad_in,
    qweight_in,
    sleft_in,
    sright_in,
    disp_out,
    vel_out,
    fdisp_out,
    fvel_out,
    disp,
    vel,
    coord,
    modulus,
    step,
    family,
    live,
    ptile,
    pblend,
    pnodes,
    fdisp,
    fvel,
    fstep,
    fmod,
    enodes,
    sgrad,
    qweight,
    sleft,
    sright,
    pdx,
    ub0,
    ub1,
    place,
    lists_in,
    lists_sent,
    lists,
    pm,
    split_pm,
    table,
    speed,
    split_table,
    onehot,
    hrow,
    ids,
    link,
    del_,
    fel,
    sgt,
    acc,
    bonds,
    far_bonds,
    far_state,
    cur,
    pel_send,
    pel_recv,
    late_send,
    late_recv,
    bd_send,
    bd_recv,
    ssem,
    rsem,
    lsem,
):
    d = lax.axis_index("dom")
    b = lax.axis_index("blk")
    o = 1 - b
    has_left = d > 0
    has_right = d < n_dom - 1
    has_left2 = d > 1
    has_right2 = d < n_dom - 2
    left = jnp.maximum(d - 1, 0)
    right = jnp.minimum(d + 1, n_dom - 1)
    left2 = jnp.maximum(d - 2, 0)
    right2 = jnp.minimum(d + 2, n_dom - 1)
    peers = ((d, o),) + tuple(
        (x, j) for x in (left, right, left2, right2) for j in range(2)
    )
    there = (None,) + tuple(
        x for x in (has_left, has_right, has_left2, has_right2) for j in range(2)
    )

    def if_there(cond, act):
        if cond is None:
            act()
        else:
            pl.when(cond)(act)

    barrier = pltpu.get_barrier_semaphore()
    for peer, cond in zip(peers, there):
        if_there(
            cond,
            functools.partial(
                pl.semaphore_signal,
                barrier,
                inc=1,
                device_id=peer,
                device_id_type=MESH,
            ),
        )

    loads = {}
    for at, (src, dst) in enumerate(
        (
            (fdisp_in, fdisp),
            (coord_in, coord),
            (modulus_in, modulus),
            (disp_in, disp),
            (pnodes_in, pnodes),
            (pmat_in.at[0], pm.at[b]),
            (fvel_in, fvel),
            (fstep_in, fstep),
            (enodes_in, enodes),
            (vel_in, vel),
            (step_in, step),
            (family_in, family),
            (family_in, lists_in),
            (live_in, live),
            (ptile_in, ptile),
            (pblend_in, pblend),
            (fmod_in, fmod),
            (sgrad_in, sgrad),
            (qweight_in, qweight),
            (sleft_in, sleft),
            (sright_in, sright),
        )
    ):
        loads[at] = pltpu.make_async_copy(src, dst, lsem.at[at])
        loads[at].start()

    def loaded(*which):
        for at in which:
            loads[at].wait()

    started = []

    def send(src, dst, ssem_at, rsem_at, peer, cond):
        copy = pltpu.make_async_remote_copy(
            src_ref=src,
            dst_ref=dst,
            send_sem=ssem.at[ssem_at],
            recv_sem=rsem.at[rsem_at],
            device_id=peer,
            device_id_type=MESH,
        )
        if_there(cond, copy.start)
        started.append((copy, cond))

    def arrived(dst, rsem_at, cond):
        copy = pltpu.make_async_remote_copy(
            src_ref=dst,
            dst_ref=dst,
            send_sem=ssem.at[0],
            recv_sem=rsem.at[rsem_at],
            device_id=(d, o),
            device_id_type=MESH,
        )
        if_there(cond, copy.wait_recv)

    own = 8 + 2 * b
    theirs = 8 + 2 * o

    loaded(1, 2, 3, 4)
    for t in range(2):
        pdx[own + t] = jnp.concatenate(
            [
                coord[t],
                modulus[t : t + 1, :],
                disp[t],
                pnodes[...].astype(F32),
                jnp.zeros((2, 128), F32),
            ],
            axis=0,
        )
    loaded(0)
    table[b, 24:32, :] = jnp.zeros((8, LO), F32)
    table[b, 56:64, :] = jnp.zeros((8, LO), F32)
    for r in range(HALF_ROWS):
        for c in range(2):
            at = PAD_ROWS * c + r
            table[b, at : at + 1, :] = fdisp[c : c + 1, r * LO : (r + 1) * LO]
    loaded(6, 7)
    speed[b, 24:32, :] = jnp.zeros((8, LO), F32)
    speed[b, 56:64, :] = jnp.zeros((8, LO), F32)
    speed[b, 88:96, :] = jnp.zeros((8, LO), F32)
    for r in range(HALF_ROWS):
        for c in range(2):
            at = PAD_ROWS * c + r
            speed[b, at : at + 1, :] = fvel[c : c + 1, r * LO : (r + 1) * LO]
    for p in range(2):
        lanes = slice(p * 128, (p + 1) * 128)
        speed[b, 2 * PAD_ROWS : 2 * PAD_ROWS + HALF_ROWS, lanes] = fstep[
            pl.ds(p, HALF_ROWS, stride=2), :
        ]
    loaded(*range(8, 21))

    lo_iota = lax.broadcasted_iota(I32, (LO, 128), 0)

    def table_row(node):
        hi = lax.shift_right_arithmetic(node, 8)
        return jnp.where(hi >= HALF_ROWS, hi + (PAD_ROWS - HALF_ROWS), hi)

    def onehot_of(lo_row):
        return jnp.where(
            lo_iota == jnp.broadcast_to(lo_row, (LO, 128)), 1.0, 0.0
        ).astype(BF16)

    @pl.loop(0, 64 // CHUNK, unroll=2)
    def _(i):
        node = enodes[pl.ds(pl.multiple_of(i * CHUNK, CHUNK), CHUNK), :]
        hrow[pl.ds(pl.multiple_of(i * CHUNK, CHUNK), CHUNK), :] = table_row(node)
        lo = lax.bitwise_and(node, LO - 1)
        base = pl.multiple_of(i * (CHUNK * 128), CHUNK * 128)
        for g in range(CHUNK):
            onehot[:, pl.ds(base + g * 128, 128)] = onehot_of(lo[g : g + 1, :])

    sgt[...] = sgrad[...].T
    eye = lax.broadcasted_iota(I32, (64, 64), 0) == lax.broadcasted_iota(
        I32, (64, 64), 1
    )
    weight = jnp.sum(
        jnp.where(eye, jnp.broadcast_to(qweight[...], (64, 64)), 0.0),
        axis=1,
        keepdims=True,
    )
    scale = weight * fmod[...]


    lists_sent[2 + b] = jnp.zeros((8, 128), I32)
    lists_sent[2 + b, 0:2, 0:3] = lists_in[...]

    @pl.when(jnp.logical_not(has_left))
    def _():
        lists_sent[0:2] = jnp.zeros((2, 8, 128), I32)

    @pl.when(jnp.logical_not(has_right))
    def _():
        lists_sent[4:6] = jnp.zeros((2, 8, 128), I32)

    ids[...] = jnp.full((8, 128), -1, I32)
    ids[pl.ds(b, 1), :] = pnodes[...]
    ids[2:3, 0:113] = sleft[...]
    ids[3:4, 0:113] = sright[...]
    few_lo = lax.bitwise_and(ids[...], LO - 1)
    for g in (2, 3):
        onehot[:, 8192 + g * 128 : 8320 + g * 128] = onehot_of(few_lo[g : g + 1, :])

    pl.semaphore_wait(
        barrier, 1 + 2 * sum(x.astype(I32) for x in (has_left, has_right, has_left2, has_right2))
    )

    send(table.at[b], table.at[b], 0, 0, (d, o), None)
    slots = (own,) + tuple(x + 2 * b for x in (12, 12, 4, 4, 16, 16, 0, 0))
    marks = (0,) + tuple(x + b for x in (3, 3, 1, 1, 7, 7, 5, 5))
    homes = (2 + b,) + tuple(x + b for x in (4, 4, 0, 0))
    loaded(5)
    send(pm.at[b], pm.at[b], 1, 1, (d, o), None)
    for j in range(9):
        send(
            pdx.at[pl.ds(own, 2)],
            pdx.at[pl.ds(slots[j], 2)],
            3 + j,
            3 + marks[j],
            peers[j],
            there[j],
        )
    sources = (theirs, 4, 6, 12, 14, 0, 2, 16, 18)
    sources_lists = (2 + o, 0, 1, 4, 5)
    send(speed.at[b], speed.at[b], 2, 2, (d, o), None)
    states = (started[0][0], started.pop()[0])
    del started[0]
    for j in range(5):
        send(
            lists_sent.at[2 + b],
            lists_sent.at[homes[j]],
            12 + j,
            12 + marks[j],
            peers[j],
            there[j],
        )

    arrived(pdx.at[pl.ds(theirs, 2)], 3, None)
    ids[pl.ds(o, 1), :] = pdx[theirs, 5:6, :].astype(I32)
    few = ids[...]
    hrow[64:72, :] = table_row(few)
    few_lo = lax.bitwise_and(few, LO - 1)
    for g in range(2):
        onehot[:, 8192 + g * 128 : 8320 + g * 128] = onehot_of(few_lo[g : g + 1, :])

    REST, INFL0, NX, NY, STR, INFL = range(6)
    cur[...] = vel[...]

    def keep_pair(into, p, far, me):
        far_t = pdx[far].T
        for q in range(0, 128, 32):
            rows = slice(q, q + 32)
            ox = far_t[rows, 0:1] - me[0:1, :]
            oy = far_t[rows, 1:2] - me[1:2, :]
            r2 = ox * ox + oy * oy
            into[REST, p, rows] = jnp.sqrt(r2 + CORE_SQ)
            into[INFL0, p, rows] = jnp.exp(-0.5 * r2)

    def named(p):
        return family[p // 3, p % 3]

    def named_far(f, k):
        listed = lists[lax.shift_right_arithmetic(f, 1), lax.bitwise_and(f, 1), k]
        return listed + lax.shift_left(lax.shift_right_arithmetic(f, 2), 2)

    def keep_bonds():
        for p in range(6):
            keep_pair(bonds, p, named(p) + 4, pdx[own + p // 3])

        @pl.loop(0, 6, unroll=2)
        def _(p):
            t = p // 3
            f = family[t, p - 3 * t]
            me = pdx[f + 4]
            for k in range(3):
                keep_pair(far_bonds, 3 * p + k, named_far(f, k), me)

    def stretched(kept, p, rows, far_t, me):
        yx = far_t[rows, 0:1] - me[0:1, :]
        yy = far_t[rows, 1:2] - me[1:2, :]
        y2 = yx * yx + yy * yy + CORE_SQ
        inverse = lax.rsqrt(y2)
        rest = kept[REST, p, rows]
        stretch = y2 * inverse - rest
        ratio = stretch * (1.0 / STRETCH)
        influence = kept[INFL0, p, rows] * inverted(1.0 + ratio * ratio)
        return yx, yy, inverse, rest, stretch, influence

    def columns(far):
        return jnp.concatenate([place[far], jnp.zeros((6, 128), F32)], axis=0).T

    def state_of(total):
        dilated, volume = [jnp.sum(x, axis=0, keepdims=True) for x in total]
        return jnp.concatenate([2.0 * dilated / volume, volume], axis=0)

    row_iota = lax.broadcasted_iota(I32, (64, 128), 0)

    def masked_rows(product, row):
        both = product[0:128] + product[128:256]
        hit = row_iota == jnp.broadcast_to(row, (64, 128))
        out = []
        for c in range(2):
            x = jnp.where(hit[0:32], both[c * 32 : c * 32 + 32], 0.0)
            x = x + jnp.where(hit[32:64], both[64 + c * 32 : 96 + c * 32], 0.0)
            out.append(jnp.sum(x, axis=0, keepdims=True))
        return out

    def spread(values, row):
        hit = row_iota == jnp.broadcast_to(row, (64, 128))
        blocks = []
        for part in range(2):
            wide = [
                jnp.where(hit, jnp.broadcast_to(values[part][c], (64, 128)), 0.0)
                for c in range(2)
            ]
            for half in range(2):
                for c in range(2):
                    blocks.append(wide[c][half * 32 : half * 32 + 32])
        return jnp.concatenate(blocks, axis=0).astype(BF16)

    def blend(s, picked):
        ub = (ub0, ub1)[s]
        base = 17 + 10 * s
        targets = []
        for q in range(2):
            x = nt(two_parts(picked[q]), split_pm[q])
            targets.append(x[0:2, 0:128] + x[2:4, 0:128] + x[0:2, 128:256])
        for k in range(4):
            u = pdx[8 + k, 3:5, :] if s == 0 else ub[8 + k]
            new = u
            for q in range(2):
                hit = jnp.full((2, 128), ptile[q], I32) == k
                new = jnp.where(hit, u + pblend[q : q + 1, :] * (targets[q] - u), new)
            ub[8 + k] = new
        mine = ub.at[pl.ds(8, 4)]
        for j, (to, at, peer, cond) in enumerate(
            (
                (16, 3, left2, has_left2),
                (0, 2, right2, has_right2),
                (12, 1, left, has_left),
                (4, 0, right, has_right),
            )
        ):
            send(mine, ub.at[pl.ds(to, 4)], base + j, base + at, (peer, b), cond)

    for s in range(2):
        ub = (ub0, ub1)[s]
        base = 17 + 10 * s
        if s == 0:
            arrived(table.at[o], 0, None)
            arrived(pm.at[o], 1, None)
            for q in range(2):
                top, low = split2(pm[q])
                split_pm[q, 0:128] = top
                split_pm[q, 128:256] = low

        top, low = split2(table[...].reshape(128, LO))
        split_table[0:128, :] = top
        split_table[128:256, :] = low
        if s == 0:
            product = jnp.dot(
                split_table[...], onehot[:, 8192:8448], preferred_element_type=F32
            )
            blend(
                0,
                [
                    jnp.concatenate(
                        masked_rows(
                            product[:, q * 128 : (q + 1) * 128], hrow[64 + q : 65 + q, :]
                        ),
                        axis=0,
                    )
                    for q in range(2)
                ],
            )

        @pl.loop(0, 64 // CHUNK, unroll=2)
        def _(i):
            rows = pl.ds(pl.multiple_of(i * CHUNK, CHUNK), CHUNK)
            lanes = pl.ds(pl.multiple_of(i * (CHUNK * 128), CHUNK * 128), CHUNK * 128)
            product = jnp.dot(
                split_table[...], onehot[:, lanes], preferred_element_type=F32
            )
            row = hrow[rows, :]
            found = [
                masked_rows(product[:, g * 128 : (g + 1) * 128], row[g : g + 1, :])
                for g in range(CHUNK)
            ]
            for c in range(2):
                del_[rows, c * 128 : (c + 1) * 128] = jnp.concatenate(
                    [f[c] for f in found], axis=0
                )

        if s == 0:
            few_f = ids[...].astype(F32)
            few_t = few_f.T
            for q in range(2):
                for side in range(2):
                    link[
                        q * 128 : (q + 1) * 128, side * 128 : (side + 1) * 128
                    ] = jnp.where(
                        few_t[:, q : q + 1] == few_f[2 + side : 3 + side, :], 1.0, 0.0
                    ).astype(BF16)

        grad = jnp.dot(sgrad[...], del_[...], precision=EXACT, preferred_element_type=F32)
        exx = grad[0:64, 0:128]
        eyy = grad[64:128, 128:256]
        exy = 0.5 * (grad[64:128, 0:128] + grad[0:64, 128:256])
        scaled = scale * (1.0 + exx * exx + eyy * eyy + 2.0 * exy * exy)
        both = exx + eyy
        sxx = scaled * (both + 2.0 * exx)
        syy = scaled * (both + 2.0 * eyy)
        sxy = scaled * 2.0 * exy
        stress = jnp.concatenate(
            [
                jnp.concatenate([sxx, sxy], axis=1),
                jnp.concatenate([sxy, syy], axis=1),
            ],
            axis=0,
        )
        fel[...] = jnp.dot(sgt[...], stress, precision=EXACT, preferred_element_type=F32)
        acc[...] = jnp.zeros((256, LO), F32)

        @pl.loop(0, 64 // CHUNK, unroll=2)
        def _(i):
            rows = pl.ds(pl.multiple_of(i * CHUNK, CHUNK), CHUNK)
            lanes = pl.ds(pl.multiple_of(i * (CHUNK * 128), CHUNK * 128), CHUNK * 128)
            row = hrow[rows, :]
            f = fel[rows, :]
            f_top = f.astype(BF16).astype(F32)
            f_low = f - f_top
            left_side = jnp.concatenate(
                [
                    spread(
                        [
                            [x[g : g + 1, 0:128], x[g : g + 1, 128:256]]
                            for x in (f_top, f_low)
                        ],
                        row[g : g + 1, :],
                    )
                    for g in range(CHUNK)
                ],
                axis=1,
            )
            acc[...] += nt(left_side, onehot[:, lanes])

        partial = acc[0:128, :] + acc[128:256, :]
        pel_send[s] = partial
        if s == 0:
            send(pel_send.at[s], pel_recv.at[s], base + 4, base + 4, (d, o), None)
        else:
            cut = pl.ds(o * 64, 64)
            send(
                pel_send.at[s, cut],
                pel_recv.at[s, cut],
                base + 4,
                base + 4,
                (d, o),
                None,
            )
        top, low = split2(partial)
        product = jnp.dot(
            jnp.concatenate([top, low], axis=0),
            onehot[:, 8448:8704],
            preferred_element_type=F32,
        )
        border = []
        for side in range(2):
            found = masked_rows(
                product[:, side * 128 : (side + 1) * 128],
                hrow[66 + side : 67 + side, :],
            )
            border.append(jnp.concatenate(found, axis=0))

        if s == 0:
            for j in range(1, 9):
                arrived(pdx.at[pl.ds(sources[j], 2)], 3 + j, there[j])
            for j in range(5):
                arrived(lists_sent.at[sources_lists[j]], 12 + j, there[j])
            scalars = pltpu.make_async_copy(lists_sent, lists, lsem.at[21])
            scalars.start()
            scalars.wait()
            keep_bonds()

        arrived(ub.at[pl.ds(4, 4)], base, has_left)
        arrived(ub.at[pl.ds(12, 4)], base + 1, has_right)
        place[4:16] = pdx[4:16, 0:2, :] + ub[4:16]

        totals = [[jnp.zeros((8, 128), F32)] * 2 for _ in range(2)]
        for p in range(6):
            t = p // 3
            far_t = columns(named(p) + 4)
            me = place[own + t]
            for q in range(0, 128, 32):
                rows = slice(q, q + 32)
                yx, yy, inverse, rest, stretch, influence = stretched(
                    bonds, p, rows, far_t, me
                )
                bonds[NX, p, rows] = yx * inverse
                bonds[NY, p, rows] = yy * inverse
                bonds[STR, p, rows] = stretch
                bonds[INFL, p, rows] = influence
                weighted = influence * rest
                totals[t][0] = totals[t][0] + folded(weighted * stretch)
                totals[t][1] = totals[t][1] + folded(weighted * rest)
        states_own = [state_of(x) for x in totals]
        arrived(ub.at[pl.ds(0, 4)], base + 2, has_left2)
        arrived(ub.at[pl.ds(16, 4)], base + 3, has_right2)
        place[0:4] = pdx[0:4, 0:2, :] + ub[0:4]
        place[16:20] = pdx[16:20, 0:2, :] + ub[16:20]

        @pl.loop(0, 3)
        def _(i):
            for j in range(2):
                p = 2 * i + j
                t = p // 3
                f = family[t, p - 3 * t]
                me = place[f + 4]
                total = [jnp.zeros((8, 128), F32)] * 2
                for k in range(3):
                    far_t = columns(named_far(f, k))
                    for q in range(0, 128, 32):
                        *_, rest, stretch, influence = stretched(
                            far_bonds, 3 * p + k, slice(q, q + 32), far_t, me
                        )
                        weighted = influence * rest
                        total[0] = total[0] + folded(weighted * stretch)
                        total[1] = total[1] + folded(weighted * rest)
                far_state[p] = state_of(total)

        def coefficients(k, state):
            theta, volume = state[0:1, :], state[1:2, :]
            return 2.0 * k * theta / volume, 4.0 * k / volume, 0.5 * theta

        totals = [[jnp.zeros((8, 128), F32)] * 2 for _ in range(2)]
        near = [coefficients(pdx[own + t][2:3, :], states_own[t]) for t in range(2)]
        for p in range(6):
            t = p // 3
            far = coefficients(pdx[named(p) + 4][2:3, :], far_state[p])
            far_t = jnp.concatenate(far + (jnp.zeros((5, 128), F32),), axis=0).T
            oa, ob, oc = near[t]
            for q in range(0, 128, 32):
                rows = slice(q, q + 32)
                rest = bonds[REST, p, rows]
                stretch = bonds[STR, p, rows]
                mine = oa * rest + ob * (stretch - oc * rest)
                away = far_t[rows, 0:1] * rest + far_t[rows, 1:2] * (
                    stretch - far_t[rows, 2:3] * rest
                )
                force = bonds[INFL, p, rows] * (mine + away)
                totals[t][0] = totals[t][0] + folded(force * bonds[NX, p, rows])
                totals[t][1] = totals[t][1] + folded(force * bonds[NY, p, rows])

        forces, moved = [], []
        for t in range(2):
            alive = jnp.full((2, 128), 2 * b + t, I32) < live[0]
            total = [jnp.sum(x, axis=0, keepdims=True) for x in totals[t]]
            force = jnp.where(alive, jnp.concatenate(total, axis=0), 0.0)
            forces.append(force)
            v = jnp.where(alive, cur[t] + step[t : t + 1, :] * force, 0.0)
            u = jnp.where(alive, ub[own + t] + TIME_STEP * v, 0.0)
            cur[t] = v
            moved.append(u)

        reaction = []
        for q in range(2):
            w = jnp.zeros((2, 128), F32)
            for t in range(2):
                hit = jnp.full((2, 128), ptile[q], I32) == 2 * b + t
                w = w + jnp.where(hit, pblend[q : q + 1, :] * forces[t], 0.0)
            w = two_parts(w)
            x = jnp.dot(w, split_pm[q, 0:128], preferred_element_type=F32)
            y = jnp.dot(w, split_pm[q, 128:256], preferred_element_type=F32)
            reaction.append(x[0:2, :] + x[2:4, :] + y[0:2, :])
        late = jnp.concatenate(reaction + moved, axis=0)
        late_send[s] = late
        send(late_send.at[s], late_recv.at[s], base + 5, base + 5, (d, o), None)
        wide = jnp.concatenate(reaction, axis=1)
        met = jnp.dot(two_parts(wide), link[...], preferred_element_type=F32)
        met = met[0:2, :] + met[2:4, :]
        for side in range(2):
            bd_send[s, side] = met[:, side * 128 : (side + 1) * 128] - border[side]
        for j in range(4):
            side = j // 2
            send(
                bd_send.at[s, side],
                bd_recv.at[s, 2 * (1 - side) + b],
                base + 6 + j,
                base + 6 + 2 * (1 - side) + b,
                peers[1 + j],
                there[1 + j],
            )
        if s == 0:
            for t in range(2):
                ub1[own + t] = moved[t]
        else:
            for t in range(2):
                disp_out[t] = moved[t]
                vel_out[t] = cur[t]

        halves = range(2) if s == 0 else (b,)
        if s == 0:
            arrived(speed.at[o], 2, None)
            arrived(pel_recv.at[s], base + 4, None)
            for copy in states:
                copy.wait_send()
        else:
            arrived(pel_recv.at[s, pl.ds(b * 64, 64)], base + 4, None)
        for h in halves:
            for c in range(2):
                cut = pl.ds(h * 64 + c * 32, 32)
                rows = slice(c * 32, c * 32 + 32)
                speed[h, rows, :] = speed[h, rows, :] - speed[h, 64:96, :] * (
                    pel_send[s, cut, :] + pel_recv[s, cut, :]
                )
        if s == 0:
            rows = []
            for h in range(2):
                for c in range(2):
                    cut = slice(c * 32, c * 32 + 32)
                    rows.append(table[h, cut, :] + TIME_STEP * speed[h, cut, :])
            rows = rows + [speed[0, 64:96, :], speed[1, 64:96, :]]
            top, low = split2(jnp.concatenate(rows, axis=0))
            product = jnp.dot(
                jnp.concatenate([top, low], axis=0),
                onehot[:, 8192:8448],
                preferred_element_type=F32,
            )
            early, pace = [], []
            for q in range(2):
                row = hrow[64 + q : 65 + q, :]
                part = product[:, q * 128 : (q + 1) * 128]
                early.append(
                    jnp.concatenate(
                        masked_rows(
                            jnp.concatenate([part[0:128], part[192:320]], axis=0), row
                        ),
                        axis=0,
                    )
                )
                steps = part[128:192] + part[320:384]
                hit = row_iota == jnp.broadcast_to(row, (64, 128))
                pace.append(
                    jnp.sum(jnp.where(hit, steps, 0.0), axis=0, keepdims=True)
                )
        arrived(late_recv.at[s], base + 5, None)
        other = late_recv[s]
        if s == 0:
            for t in range(2):
                ub1[theirs + t] = other[4 + 2 * t : 6 + 2 * t, :]
        for j in range(4):
            arrived(bd_recv.at[s, j], base + 6 + j, there[1 + j])
        shared = [
            jnp.where(
                jnp.full((2, 128), d, I32) > 0, bd_recv[s, 0] + bd_recv[s, 1], 0.0
            ),
            jnp.where(
                jnp.full((2, 128), d, I32) < n_dom - 1,
                bd_recv[s, 2] + bd_recv[s, 3],
                0.0,
            ),
        ]
        if s == 0:
            met = nt(two_parts(jnp.concatenate(shared, axis=1)), link[...])
            met = met[0:2, :] + met[2:4, :]
            blend(
                1,
                [
                    early[q]
                    + TIME_STEP
                    * pace[q]
                    * (
                        late[2 * q : 2 * q + 2, :]
                        + other[2 * q : 2 * q + 2, :]
                        + met[:, q * 128 : (q + 1) * 128]
                    )
                    for q in range(2)
                ],
            )
        sides = []
        for g, x in enumerate(
            [late[0:2, :] + other[0:2, :], late[2:4, :] + other[2:4, :]] + shared
        ):
            x_top = x.astype(BF16).astype(F32)
            x_low = x - x_top
            sides.append(
                spread(
                    [[y[0:1, :], y[1:2, :]] for y in (x_top, x_low)],
                    hrow[64 + g : 65 + g, :],
                )
            )
        extra = nt(jnp.concatenate(sides, axis=1), onehot[:, 8192:8704])
        acc[0:128, :] = extra[0:128, :] + extra[128:256, :]
        for h in halves:
            for c in range(2):
                cut = pl.ds(h * 64 + c * 32, 32)
                rows = slice(c * 32, c * 32 + 32)
                v = speed[h, rows, :] + speed[h, 64:96, :] * acc[cut, :]
                speed[h, rows, :] = v
                table[h, rows, :] = table[h, rows, :] + TIME_STEP * v

    for r in range(HALF_ROWS):
        lanes = slice(r * LO, (r + 1) * LO)
        for c in range(2):
            at = PAD_ROWS * c + r
            fdisp_out[c : c + 1, lanes] = table[b, at : at + 1, :]
            fvel_out[c : c + 1, lanes] = speed[b, at : at + 1, :]
    for copy, cond in started:
        if_there(cond, copy.wait_send)


def hand_over(*refs):
    ins, outs, sems = refs[:4], refs[4:8], refs[8]
    copies = [
        pltpu.make_async_copy(src, dst, sems.at[at])
        for at, (src, dst) in enumerate(zip(ins, outs))
    ]
    for copy in copies:
        copy.start()
    for copy in copies:
        copy.wait()


def shards(n_dom, *args):
    (
        pd_disp,
        pd_vel,
        pd_coord,
        pd_modulus,
        pd_step,
        family,
        live,
        patch_tile,
        patch_blend,
        patch_nodes,
        patch_matrix,
        fe_disp,
        fe_vel,
        fe_step,
        fe_modulus,
        element_nodes,
        shape_grad,
        quad_weight,
        shared_left,
        shared_right,
    ) = args
    vmem = pl.BlockSpec(memory_space=pltpu.VMEM)
    hbm = pl.BlockSpec(memory_space=pltpu.HBM)
    rows = fe_step.shape[0] // 128

    def f32(*shape):
        return pltpu.VMEM(shape, F32)

    results = pl.pallas_call(
        functools.partial(kernel, n_dom),
        out_shape=[
            pltpu.VMEM(pd_disp.shape, F32),
            pltpu.VMEM(pd_vel.shape, F32),
            pltpu.VMEM(fe_disp.shape, F32),
            pltpu.VMEM(fe_vel.shape, F32),
        ],
        in_specs=[hbm] * 20,
        out_specs=[vmem] * 4,
        scratch_shapes=[
            f32(2, 2, 128),
            f32(2, 2, 128),
            f32(2, 2, 128),
            f32(2, 128),
            f32(2, 128),
            pltpu.SMEM((2, 3), I32),
            pltpu.SMEM((1,), I32),
            pltpu.SMEM((2,), I32),
            f32(2, 128),
            pltpu.VMEM((1, 128), I32),
            f32(*fe_disp.shape),
            f32(*fe_vel.shape),
            f32(rows, 128),
            f32(1, 128),
            pltpu.VMEM((64, 128), I32),
            f32(128, 64),
            f32(1, 64),
            pltpu.VMEM((1, 113), I32),
            pltpu.VMEM((1, 113), I32),
            f32(20, 8, 128),
            f32(20, 2, 128),
            f32(20, 2, 128),
            f32(20, 2, 128),
            pltpu.VMEM((2, 3), I32),
            pltpu.VMEM((6, 8, 128), I32),
            pltpu.SMEM((6, 8, 128), I32),
            f32(2, 128, 128),
            pltpu.VMEM((2, 256, 128), BF16),
            f32(2, 64, LO),
            f32(2, 96, LO),
            pltpu.VMEM((256, LO), BF16),
            pltpu.VMEM((LO, 8704), BF16),
            pltpu.VMEM((72, 128), I32),
            pltpu.VMEM((8, 128), I32),
            pltpu.VMEM((256, 256), BF16),
            f32(64, 256),
            f32(64, 256),
            f32(64, 128),
            f32(256, LO),
            f32(6, 6, 128, 128),
            f32(2, 18, 128, 128),
            f32(6, 2, 128),
            f32(2, 2, 128),
            f32(2, 128, LO),
            f32(2, 128, LO),
            f32(2, 8, 128),
            f32(2, 8, 128),
            f32(2, 2, 2, 128),
            f32(2, 4, 2, 128),
            pltpu.SemaphoreType.DMA((N_COPIES,)),
            pltpu.SemaphoreType.DMA((N_COPIES,)),
            pltpu.SemaphoreType.DMA((22,)),
        ],
        compiler_params=pltpu.CompilerParams(
            collective_id=0, has_side_effects=True, vmem_limit_bytes=VMEM_BYTES
        ),
    )(
        pd_disp,
        pd_vel,
        pd_coord,
        pd_modulus,
        pd_step,
        family,
        live,
        patch_tile,
        patch_blend,
        patch_nodes,
        patch_matrix,
        fe_disp,
        fe_vel,
        fe_step.reshape(-1, 128),
        fe_modulus.reshape(1, -1),
        element_nodes,
        shape_grad.reshape(-1, shape_grad.shape[2]),
        quad_weight.reshape(1, -1),
        shared_left,
        shared_right,
    )
    return pl.pallas_call(
        hand_over,
        out_shape=[jax.ShapeDtypeStruct(x.shape, F32) for x in results],
        in_specs=[vmem] * 4,
        out_specs=[hbm] * 4,
        scratch_shapes=[pltpu.SemaphoreType.DMA((4,))],
        compiler_params=pltpu.CompilerParams(vmem_limit_bytes=2**20),
    )(*results)


def solution(mesh):
    both = ("dom", "blk")
    return jax.shard_map(
        functools.partial(shards, mesh.shape["dom"]),
        mesh=mesh,
        in_specs=(
            P(both, None, None),
            P(both, None, None),
            P(both, None, None),
            P(both, None),
            P(both, None),
            P(both, None),
            P("dom"),
            P("dom"),
            P("dom", None),
            P(both, None),
            P(both, None, None),
            P(None, both),
            P(None, both),
            P(both),
            P(both),
            P(None, both),
            P(),
            P(),
            P("dom", None),
            P("dom", None),
        ),
        out_specs=(
            P(both, None, None),
            P(both, None, None),
            P(None, both),
            P(None, both),
        ),
        check_vma=False,
    )
```

```python
import functools

import jax
import jax.numpy as jnp
from jax import lax
from jax.experimental import pallas as pl
from jax.experimental.pallas import tpu as pltpu
from jax.sharding import PartitionSpec as P

MESH = pl.DeviceIdType.MESH
F32 = jnp.float32
BF16 = jnp.bfloat16
I32 = jnp.int32
EXACT = lax.Precision.HIGHEST

TIME_STEP = 0.5
CORE_SQ = 0.01
STRETCH = 0.3

LO = 256
HALF_ROWS = 25
PAD_ROWS = 32
CHUNK = 8
N_COPIES = 37
VMEM_BYTES = 60 * 2**20


def split2(x):
    top = x.astype(BF16)
    return top, (x - top.astype(F32)).astype(BF16)


def folded(x):
    return jnp.sum(x.reshape(-1, 8, x.shape[1]), axis=0)


def inverted(x):
    y = pl.reciprocal(x, approx=True)
    return y * (2.0 - x * y)


def two_parts(x):
    top, low = split2(x)
    return jnp.concatenate([top, low, jnp.zeros((12, x.shape[1]), BF16)], axis=0)


def nt(a, b, **kw):
    return lax.dot_general(
        a, b, (((1,), (1,)), ((), ())), preferred_element_type=F32, **kw
    )


def kernel(
    n_dom,
    disp_in,
    vel_in,
    coord_in,
    modulus_in,
    step_in,
    family_in,
    live_in,
    ptile_in,
    pblend_in,
    pnodes_in,
    pmat_in,
    fdisp_in,
    fvel_in,
    fstep_in,
    fmod_in,
    enodes_in,
    sgrad_in,
    qweight_in,
    sleft_in,
    sright_in,
    disp_out,
    vel_out,
    fdisp_out,
    fvel_out,
    disp,
    vel,
    coord,
    modulus,
    step,
    family,
    live,
    ptile,
    pblend,
    pnodes,
    fdisp,
    fvel,
    fstep,
    fmod,
    enodes,
    sgrad,
    qweight,
    sleft,
    sright,
    pdx,
    ub0,
    ub1,
    place,
    lists_in,
    lists_sent,
    lists,
    pm,
    split_pm,
    table,
    speed,
    split_table,
    onehot,
    hrow,
    ids,
    link,
    del_,
    fel,
    sgt,
    acc,
    bonds,
    far_bonds,
    far_state,
    cur,
    pel_send,
    pel_recv,
    late_send,
    late_recv,
    bd_send,
    bd_recv,
    ssem,
    rsem,
    lsem,
):
    d = lax.axis_index("dom")
    b = lax.axis_index("blk")
    o = 1 - b
    has_left = d > 0
    has_right = d < n_dom - 1
    has_left2 = d > 1
    has_right2 = d < n_dom - 2
    left = jnp.maximum(d - 1, 0)
    right = jnp.minimum(d + 1, n_dom - 1)
    left2 = jnp.maximum(d - 2, 0)
    right2 = jnp.minimum(d + 2, n_dom - 1)
    peers = ((d, o),) + tuple(
        (x, j) for x in (left, right, left2, right2) for j in range(2)
    )
    there = (None,) + tuple(
        x for x in (has_left, has_right, has_left2, has_right2) for j in range(2)
    )

    def if_there(cond, act):
        if cond is None:
            act()
        else:
            pl.when(cond)(act)

    barrier = pltpu.get_barrier_semaphore()
    for peer, cond in zip(peers, there):
        if_there(
            cond,
            functools.partial(
                pl.semaphore_signal,
                barrier,
                inc=1,
                device_id=peer,
                device_id_type=MESH,
            ),
        )

    loads = {}
    for at, (src, dst) in enumerate(
        (
            (fdisp_in, fdisp),
            (coord_in, coord),
            (modulus_in, modulus),
            (disp_in, disp),
            (pnodes_in, pnodes),
            (pmat_in.at[0], pm.at[b]),
            (fvel_in, fvel),
            (fstep_in, fstep),
            (enodes_in, enodes),
            (vel_in, vel),
            (step_in, step),
            (family_in, family),
            (family_in, lists_in),
            (live_in, live),
            (ptile_in, ptile),
            (pblend_in, pblend),
            (fmod_in, fmod),
            (sgrad_in, sgrad),
            (qweight_in, qweight),
            (sleft_in, sleft),
            (sright_in, sright),
        )
    ):
        loads[at] = pltpu.make_async_copy(src, dst, lsem.at[at])
        loads[at].start()

    def loaded(*which):
        for at in which:
            loads[at].wait()

    started = []

    def send(src, dst, ssem_at, rsem_at, peer, cond):
        copy = pltpu.make_async_remote_copy(
            src_ref=src,
            dst_ref=dst,
            send_sem=ssem.at[ssem_at],
            recv_sem=rsem.at[rsem_at],
            device_id=peer,
            device_id_type=MESH,
        )
        if_there(cond, copy.start)
        started.append((copy, cond))

    def arrived(dst, rsem_at, cond):
        copy = pltpu.make_async_remote_copy(
            src_ref=dst,
            dst_ref=dst,
            send_sem=ssem.at[0],
            recv_sem=rsem.at[rsem_at],
            device_id=(d, o),
            device_id_type=MESH,
        )
        if_there(cond, copy.wait_recv)

    own = 8 + 2 * b
    theirs = 8 + 2 * o

    loaded(1, 2, 3, 4)
    for t in range(2):
        pdx[own + t] = jnp.concatenate(
            [
                coord[t],
                modulus[t : t + 1, :],
                disp[t],
                pnodes[...].astype(F32),
                jnp.zeros((2, 128), F32),
            ],
            axis=0,
        )
    loaded(0)
    table[b, 24:32, :] = jnp.zeros((8, LO), F32)
    table[b, 56:64, :] = jnp.zeros((8, LO), F32)
    for r in range(HALF_ROWS):
        for c in range(2):
            at = PAD_ROWS * c + r
            table[b, at : at + 1, :] = fdisp[c : c + 1, r * LO : (r + 1) * LO]
    loaded(6, 7)
    speed[b, 24:32, :] = jnp.zeros((8, LO), F32)
    speed[b, 56:64, :] = jnp.zeros((8, LO), F32)
    speed[b, 88:96, :] = jnp.zeros((8, LO), F32)
    for r in range(HALF_ROWS):
        for c in range(2):
            at = PAD_ROWS * c + r
            speed[b, at : at + 1, :] = fvel[c : c + 1, r * LO : (r + 1) * LO]
    for p in range(2):
        lanes = slice(p * 128, (p + 1) * 128)
        speed[b, 2 * PAD_ROWS : 2 * PAD_ROWS + HALF_ROWS, lanes] = fstep[
            pl.ds(p, HALF_ROWS, stride=2), :
        ]
    loaded(*range(8, 21))

    lo_iota = lax.broadcasted_iota(I32, (LO, 128), 0)

    def table_row(node):
        hi = lax.shift_right_arithmetic(node, 8)
        return jnp.where(hi >= HALF_ROWS, hi + (PAD_ROWS - HALF_ROWS), hi)

    def onehot_of(lo_row):
        return jnp.where(
            lo_iota == jnp.broadcast_to(lo_row, (LO, 128)), 1.0, 0.0
        ).astype(BF16)

    @pl.loop(0, 64 // CHUNK, unroll=4)
    def _(i):
        node = enodes[pl.ds(pl.multiple_of(i * CHUNK, CHUNK), CHUNK), :]
        hrow[pl.ds(pl.multiple_of(i * CHUNK, CHUNK), CHUNK), :] = table_row(node)
        lo = lax.bitwise_and(node, LO - 1)
        base = pl.multiple_of(i * (CHUNK * 128), CHUNK * 128)
        for g in range(CHUNK):
            onehot[:, pl.ds(base + g * 128, 128)] = onehot_of(lo[g : g + 1, :])

    sgt[...] = sgrad[...].T
    eye = lax.broadcasted_iota(I32, (64, 64), 0) == lax.broadcasted_iota(
        I32, (64, 64), 1
    )
    weight = jnp.sum(
        jnp.where(eye, jnp.broadcast_to(qweight[...], (64, 64)), 0.0),
        axis=1,
        keepdims=True,
    )
    scale = weight * fmod[...]


    lists_sent[2 + b] = jnp.zeros((8, 128), I32)
    lists_sent[2 + b, 0:2, 0:3] = lists_in[...]

    @pl.when(jnp.logical_not(has_left))
    def _():
        lists_sent[0:2] = jnp.zeros((2, 8, 128), I32)

    @pl.when(jnp.logical_not(has_right))
    def _():
        lists_sent[4:6] = jnp.zeros((2, 8, 128), I32)

    ids[...] = jnp.full((8, 128), -1, I32)
    ids[pl.ds(b, 1), :] = pnodes[...]
    ids[2:3, 0:113] = sleft[...]
    ids[3:4, 0:113] = sright[...]
    few_lo = lax.bitwise_and(ids[...], LO - 1)
    for g in (2, 3):
        onehot[:, 8192 + g * 128 : 8320 + g * 128] = onehot_of(few_lo[g : g + 1, :])

    pl.semaphore_wait(
        barrier, 1 + 2 * sum(x.astype(I32) for x in (has_left, has_right, has_left2, has_right2))
    )

    send(table.at[b], table.at[b], 0, 0, (d, o), None)
    slots = (own,) + tuple(x + 2 * b for x in (12, 12, 4, 4, 16, 16, 0, 0))
    marks = (0,) + tuple(x + b for x in (3, 3, 1, 1, 7, 7, 5, 5))
    homes = (2 + b,) + tuple(x + b for x in (4, 4, 0, 0))
    loaded(5)
    send(pm.at[b], pm.at[b], 1, 1, (d, o), None)
    for j in range(9):
        send(
            pdx.at[pl.ds(own, 2)],
            pdx.at[pl.ds(slots[j], 2)],
            3 + j,
            3 + marks[j],
            peers[j],
            there[j],
        )
    sources = (theirs, 4, 6, 12, 14, 0, 2, 16, 18)
    sources_lists = (2 + o, 0, 1, 4, 5)
    send(speed.at[b], speed.at[b], 2, 2, (d, o), None)
    states = (started[0][0], started.pop()[0])
    del started[0]
    for j in range(5):
        send(
            lists_sent.at[2 + b],
            lists_sent.at[homes[j]],
            12 + j,
            12 + marks[j],
            peers[j],
            there[j],
        )

    arrived(pdx.at[pl.ds(theirs, 2)], 3, None)
    ids[pl.ds(o, 1), :] = pdx[theirs, 5:6, :].astype(I32)
    few = ids[...]
    hrow[64:72, :] = table_row(few)
    few_lo = lax.bitwise_and(few, LO - 1)
    for g in range(2):
        onehot[:, 8192 + g * 128 : 8320 + g * 128] = onehot_of(few_lo[g : g + 1, :])

    REST, INFL0, NX, NY, STR, INFL = range(6)
    cur[...] = vel[...]

    def keep_pair(into, p, far, me):
        far_t = pdx[far].T
        for q in range(0, 128, 32):
            rows = slice(q, q + 32)
            ox = far_t[rows, 0:1] - me[0:1, :]
            oy = far_t[rows, 1:2] - me[1:2, :]
            r2 = ox * ox + oy * oy
            into[REST, p, rows] = jnp.sqrt(r2 + CORE_SQ)
            into[INFL0, p, rows] = jnp.exp(-0.5 * r2)

    def named(p):
        return family[p // 3, p % 3]

    def named_far(f, k):
        listed = lists[lax.shift_right_arithmetic(f, 1), lax.bitwise_and(f, 1), k]
        return listed + lax.shift_left(lax.shift_right_arithmetic(f, 2), 2)

    def keep_bonds():
        for p in range(6):
            keep_pair(bonds, p, named(p) + 4, pdx[own + p // 3])

        @pl.loop(0, 6, unroll=6)
        def _(p):
            t = p // 3
            f = family[t, p - 3 * t]
            me = pdx[f + 4]
            for k in range(3):
                keep_pair(far_bonds, 3 * p + k, named_far(f, k), me)

    def stretched(kept, p, rows, far_t, me):
        yx = far_t[rows, 0:1] - me[0:1, :]
        yy = far_t[rows, 1:2] - me[1:2, :]
        y2 = yx * yx + yy * yy + CORE_SQ
        inverse = lax.rsqrt(y2)
        rest = kept[REST, p, rows]
        stretch = y2 * inverse - rest
        ratio = stretch * (1.0 / STRETCH)
        influence = kept[INFL0, p, rows] * inverted(1.0 + ratio * ratio)
        return yx, yy, inverse, rest, stretch, influence

    def columns(far):
        return jnp.concatenate([place[far], jnp.zeros((6, 128), F32)], axis=0).T

    def state_of(total):
        dilated, volume = [jnp.sum(x, axis=0, keepdims=True) for x in total]
        return jnp.concatenate([2.0 * dilated / volume, volume], axis=0)

    row_iota = lax.broadcasted_iota(I32, (64, 128), 0)

    def masked_rows(product, row):
        both = product[0:128] + product[128:256]
        hit = row_iota == jnp.broadcast_to(row, (64, 128))
        out = []
        for c in range(2):
            x = jnp.where(hit[0:32], both[c * 32 : c * 32 + 32], 0.0)
            x = x + jnp.where(hit[32:64], both[64 + c * 32 : 96 + c * 32], 0.0)
            out.append(jnp.sum(x, axis=0, keepdims=True))
        return out

    def spread(values, row):
        hit = row_iota == jnp.broadcast_to(row, (64, 128))
        blocks = []
        for part in range(2):
            wide = [
                jnp.where(hit, jnp.broadcast_to(values[part][c], (64, 128)), 0.0)
                for c in range(2)
            ]
            for half in range(2):
                for c in range(2):
                    blocks.append(wide[c][half * 32 : half * 32 + 32])
        return jnp.concatenate(blocks, axis=0).astype(BF16)

    def blend(s, picked):
        ub = (ub0, ub1)[s]
        base = 17 + 10 * s
        targets = []
        for q in range(2):
            x = nt(two_parts(picked[q]), split_pm[q])
            targets.append(x[0:2, 0:128] + x[2:4, 0:128] + x[0:2, 128:256])
        for k in range(4):
            u = pdx[8 + k, 3:5, :] if s == 0 else ub[8 + k]
            new = u
            for q in range(2):
                hit = jnp.full((2, 128), ptile[q], I32) == k
                new = jnp.where(hit, u + pblend[q : q + 1, :] * (targets[q] - u), new)
            ub[8 + k] = new
        mine = ub.at[pl.ds(8, 4)]
        for j, (to, at, peer, cond) in enumerate(
            (
                (16, 3, left2, has_left2),
                (0, 2, right2, has_right2),
                (12, 1, left, has_left),
                (4, 0, right, has_right),
            )
        ):
            send(mine, ub.at[pl.ds(to, 4)], base + j, base + at, (peer, b), cond)

    for s in range(2):
        ub = (ub0, ub1)[s]
        base = 17 + 10 * s
        if s == 0:
            arrived(table.at[o], 0, None)
            arrived(pm.at[o], 1, None)
            for q in range(2):
                top, low = split2(pm[q])
                split_pm[q, 0:128] = top
                split_pm[q, 128:256] = low

        top, low = split2(table[...].reshape(128, LO))
        split_table[0:128, :] = top
        split_table[128:256, :] = low
        if s == 0:
            product = jnp.dot(
                split_table[...], onehot[:, 8192:8448], preferred_element_type=F32
            )
            blend(
                0,
                [
                    jnp.concatenate(
                        masked_rows(
                            product[:, q * 128 : (q + 1) * 128], hrow[64 + q : 65 + q, :]
                        ),
                        axis=0,
                    )
                    for q in range(2)
                ],
            )

        @pl.loop(0, 64 // CHUNK, unroll=4)
        def _(i):
            rows = pl.ds(pl.multiple_of(i * CHUNK, CHUNK), CHUNK)
            lanes = pl.ds(pl.multiple_of(i * (CHUNK * 128), CHUNK * 128), CHUNK * 128)
            product = jnp.dot(
                split_table[...], onehot[:, lanes], preferred_element_type=F32
            )
            row = hrow[rows, :]
            found = [
                masked_rows(product[:, g * 128 : (g + 1) * 128], row[g : g + 1, :])
                for g in range(CHUNK)
            ]
            for c in range(2):
                del_[rows, c * 128 : (c + 1) * 128] = jnp.concatenate(
                    [f[c] for f in found], axis=0
                )

        if s == 0:
            few_f = ids[...].astype(F32)
            few_t = few_f.T
            for q in range(2):
                for side in range(2):
                    link[
                        q * 128 : (q + 1) * 128, side * 128 : (side + 1) * 128
                    ] = jnp.where(
                        few_t[:, q : q + 1] == few_f[2 + side : 3 + side, :], 1.0, 0.0
                    ).astype(BF16)

        grad = jnp.dot(sgrad[...], del_[...], precision=EXACT, preferred_element_type=F32)
        exx = grad[0:64, 0:128]
        eyy = grad[64:128, 128:256]
        exy = 0.5 * (grad[64:128, 0:128] + grad[0:64, 128:256])
        scaled = scale * (1.0 + exx * exx + eyy * eyy + 2.0 * exy * exy)
        both = exx + eyy
        sxx = scaled * (both + 2.0 * exx)
        syy = scaled * (both + 2.0 * eyy)
        sxy = scaled * 2.0 * exy
        stress = jnp.concatenate(
            [
                jnp.concatenate([sxx, sxy], axis=1),
                jnp.concatenate([sxy, syy], axis=1),
            ],
            axis=0,
        )
        fel[...] = jnp.dot(sgt[...], stress, precision=EXACT, preferred_element_type=F32)
        acc[...] = jnp.zeros((256, LO), F32)

        @pl.loop(0, 64 // CHUNK, unroll=4)
        def _(i):
            rows = pl.ds(pl.multiple_of(i * CHUNK, CHUNK), CHUNK)
            lanes = pl.ds(pl.multiple_of(i * (CHUNK * 128), CHUNK * 128), CHUNK * 128)
            row = hrow[rows, :]
            f = fel[rows, :]
            f_top = f.astype(BF16).astype(F32)
            f_low = f - f_top
            left_side = jnp.concatenate(
                [
                    spread(
                        [
                            [x[g : g + 1, 0:128], x[g : g + 1, 128:256]]
                            for x in (f_top, f_low)
                        ],
                        row[g : g + 1, :],
                    )
                    for g in range(CHUNK)
                ],
                axis=1,
            )
            acc[...] += nt(left_side, onehot[:, lanes])

        partial = acc[0:128, :] + acc[128:256, :]
        pel_send[s] = partial
        if s == 0:
            send(pel_send.at[s], pel_recv.at[s], base + 4, base + 4, (d, o), None)
        else:
            cut = pl.ds(o * 64, 64)
            send(
                pel_send.at[s, cut],
                pel_recv.at[s, cut],
                base + 4,
                base + 4,
                (d, o),
                None,
            )
        top, low = split2(partial)
        product = jnp.dot(
            jnp.concatenate([top, low], axis=0),
            onehot[:, 8448:8704],
            preferred_element_type=F32,
        )
        border = []
        for side in range(2):
            found = masked_rows(
                product[:, side * 128 : (side + 1) * 128],
                hrow[66 + side : 67 + side, :],
            )
            border.append(jnp.concatenate(found, axis=0))

        if s == 0:
            for j in range(1, 9):
                arrived(pdx.at[pl.ds(sources[j], 2)], 3 + j, there[j])
            for j in range(5):
                arrived(lists_sent.at[sources_lists[j]], 12 + j, there[j])
            scalars = pltpu.make_async_copy(lists_sent, lists, lsem.at[21])
            scalars.start()
            scalars.wait()
            keep_bonds()

        arrived(ub.at[pl.ds(4, 4)], base, has_left)
        arrived(ub.at[pl.ds(12, 4)], base + 1, has_right)
        place[4:16] = pdx[4:16, 0:2, :] + ub[4:16]

        totals = [[jnp.zeros((8, 128), F32)] * 2 for _ in range(2)]
        for p in range(6):
            t = p // 3
            far_t = columns(named(p) + 4)
            me = place[own + t]
            for q in range(0, 128, 32):
                rows = slice(q, q + 32)
                yx, yy, inverse, rest, stretch, influence = stretched(
                    bonds, p, rows, far_t, me
                )
                bonds[NX, p, rows] = yx * inverse
                bonds[NY, p, rows] = yy * inverse
                bonds[STR, p, rows] = stretch
                bonds[INFL, p, rows] = influence
                weighted = influence * rest
                totals[t][0] = totals[t][0] + folded(weighted * stretch)
                totals[t][1] = totals[t][1] + folded(weighted * rest)
        states_own = [state_of(x) for x in totals]
        arrived(ub.at[pl.ds(0, 4)], base + 2, has_left2)
        arrived(ub.at[pl.ds(16, 4)], base + 3, has_right2)
        place[0:4] = pdx[0:4, 0:2, :] + ub[0:4]
        place[16:20] = pdx[16:20, 0:2, :] + ub[16:20]

        @pl.loop(0, 3, unroll=3)
        def _(i):
            for j in range(2):
                p = 2 * i + j
                t = p // 3
                f = family[t, p - 3 * t]
                me = place[f + 4]
                total = [jnp.zeros((8, 128), F32)] * 2
                for k in range(3):
                    far_t = columns(named_far(f, k))
                    for q in range(0, 128, 32):
                        *_, rest, stretch, influence = stretched(
                            far_bonds, 3 * p + k, slice(q, q + 32), far_t, me
                        )
                        weighted = influence * rest
                        total[0] = total[0] + folded(weighted * stretch)
                        total[1] = total[1] + folded(weighted * rest)
                far_state[p] = state_of(total)

        def coefficients(k, state):
            theta, volume = state[0:1, :], state[1:2, :]
            return 2.0 * k * theta / volume, 4.0 * k / volume, 0.5 * theta

        totals = [[jnp.zeros((8, 128), F32)] * 2 for _ in range(2)]
        near = [coefficients(pdx[own + t][2:3, :], states_own[t]) for t in range(2)]
        for p in range(6):
            t = p // 3
            far = coefficients(pdx[named(p) + 4][2:3, :], far_state[p])
            far_t = jnp.concatenate(far + (jnp.zeros((5, 128), F32),), axis=0).T
            oa, ob, oc = near[t]
            for q in range(0, 128, 32):
                rows = slice(q, q + 32)
                rest = bonds[REST, p, rows]
                stretch = bonds[STR, p, rows]
                mine = oa * rest + ob * (stretch - oc * rest)
                away = far_t[rows, 0:1] * rest + far_t[rows, 1:2] * (
                    stretch - far_t[rows, 2:3] * rest
                )
                force = bonds[INFL, p, rows] * (mine + away)
                totals[t][0] = totals[t][0] + folded(force * bonds[NX, p, rows])
                totals[t][1] = totals[t][1] + folded(force * bonds[NY, p, rows])

        forces, moved = [], []
        for t in range(2):
            alive = jnp.full((2, 128), 2 * b + t, I32) < live[0]
            total = [jnp.sum(x, axis=0, keepdims=True) for x in totals[t]]
            force = jnp.where(alive, jnp.concatenate(total, axis=0), 0.0)
            forces.append(force)
            v = jnp.where(alive, cur[t] + step[t : t + 1, :] * force, 0.0)
            u = jnp.where(alive, ub[own + t] + TIME_STEP * v, 0.0)
            cur[t] = v
            moved.append(u)

        reaction = []
        for q in range(2):
            w = jnp.zeros((2, 128), F32)
            for t in range(2):
                hit = jnp.full((2, 128), ptile[q], I32) == 2 * b + t
                w = w + jnp.where(hit, pblend[q : q + 1, :] * forces[t], 0.0)
            w = two_parts(w)
            x = jnp.dot(w, split_pm[q, 0:128], preferred_element_type=F32)
            y = jnp.dot(w, split_pm[q, 128:256], preferred_element_type=F32)
            reaction.append(x[0:2, :] + x[2:4, :] + y[0:2, :])
        late = jnp.concatenate(reaction + moved, axis=0)
        late_send[s] = late
        send(late_send.at[s], late_recv.at[s], base + 5, base + 5, (d, o), None)
        wide = jnp.concatenate(reaction, axis=1)
        met = jnp.dot(two_parts(wide), link[...], preferred_element_type=F32)
        met = met[0:2, :] + met[2:4, :]
        for side in range(2):
            bd_send[s, side] = met[:, side * 128 : (side + 1) * 128] - border[side]
        for j in range(4):
            side = j // 2
            send(
                bd_send.at[s, side],
                bd_recv.at[s, 2 * (1 - side) + b],
                base + 6 + j,
                base + 6 + 2 * (1 - side) + b,
                peers[1 + j],
                there[1 + j],
            )
        if s == 0:
            for t in range(2):
                ub1[own + t] = moved[t]
        else:
            for t in range(2):
                disp_out[t] = moved[t]
                vel_out[t] = cur[t]

        halves = range(2) if s == 0 else (b,)
        if s == 0:
            arrived(speed.at[o], 2, None)
            arrived(pel_recv.at[s], base + 4, None)
            for copy in states:
                copy.wait_send()
        else:
            arrived(pel_recv.at[s, pl.ds(b * 64, 64)], base + 4, None)
        for h in halves:
            for c in range(2):
                cut = pl.ds(h * 64 + c * 32, 32)
                rows = slice(c * 32, c * 32 + 32)
                speed[h, rows, :] = speed[h, rows, :] - speed[h, 64:96, :] * (
                    pel_send[s, cut, :] + pel_recv[s, cut, :]
                )
        if s == 0:
            rows = []
            for h in range(2):
                for c in range(2):
                    cut = slice(c * 32, c * 32 + 32)
                    rows.append(table[h, cut, :] + TIME_STEP * speed[h, cut, :])
            rows = rows + [speed[0, 64:96, :], speed[1, 64:96, :]]
            top, low = split2(jnp.concatenate(rows, axis=0))
            product = jnp.dot(
                jnp.concatenate([top, low], axis=0),
                onehot[:, 8192:8448],
                preferred_element_type=F32,
            )
            early, pace = [], []
            for q in range(2):
                row = hrow[64 + q : 65 + q, :]
                part = product[:, q * 128 : (q + 1) * 128]
                early.append(
                    jnp.concatenate(
                        masked_rows(
                            jnp.concatenate([part[0:128], part[192:320]], axis=0), row
                        ),
                        axis=0,
                    )
                )
                steps = part[128:192] + part[320:384]
                hit = row_iota == jnp.broadcast_to(row, (64, 128))
                pace.append(
                    jnp.sum(jnp.where(hit, steps, 0.0), axis=0, keepdims=True)
                )
        arrived(late_recv.at[s], base + 5, None)
        other = late_recv[s]
        if s == 0:
            for t in range(2):
                ub1[theirs + t] = other[4 + 2 * t : 6 + 2 * t, :]
        for j in range(4):
            arrived(bd_recv.at[s, j], base + 6 + j, there[1 + j])
        shared = [
            jnp.where(
                jnp.full((2, 128), d, I32) > 0, bd_recv[s, 0] + bd_recv[s, 1], 0.0
            ),
            jnp.where(
                jnp.full((2, 128), d, I32) < n_dom - 1,
                bd_recv[s, 2] + bd_recv[s, 3],
                0.0,
            ),
        ]
        if s == 0:
            met = nt(two_parts(jnp.concatenate(shared, axis=1)), link[...])
            met = met[0:2, :] + met[2:4, :]
            blend(
                1,
                [
                    early[q]
                    + TIME_STEP
                    * pace[q]
                    * (
                        late[2 * q : 2 * q + 2, :]
                        + other[2 * q : 2 * q + 2, :]
                        + met[:, q * 128 : (q + 1) * 128]
                    )
                    for q in range(2)
                ],
            )
        sides = []
        for g, x in enumerate(
            [late[0:2, :] + other[0:2, :], late[2:4, :] + other[2:4, :]] + shared
        ):
            x_top = x.astype(BF16).astype(F32)
            x_low = x - x_top
            sides.append(
                spread(
                    [[y[0:1, :], y[1:2, :]] for y in (x_top, x_low)],
                    hrow[64 + g : 65 + g, :],
                )
            )
        extra = nt(jnp.concatenate(sides, axis=1), onehot[:, 8192:8704])
        acc[0:128, :] = extra[0:128, :] + extra[128:256, :]
        for h in halves:
            for c in range(2):
                cut = pl.ds(h * 64 + c * 32, 32)
                rows = slice(c * 32, c * 32 + 32)
                v = speed[h, rows, :] + speed[h, 64:96, :] * acc[cut, :]
                speed[h, rows, :] = v
                table[h, rows, :] = table[h, rows, :] + TIME_STEP * v

    for r in range(HALF_ROWS):
        lanes = slice(r * LO, (r + 1) * LO)
        for c in range(2):
            at = PAD_ROWS * c + r
            fdisp_out[c : c + 1, lanes] = table[b, at : at + 1, :]
            fvel_out[c : c + 1, lanes] = speed[b, at : at + 1, :]
    for copy, cond in started:
        if_there(cond, copy.wait_send)


def hand_over(*refs):
    ins, outs, sems = refs[:4], refs[4:8], refs[8]
    copies = [
        pltpu.make_async_copy(src, dst, sems.at[at])
        for at, (src, dst) in enumerate(zip(ins, outs))
    ]
    for copy in copies:
        copy.start()
    for copy in copies:
        copy.wait()


def shards(n_dom, *args):
    (
        pd_disp,
        pd_vel,
        pd_coord,
        pd_modulus,
        pd_step,
        family,
        live,
        patch_tile,
        patch_blend,
        patch_nodes,
        patch_matrix,
        fe_disp,
        fe_vel,
        fe_step,
        fe_modulus,
        element_nodes,
        shape_grad,
        quad_weight,
        shared_left,
        shared_right,
    ) = args
    vmem = pl.BlockSpec(memory_space=pltpu.VMEM)
    hbm = pl.BlockSpec(memory_space=pltpu.HBM)
    rows = fe_step.shape[0] // 128

    def f32(*shape):
        return pltpu.VMEM(shape, F32)

    results = pl.pallas_call(
        functools.partial(kernel, n_dom),
        out_shape=[
            pltpu.VMEM(pd_disp.shape, F32),
            pltpu.VMEM(pd_vel.shape, F32),
            pltpu.VMEM(fe_disp.shape, F32),
            pltpu.VMEM(fe_vel.shape, F32),
        ],
        in_specs=[hbm] * 20,
        out_specs=[vmem] * 4,
        scratch_shapes=[
            f32(2, 2, 128),
            f32(2, 2, 128),
            f32(2, 2, 128),
            f32(2, 128),
            f32(2, 128),
            pltpu.SMEM((2, 3), I32),
            pltpu.SMEM((1,), I32),
            pltpu.SMEM((2,), I32),
            f32(2, 128),
            pltpu.VMEM((1, 128), I32),
            f32(*fe_disp.shape),
            f32(*fe_vel.shape),
            f32(rows, 128),
            f32(1, 128),
            pltpu.VMEM((64, 128), I32),
            f32(128, 64),
            f32(1, 64),
            pltpu.VMEM((1, 113), I32),
            pltpu.VMEM((1, 113), I32),
            f32(20, 8, 128),
            f32(20, 2, 128),
            f32(20, 2, 128),
            f32(20, 2, 128),
            pltpu.VMEM((2, 3), I32),
            pltpu.VMEM((6, 8, 128), I32),
            pltpu.SMEM((6, 8, 128), I32),
            f32(2, 128, 128),
            pltpu.VMEM((2, 256, 128), BF16),
            f32(2, 64, LO),
            f32(2, 96, LO),
            pltpu.VMEM((256, LO), BF16),
            pltpu.VMEM((LO, 8704), BF16),
            pltpu.VMEM((72, 128), I32),
            pltpu.VMEM((8, 128), I32),
            pltpu.VMEM((256, 256), BF16),
            f32(64, 256),
            f32(64, 256),
            f32(64, 128),
            f32(256, LO),
            f32(6, 6, 128, 128),
            f32(2, 18, 128, 128),
            f32(6, 2, 128),
            f32(2, 2, 128),
            f32(2, 128, LO),
            f32(2, 128, LO),
            f32(2, 8, 128),
            f32(2, 8, 128),
            f32(2, 2, 2, 128),
            f32(2, 4, 2, 128),
            pltpu.SemaphoreType.DMA((N_COPIES,)),
            pltpu.SemaphoreType.DMA((N_COPIES,)),
            pltpu.SemaphoreType.DMA((22,)),
        ],
        compiler_params=pltpu.CompilerParams(
            collective_id=0, has_side_effects=True, vmem_limit_bytes=VMEM_BYTES
        ),
    )(
        pd_disp,
        pd_vel,
        pd_coord,
        pd_modulus,
        pd_step,
        family,
        live,
        patch_tile,
        patch_blend,
        patch_nodes,
        patch_matrix,
        fe_disp,
        fe_vel,
        fe_step.reshape(-1, 128),
        fe_modulus.reshape(1, -1),
        element_nodes,
        shape_grad.reshape(-1, shape_grad.shape[2]),
        quad_weight.reshape(1, -1),
        shared_left,
        shared_right,
    )
    return pl.pallas_call(
        hand_over,
        out_shape=[jax.ShapeDtypeStruct(x.shape, F32) for x in results],
        in_specs=[vmem] * 4,
        out_specs=[hbm] * 4,
        scratch_shapes=[pltpu.SemaphoreType.DMA((4,))],
        compiler_params=pltpu.CompilerParams(vmem_limit_bytes=2**20),
    )(*results)


def solution(mesh):
    both = ("dom", "blk")
    return jax.shard_map(
        functools.partial(shards, mesh.shape["dom"]),
        mesh=mesh,
        in_specs=(
            P(both, None, None),
            P(both, None, None),
            P(both, None, None),
            P(both, None),
            P(both, None),
            P(both, None),
            P("dom"),
            P("dom"),
            P("dom", None),
            P(both, None),
            P(both, None, None),
            P(None, both),
            P(None, both),
            P(both),
            P(both),
            P(None, both),
            P(),
            P(),
            P("dom", None),
            P("dom", None),
        ),
        out_specs=(
            P(both, None, None),
            P(both, None, None),
            P(None, both),
            P(None, both),
        ),
        check_vma=False,
    )
```

```python
import functools

import jax
import jax.numpy as jnp
from jax import lax
from jax.experimental import pallas as pl
from jax.experimental.pallas import tpu as pltpu
from jax.sharding import PartitionSpec as P

MESH = pl.DeviceIdType.MESH
F32 = jnp.float32
BF16 = jnp.bfloat16
I32 = jnp.int32
EXACT = lax.Precision.HIGHEST

TIME_STEP = 0.5
CORE_SQ = 0.01
STRETCH = 0.3

LO = 256
HALF_ROWS = 25
PAD_ROWS = 32
CHUNK = 8
N_COPIES = 37
VMEM_BYTES = 60 * 2**20


def split2(x):
    top = x.astype(BF16)
    return top, (x - top.astype(F32)).astype(BF16)


def folded(x):
    return jnp.sum(x.reshape(-1, 8, x.shape[1]), axis=0)


def inverted(x):
    y = pl.reciprocal(x, approx=True)
    return y * (2.0 - x * y)


def two_parts(x):
    top, low = split2(x)
    return jnp.concatenate([top, low, jnp.zeros((12, x.shape[1]), BF16)], axis=0)


def nt(a, b, **kw):
    return lax.dot_general(
        a, b, (((1,), (1,)), ((), ())), preferred_element_type=F32, **kw
    )


def kernel(
    n_dom,
    disp_in,
    vel_in,
    coord_in,
    modulus_in,
    step_in,
    family_in,
    live_in,
    ptile_in,
    pblend_in,
    pnodes_in,
    pmat_in,
    fdisp_in,
    fvel_in,
    fstep_in,
    fmod_in,
    enodes_in,
    sgrad_in,
    qweight_in,
    sleft_in,
    sright_in,
    disp_out,
    vel_out,
    fdisp_out,
    fvel_out,
    disp,
    vel,
    coord,
    modulus,
    step,
    family,
    live,
    ptile,
    pblend,
    pnodes,
    fdisp,
    fvel,
    fstep,
    fmod,
    enodes,
    sgrad,
    qweight,
    sleft,
    sright,
    pdx,
    ub0,
    ub1,
    place,
    lists_in,
    lists_sent,
    lists,
    pm,
    split_pm,
    table,
    speed,
    split_table,
    onehot,
    hrow,
    ids,
    link,
    del_,
    fel,
    sgt,
    acc,
    bonds,
    far_bonds,
    far_state,
    cur,
    pel_send,
    pel_recv,
    late_send,
    late_recv,
    bd_send,
    bd_recv,
    ssem,
    rsem,
    lsem,
):
    d = lax.axis_index("dom")
    b = lax.axis_index("blk")
    o = 1 - b
    has_left = d > 0
    has_right = d < n_dom - 1
    has_left2 = d > 1
    has_right2 = d < n_dom - 2
    left = jnp.maximum(d - 1, 0)
    right = jnp.minimum(d + 1, n_dom - 1)
    left2 = jnp.maximum(d - 2, 0)
    right2 = jnp.minimum(d + 2, n_dom - 1)
    peers = ((d, o),) + tuple(
        (x, j) for x in (left, right, left2, right2) for j in range(2)
    )
    there = (None,) + tuple(
        x for x in (has_left, has_right, has_left2, has_right2) for j in range(2)
    )

    def if_there(cond, act):
        if cond is None:
            act()
        else:
            pl.when(cond)(act)

    barrier = pltpu.get_barrier_semaphore()
    for peer, cond in zip(peers, there):
        if_there(
            cond,
            functools.partial(
                pl.semaphore_signal,
                barrier,
                inc=1,
                device_id=peer,
                device_id_type=MESH,
            ),
        )

    loads = {}
    for at, (src, dst) in enumerate(
        (
            (fdisp_in, fdisp),
            (coord_in, coord),
            (modulus_in, modulus),
            (disp_in, disp),
            (pnodes_in, pnodes),
            (pmat_in.at[0], pm.at[b]),
            (fvel_in, fvel),
            (fstep_in, fstep),
            (enodes_in, enodes),
            (vel_in, vel),
            (step_in, step),
            (family_in, family),
            (family_in, lists_in),
            (live_in, live),
            (ptile_in, ptile),
            (pblend_in, pblend),
            (fmod_in, fmod),
            (sgrad_in, sgrad),
            (qweight_in, qweight),
            (sleft_in, sleft),
            (sright_in, sright),
        )
    ):
        loads[at] = pltpu.make_async_copy(src, dst, lsem.at[at])
        loads[at].start()

    def loaded(*which):
        for at in which:
            loads[at].wait()

    started = []

    def send(src, dst, ssem_at, rsem_at, peer, cond):
        copy = pltpu.make_async_remote_copy(
            src_ref=src,
            dst_ref=dst,
            send_sem=ssem.at[ssem_at],
            recv_sem=rsem.at[rsem_at],
            device_id=peer,
            device_id_type=MESH,
        )
        if_there(cond, copy.start)
        started.append((copy, cond))

    def arrived(dst, rsem_at, cond):
        copy = pltpu.make_async_remote_copy(
            src_ref=dst,
            dst_ref=dst,
            send_sem=ssem.at[0],
            recv_sem=rsem.at[rsem_at],
            device_id=(d, o),
            device_id_type=MESH,
        )
        if_there(cond, copy.wait_recv)

    own = 8 + 2 * b
    theirs = 8 + 2 * o

    loaded(1, 2, 3, 4)
    for t in range(2):
        pdx[own + t] = jnp.concatenate(
            [
                coord[t],
                modulus[t : t + 1, :],
                disp[t],
                pnodes[...].astype(F32),
                jnp.zeros((2, 128), F32),
            ],
            axis=0,
        )
    loaded(0)
    table[b, 24:32, :] = jnp.zeros((8, LO), F32)
    table[b, 56:64, :] = jnp.zeros((8, LO), F32)
    for r in range(HALF_ROWS):
        for c in range(2):
            at = PAD_ROWS * c + r
            table[b, at : at + 1, :] = fdisp[c : c + 1, r * LO : (r + 1) * LO]
    loaded(6, 7)
    speed[b, 24:32, :] = jnp.zeros((8, LO), F32)
    speed[b, 56:64, :] = jnp.zeros((8, LO), F32)
    speed[b, 88:96, :] = jnp.zeros((8, LO), F32)
    for r in range(HALF_ROWS):
        for c in range(2):
            at = PAD_ROWS * c + r
            speed[b, at : at + 1, :] = fvel[c : c + 1, r * LO : (r + 1) * LO]
    for p in range(2):
        lanes = slice(p * 128, (p + 1) * 128)
        speed[b, 2 * PAD_ROWS : 2 * PAD_ROWS + HALF_ROWS, lanes] = fstep[
            pl.ds(p, HALF_ROWS, stride=2), :
        ]
    loaded(*range(8, 21))

    lo_iota = lax.broadcasted_iota(I32, (LO, 128), 0)

    def table_row(node):
        hi = lax.shift_right_arithmetic(node, 8)
        return jnp.where(hi >= HALF_ROWS, hi + (PAD_ROWS - HALF_ROWS), hi)

    def onehot_of(lo_row):
        return jnp.where(
            lo_iota == jnp.broadcast_to(lo_row, (LO, 128)), 1.0, 0.0
        ).astype(BF16)

    @pl.loop(0, 64 // CHUNK, unroll=4)
    def _(i):
        node = enodes[pl.ds(pl.multiple_of(i * CHUNK, CHUNK), CHUNK), :]
        hrow[pl.ds(pl.multiple_of(i * CHUNK, CHUNK), CHUNK), :] = table_row(node)
        lo = lax.bitwise_and(node, LO - 1)
        base = pl.multiple_of(i * (CHUNK * 128), CHUNK * 128)
        for g in range(CHUNK):
            onehot[:, pl.ds(base + g * 128, 128)] = onehot_of(lo[g : g + 1, :])

    sgt[...] = sgrad[...].T
    eye = lax.broadcasted_iota(I32, (64, 64), 0) == lax.broadcasted_iota(
        I32, (64, 64), 1
    )
    weight = jnp.sum(
        jnp.where(eye, jnp.broadcast_to(qweight[...], (64, 64)), 0.0),
        axis=1,
        keepdims=True,
    )
    scale = weight * fmod[...]


    lists_sent[2 + b] = jnp.zeros((8, 128), I32)
    lists_sent[2 + b, 0:2, 0:3] = lists_in[...]

    @pl.when(jnp.logical_not(has_left))
    def _():
        lists_sent[0:2] = jnp.zeros((2, 8, 128), I32)

    @pl.when(jnp.logical_not(has_right))
    def _():
        lists_sent[4:6] = jnp.zeros((2, 8, 128), I32)

    ids[...] = jnp.full((8, 128), -1, I32)
    ids[pl.ds(b, 1), :] = pnodes[...]
    ids[2:3, 0:113] = sleft[...]
    ids[3:4, 0:113] = sright[...]
    few_lo = lax.bitwise_and(ids[...], LO - 1)
    for g in (2, 3):
        onehot[:, 8192 + g * 128 : 8320 + g * 128] = onehot_of(few_lo[g : g + 1, :])

    pl.semaphore_wait(
        barrier, 1 + 2 * sum(x.astype(I32) for x in (has_left, has_right, has_left2, has_right2))
    )

    send(table.at[b], table.at[b], 0, 0, (d, o), None)
    slots = (own,) + tuple(x + 2 * b for x in (12, 12, 4, 4, 16, 16, 0, 0))
    marks = (0,) + tuple(x + b for x in (3, 3, 1, 1, 7, 7, 5, 5))
    homes = (2 + b,) + tuple(x + b for x in (4, 4, 0, 0))
    loaded(5)
    send(pm.at[b], pm.at[b], 1, 1, (d, o), None)
    for j in range(9):
        send(
            pdx.at[pl.ds(own, 2)],
            pdx.at[pl.ds(slots[j], 2)],
            3 + j,
            3 + marks[j],
            peers[j],
            there[j],
        )
    sources = (theirs, 4, 6, 12, 14, 0, 2, 16, 18)
    sources_lists = (2 + o, 0, 1, 4, 5)
    send(speed.at[b], speed.at[b], 2, 2, (d, o), None)
    states = (started[0][0], started.pop()[0])
    del started[0]
    for j in range(5):
        send(
            lists_sent.at[2 + b],
            lists_sent.at[homes[j]],
            12 + j,
            12 + marks[j],
            peers[j],
            there[j],
        )

    arrived(pdx.at[pl.ds(theirs, 2)], 3, None)
    ids[pl.ds(o, 1), :] = pdx[theirs, 5:6, :].astype(I32)
    few = ids[...]
    hrow[64:72, :] = table_row(few)
    few_lo = lax.bitwise_and(few, LO - 1)
    for g in range(2):
        onehot[:, 8192 + g * 128 : 8320 + g * 128] = onehot_of(few_lo[g : g + 1, :])

    REST, INFL0, NX, NY, STR, INFL = range(6)
    cur[...] = vel[...]

    def keep_pair(into, p, far, me):
        far_t = pdx[far].T
        for q in range(0, 128, 32):
            rows = slice(q, q + 32)
            ox = far_t[rows, 0:1] - me[0:1, :]
            oy = far_t[rows, 1:2] - me[1:2, :]
            r2 = ox * ox + oy * oy
            into[REST, p, rows] = jnp.sqrt(r2 + CORE_SQ)
            into[INFL0, p, rows] = jnp.exp(-0.5 * r2)

    def named(p):
        return family[p // 3, p % 3]

    def named_far(f, k):
        listed = lists[lax.shift_right_arithmetic(f, 1), lax.bitwise_and(f, 1), k]
        return listed + lax.shift_left(lax.shift_right_arithmetic(f, 2), 2)

    def keep_bonds():
        for p in range(6):
            keep_pair(bonds, p, named(p) + 4, pdx[own + p // 3])

        @pl.loop(0, 6, unroll=6)
        def _(p):
            t = p // 3
            f = family[t, p - 3 * t]
            me = pdx[f + 4]
            for k in range(3):
                keep_pair(far_bonds, 3 * p + k, named_far(f, k), me)

    def stretched(kept, p, rows, far_t, me):
        yx = far_t[rows, 0:1] - me[0:1, :]
        yy = far_t[rows, 1:2] - me[1:2, :]
        y2 = yx * yx + yy * yy + CORE_SQ
        inverse = lax.rsqrt(y2)
        rest = kept[REST, p, rows]
        stretch = y2 * inverse - rest
        ratio = stretch * (1.0 / STRETCH)
        influence = kept[INFL0, p, rows] * inverted(1.0 + ratio * ratio)
        return yx, yy, inverse, rest, stretch, influence

    def columns(far):
        return jnp.concatenate([place[far], jnp.zeros((6, 128), F32)], axis=0).T

    def state_of(total):
        dilated, volume = [jnp.sum(x, axis=0, keepdims=True) for x in total]
        return jnp.concatenate([2.0 * dilated / volume, volume], axis=0)

    row_iota = lax.broadcasted_iota(I32, (64, 128), 0)

    def masked_rows(product, row):
        both = product[0:128] + product[128:256]
        hit = row_iota == jnp.broadcast_to(row, (64, 128))
        out = []
        for c in range(2):
            x = jnp.where(hit[0:32], both[c * 32 : c * 32 + 32], 0.0)
            x = x + jnp.where(hit[32:64], both[64 + c * 32 : 96 + c * 32], 0.0)
            out.append(jnp.sum(x, axis=0, keepdims=True))
        return out

    def spread(values, row):
        hit = row_iota == jnp.broadcast_to(row, (64, 128))
        blocks = []
        for part in range(2):
            wide = [
                jnp.where(hit, jnp.broadcast_to(values[part][c], (64, 128)), 0.0)
                for c in range(2)
            ]
            for half in range(2):
                for c in range(2):
                    blocks.append(wide[c][half * 32 : half * 32 + 32])
        return jnp.concatenate(blocks, axis=0).astype(BF16)

    def scattered(values, first):
        sides = []
        for g, x in enumerate(values):
            x_top = x.astype(BF16).astype(F32)
            x_low = x - x_top
            sides.append(
                spread(
                    [[y[0:1, :], y[1:2, :]] for y in (x_top, x_low)],
                    hrow[64 + first + g : 65 + first + g, :],
                )
            )
        at = 8192 + first * 128
        both = nt(jnp.concatenate(sides, axis=1), onehot[:, at : at + 256])
        return both[0:128, :] + both[128:256, :]

    def blend(s, picked):
        ub = (ub0, ub1)[s]
        base = 17 + 10 * s
        targets = []
        for q in range(2):
            x = nt(two_parts(picked[q]), split_pm[q])
            targets.append(x[0:2, 0:128] + x[2:4, 0:128] + x[0:2, 128:256])
        for k in range(4):
            u = pdx[8 + k, 3:5, :] if s == 0 else ub[8 + k]
            new = u
            for q in range(2):
                hit = jnp.full((2, 128), ptile[q], I32) == k
                new = jnp.where(hit, u + pblend[q : q + 1, :] * (targets[q] - u), new)
            ub[8 + k] = new
        mine = ub.at[pl.ds(8, 4)]
        for j, (to, at, peer, cond) in enumerate(
            (
                (16, 3, left2, has_left2),
                (0, 2, right2, has_right2),
                (12, 1, left, has_left),
                (4, 0, right, has_right),
            )
        ):
            send(mine, ub.at[pl.ds(to, 4)], base + j, base + at, (peer, b), cond)

    for s in range(2):
        ub = (ub0, ub1)[s]
        base = 17 + 10 * s
        if s == 0:
            arrived(table.at[o], 0, None)
            arrived(pm.at[o], 1, None)
            for q in range(2):
                top, low = split2(pm[q])
                split_pm[q, 0:128] = top
                split_pm[q, 128:256] = low

        top, low = split2(table[...].reshape(128, LO))
        split_table[0:128, :] = top
        split_table[128:256, :] = low
        if s == 0:
            product = jnp.dot(
                split_table[...], onehot[:, 8192:8448], preferred_element_type=F32
            )
            blend(
                0,
                [
                    jnp.concatenate(
                        masked_rows(
                            product[:, q * 128 : (q + 1) * 128], hrow[64 + q : 65 + q, :]
                        ),
                        axis=0,
                    )
                    for q in range(2)
                ],
            )

        @pl.loop(0, 64 // CHUNK, unroll=4)
        def _(i):
            rows = pl.ds(pl.multiple_of(i * CHUNK, CHUNK), CHUNK)
            lanes = pl.ds(pl.multiple_of(i * (CHUNK * 128), CHUNK * 128), CHUNK * 128)
            product = jnp.dot(
                split_table[...], onehot[:, lanes], preferred_element_type=F32
            )
            row = hrow[rows, :]
            found = [
                masked_rows(product[:, g * 128 : (g + 1) * 128], row[g : g + 1, :])
                for g in range(CHUNK)
            ]
            for c in range(2):
                del_[rows, c * 128 : (c + 1) * 128] = jnp.concatenate(
                    [f[c] for f in found], axis=0
                )

        if s == 0:
            few_f = ids[...].astype(F32)
            few_t = few_f.T
            for q in range(2):
                for side in range(2):
                    link[
                        q * 128 : (q + 1) * 128, side * 128 : (side + 1) * 128
                    ] = jnp.where(
                        few_t[:, q : q + 1] == few_f[2 + side : 3 + side, :], 1.0, 0.0
                    ).astype(BF16)

        grad = jnp.dot(sgrad[...], del_[...], precision=EXACT, preferred_element_type=F32)
        exx = grad[0:64, 0:128]
        eyy = grad[64:128, 128:256]
        exy = 0.5 * (grad[64:128, 0:128] + grad[0:64, 128:256])
        scaled = scale * (1.0 + exx * exx + eyy * eyy + 2.0 * exy * exy)
        both = exx + eyy
        sxx = scaled * (both + 2.0 * exx)
        syy = scaled * (both + 2.0 * eyy)
        sxy = scaled * 2.0 * exy
        stress = jnp.concatenate(
            [
                jnp.concatenate([sxx, sxy], axis=1),
                jnp.concatenate([sxy, syy], axis=1),
            ],
            axis=0,
        )
        fel[...] = jnp.dot(sgt[...], stress, precision=EXACT, preferred_element_type=F32)
        acc[...] = jnp.zeros((256, LO), F32)

        @pl.loop(0, 64 // CHUNK, unroll=4)
        def _(i):
            rows = pl.ds(pl.multiple_of(i * CHUNK, CHUNK), CHUNK)
            lanes = pl.ds(pl.multiple_of(i * (CHUNK * 128), CHUNK * 128), CHUNK * 128)
            row = hrow[rows, :]
            f = fel[rows, :]
            f_top = f.astype(BF16).astype(F32)
            f_low = f - f_top
            left_side = jnp.concatenate(
                [
                    spread(
                        [
                            [x[g : g + 1, 0:128], x[g : g + 1, 128:256]]
                            for x in (f_top, f_low)
                        ],
                        row[g : g + 1, :],
                    )
                    for g in range(CHUNK)
                ],
                axis=1,
            )
            acc[...] += nt(left_side, onehot[:, lanes])

        partial = acc[0:128, :] + acc[128:256, :]
        pel_send[s] = partial
        if s == 0:
            send(pel_send.at[s], pel_recv.at[s], base + 4, base + 4, (d, o), None)
        else:
            cut = pl.ds(o * 64, 64)
            send(
                pel_send.at[s, cut],
                pel_recv.at[s, cut],
                base + 4,
                base + 4,
                (d, o),
                None,
            )
        top, low = split2(partial)
        product = jnp.dot(
            jnp.concatenate([top, low], axis=0),
            onehot[:, 8448:8704],
            preferred_element_type=F32,
        )
        border = []
        for side in range(2):
            found = masked_rows(
                product[:, side * 128 : (side + 1) * 128],
                hrow[66 + side : 67 + side, :],
            )
            border.append(jnp.concatenate(found, axis=0))

        if s == 0:
            for j in range(1, 9):
                arrived(pdx.at[pl.ds(sources[j], 2)], 3 + j, there[j])
            for j in range(5):
                arrived(lists_sent.at[sources_lists[j]], 12 + j, there[j])
            scalars = pltpu.make_async_copy(lists_sent, lists, lsem.at[21])
            scalars.start()
            scalars.wait()
            keep_bonds()

        arrived(ub.at[pl.ds(4, 4)], base, has_left)
        arrived(ub.at[pl.ds(12, 4)], base + 1, has_right)
        place[4:16] = pdx[4:16, 0:2, :] + ub[4:16]

        totals = [[jnp.zeros((8, 128), F32)] * 2 for _ in range(2)]
        for p in range(6):
            t = p // 3
            far_t = columns(named(p) + 4)
            me = place[own + t]
            for q in range(0, 128, 32):
                rows = slice(q, q + 32)
                yx, yy, inverse, rest, stretch, influence = stretched(
                    bonds, p, rows, far_t, me
                )
                bonds[NX, p, rows] = yx * inverse
                bonds[NY, p, rows] = yy * inverse
                bonds[STR, p, rows] = stretch
                bonds[INFL, p, rows] = influence
                weighted = influence * rest
                totals[t][0] = totals[t][0] + folded(weighted * stretch)
                totals[t][1] = totals[t][1] + folded(weighted * rest)
        states_own = [state_of(x) for x in totals]
        arrived(ub.at[pl.ds(0, 4)], base + 2, has_left2)
        arrived(ub.at[pl.ds(16, 4)], base + 3, has_right2)
        place[0:4] = pdx[0:4, 0:2, :] + ub[0:4]
        place[16:20] = pdx[16:20, 0:2, :] + ub[16:20]

        @pl.loop(0, 3, unroll=3)
        def _(i):
            for j in range(2):
                p = 2 * i + j
                t = p // 3
                f = family[t, p - 3 * t]
                me = place[f + 4]
                total = [jnp.zeros((8, 128), F32)] * 2
                for k in range(3):
                    far_t = columns(named_far(f, k))
                    for q in range(0, 128, 32):
                        *_, rest, stretch, influence = stretched(
                            far_bonds, 3 * p + k, slice(q, q + 32), far_t, me
                        )
                        weighted = influence * rest
                        total[0] = total[0] + folded(weighted * stretch)
                        total[1] = total[1] + folded(weighted * rest)
                far_state[p] = state_of(total)

        def coefficients(k, state):
            theta, volume = state[0:1, :], state[1:2, :]
            return 2.0 * k * theta / volume, 4.0 * k / volume, 0.5 * theta

        totals = [[jnp.zeros((8, 128), F32)] * 2 for _ in range(2)]
        near = [coefficients(pdx[own + t][2:3, :], states_own[t]) for t in range(2)]
        for p in range(6):
            t = p // 3
            far = coefficients(pdx[named(p) + 4][2:3, :], far_state[p])
            far_t = jnp.concatenate(far + (jnp.zeros((5, 128), F32),), axis=0).T
            oa, ob, oc = near[t]
            for q in range(0, 128, 32):
                rows = slice(q, q + 32)
                rest = bonds[REST, p, rows]
                stretch = bonds[STR, p, rows]
                mine = oa * rest + ob * (stretch - oc * rest)
                away = far_t[rows, 0:1] * rest + far_t[rows, 1:2] * (
                    stretch - far_t[rows, 2:3] * rest
                )
                force = bonds[INFL, p, rows] * (mine + away)
                totals[t][0] = totals[t][0] + folded(force * bonds[NX, p, rows])
                totals[t][1] = totals[t][1] + folded(force * bonds[NY, p, rows])

        forces, moved = [], []
        for t in range(2):
            alive = jnp.full((2, 128), 2 * b + t, I32) < live[0]
            total = [jnp.sum(x, axis=0, keepdims=True) for x in totals[t]]
            force = jnp.where(alive, jnp.concatenate(total, axis=0), 0.0)
            forces.append(force)
            v = jnp.where(alive, cur[t] + step[t : t + 1, :] * force, 0.0)
            u = jnp.where(alive, ub[own + t] + TIME_STEP * v, 0.0)
            cur[t] = v
            moved.append(u)

        reaction = []
        for q in range(2):
            w = jnp.zeros((2, 128), F32)
            for t in range(2):
                hit = jnp.full((2, 128), ptile[q], I32) == 2 * b + t
                w = w + jnp.where(hit, pblend[q : q + 1, :] * forces[t], 0.0)
            w = two_parts(w)
            x = jnp.dot(w, split_pm[q, 0:128], preferred_element_type=F32)
            y = jnp.dot(w, split_pm[q, 128:256], preferred_element_type=F32)
            reaction.append(x[0:2, :] + x[2:4, :] + y[0:2, :])
        late = jnp.concatenate(reaction + moved, axis=0)
        late_send[s] = late
        send(late_send.at[s], late_recv.at[s], base + 5, base + 5, (d, o), None)
        wide = jnp.concatenate(reaction, axis=1)
        met = jnp.dot(two_parts(wide), link[...], preferred_element_type=F32)
        met = met[0:2, :] + met[2:4, :]
        for side in range(2):
            bd_send[s, side] = met[:, side * 128 : (side + 1) * 128] - border[side]
        for j in range(4):
            side = j // 2
            send(
                bd_send.at[s, side],
                bd_recv.at[s, 2 * (1 - side) + b],
                base + 6 + j,
                base + 6 + 2 * (1 - side) + b,
                peers[1 + j],
                there[1 + j],
            )
        if s == 0:
            for t in range(2):
                ub1[own + t] = moved[t]
        else:
            for t in range(2):
                disp_out[t] = moved[t]
                vel_out[t] = cur[t]

        halves = range(2) if s == 0 else (b,)
        if s == 0:
            arrived(speed.at[o], 2, None)
            arrived(pel_recv.at[s], base + 4, None)
            for copy in states:
                copy.wait_send()
        else:
            arrived(pel_recv.at[s, pl.ds(b * 64, 64)], base + 4, None)
        for h in halves:
            for c in range(2):
                cut = pl.ds(h * 64 + c * 32, 32)
                rows = slice(c * 32, c * 32 + 32)
                speed[h, rows, :] = speed[h, rows, :] - speed[h, 64:96, :] * (
                    pel_send[s, cut, :] + pel_recv[s, cut, :]
                )
        if s == 0:
            rows = []
            for h in range(2):
                for c in range(2):
                    cut = slice(c * 32, c * 32 + 32)
                    rows.append(table[h, cut, :] + TIME_STEP * speed[h, cut, :])
            rows = rows + [speed[0, 64:96, :], speed[1, 64:96, :]]
            top, low = split2(jnp.concatenate(rows, axis=0))
            product = jnp.dot(
                jnp.concatenate([top, low], axis=0),
                onehot[:, 8192:8448],
                preferred_element_type=F32,
            )
            early, pace = [], []
            for q in range(2):
                row = hrow[64 + q : 65 + q, :]
                part = product[:, q * 128 : (q + 1) * 128]
                early.append(
                    jnp.concatenate(
                        masked_rows(
                            jnp.concatenate([part[0:128], part[192:320]], axis=0), row
                        ),
                        axis=0,
                    )
                )
                steps = part[128:192] + part[320:384]
                hit = row_iota == jnp.broadcast_to(row, (64, 128))
                pace.append(
                    jnp.sum(jnp.where(hit, steps, 0.0), axis=0, keepdims=True)
                )
        arrived(late_recv.at[s], base + 5, None)
        other = late_recv[s]
        if s == 0:
            for t in range(2):
                ub1[theirs + t] = other[4 + 2 * t : 6 + 2 * t, :]
        acc[0:128, :] = scattered(
            [late[0:2, :] + other[0:2, :], late[2:4, :] + other[2:4, :]], 0
        )
        for j in range(4):
            arrived(bd_recv.at[s, j], base + 6 + j, there[1 + j])
        shared = [
            jnp.where(
                jnp.full((2, 128), d, I32) > 0, bd_recv[s, 0] + bd_recv[s, 1], 0.0
            ),
            jnp.where(
                jnp.full((2, 128), d, I32) < n_dom - 1,
                bd_recv[s, 2] + bd_recv[s, 3],
                0.0,
            ),
        ]
        if s == 0:
            met = nt(two_parts(jnp.concatenate(shared, axis=1)), link[...])
            met = met[0:2, :] + met[2:4, :]
            blend(
                1,
                [
                    early[q]
                    + TIME_STEP
                    * pace[q]
                    * (
                        late[2 * q : 2 * q + 2, :]
                        + other[2 * q : 2 * q + 2, :]
                        + met[:, q * 128 : (q + 1) * 128]
                    )
                    for q in range(2)
                ],
            )
        acc[128:256, :] = scattered(shared, 2)
        acc[0:128, :] = acc[0:128, :] + acc[128:256, :]
        for h in halves:
            for c in range(2):
                cut = pl.ds(h * 64 + c * 32, 32)
                rows = slice(c * 32, c * 32 + 32)
                v = speed[h, rows, :] + speed[h, 64:96, :] * acc[cut, :]
                speed[h, rows, :] = v
                table[h, rows, :] = table[h, rows, :] + TIME_STEP * v

    for r in range(HALF_ROWS):
        lanes = slice(r * LO, (r + 1) * LO)
        for c in range(2):
            at = PAD_ROWS * c + r
            fdisp_out[c : c + 1, lanes] = table[b, at : at + 1, :]
            fvel_out[c : c + 1, lanes] = speed[b, at : at + 1, :]
    for copy, cond in started:
        if_there(cond, copy.wait_send)


def hand_over(*refs):
    ins, outs, sems = refs[:4], refs[4:8], refs[8]
    copies = [
        pltpu.make_async_copy(src, dst, sems.at[at])
        for at, (src, dst) in enumerate(zip(ins, outs))
    ]
    for copy in copies:
        copy.start()
    for copy in copies:
        copy.wait()


def shards(n_dom, *args):
    (
        pd_disp,
        pd_vel,
        pd_coord,
        pd_modulus,
        pd_step,
        family,
        live,
        patch_tile,
        patch_blend,
        patch_nodes,
        patch_matrix,
        fe_disp,
        fe_vel,
        fe_step,
        fe_modulus,
        element_nodes,
        shape_grad,
        quad_weight,
        shared_left,
        shared_right,
    ) = args
    vmem = pl.BlockSpec(memory_space=pltpu.VMEM)
    hbm = pl.BlockSpec(memory_space=pltpu.HBM)
    rows = fe_step.shape[0] // 128

    def f32(*shape):
        return pltpu.VMEM(shape, F32)

    results = pl.pallas_call(
        functools.partial(kernel, n_dom),
        out_shape=[
            pltpu.VMEM(pd_disp.shape, F32),
            pltpu.VMEM(pd_vel.shape, F32),
            pltpu.VMEM(fe_disp.shape, F32),
            pltpu.VMEM(fe_vel.shape, F32),
        ],
        in_specs=[hbm] * 20,
        out_specs=[vmem] * 4,
        scratch_shapes=[
            f32(2, 2, 128),
            f32(2, 2, 128),
            f32(2, 2, 128),
            f32(2, 128),
            f32(2, 128),
            pltpu.SMEM((2, 3), I32),
            pltpu.SMEM((1,), I32),
            pltpu.SMEM((2,), I32),
            f32(2, 128),
            pltpu.VMEM((1, 128), I32),
            f32(*fe_disp.shape),
            f32(*fe_vel.shape),
            f32(rows, 128),
            f32(1, 128),
            pltpu.VMEM((64, 128), I32),
            f32(128, 64),
            f32(1, 64),
            pltpu.VMEM((1, 113), I32),
            pltpu.VMEM((1, 113), I32),
            f32(20, 8, 128),
            f32(20, 2, 128),
            f32(20, 2, 128),
            f32(20, 2, 128),
            pltpu.VMEM((2, 3), I32),
            pltpu.VMEM((6, 8, 128), I32),
            pltpu.SMEM((6, 8, 128), I32),
            f32(2, 128, 128),
            pltpu.VMEM((2, 256, 128), BF16),
            f32(2, 64, LO),
            f32(2, 96, LO),
            pltpu.VMEM((256, LO), BF16),
            pltpu.VMEM((LO, 8704), BF16),
            pltpu.VMEM((72, 128), I32),
            pltpu.VMEM((8, 128), I32),
            pltpu.VMEM((256, 256), BF16),
            f32(64, 256),
            f32(64, 256),
            f32(64, 128),
            f32(256, LO),
            f32(6, 6, 128, 128),
            f32(2, 18, 128, 128),
            f32(6, 2, 128),
            f32(2, 2, 128),
            f32(2, 128, LO),
            f32(2, 128, LO),
            f32(2, 8, 128),
            f32(2, 8, 128),
            f32(2, 2, 2, 128),
            f32(2, 4, 2, 128),
            pltpu.SemaphoreType.DMA((N_COPIES,)),
            pltpu.SemaphoreType.DMA((N_COPIES,)),
            pltpu.SemaphoreType.DMA((22,)),
        ],
        compiler_params=pltpu.CompilerParams(
            collective_id=0, has_side_effects=True, vmem_limit_bytes=VMEM_BYTES
        ),
    )(
        pd_disp,
        pd_vel,
        pd_coord,
        pd_modulus,
        pd_step,
        family,
        live,
        patch_tile,
        patch_blend,
        patch_nodes,
        patch_matrix,
        fe_disp,
        fe_vel,
        fe_step.reshape(-1, 128),
        fe_modulus.reshape(1, -1),
        element_nodes,
        shape_grad.reshape(-1, shape_grad.shape[2]),
        quad_weight.reshape(1, -1),
        shared_left,
        shared_right,
    )
    return pl.pallas_call(
        hand_over,
        out_shape=[jax.ShapeDtypeStruct(x.shape, F32) for x in results],
        in_specs=[vmem] * 4,
        out_specs=[hbm] * 4,
        scratch_shapes=[pltpu.SemaphoreType.DMA((4,))],
        compiler_params=pltpu.CompilerParams(vmem_limit_bytes=2**20),
    )(*results)


def solution(mesh):
    both = ("dom", "blk")
    return jax.shard_map(
        functools.partial(shards, mesh.shape["dom"]),
        mesh=mesh,
        in_specs=(
            P(both, None, None),
            P(both, None, None),
            P(both, None, None),
            P(both, None),
            P(both, None),
            P(both, None),
            P("dom"),
            P("dom"),
            P("dom", None),
            P(both, None),
            P(both, None, None),
            P(None, both),
            P(None, both),
            P(both),
            P(both),
            P(None, both),
            P(),
            P(),
            P("dom", None),
            P("dom", None),
        ),
        out_specs=(
            P(both, None, None),
            P(both, None, None),
            P(None, both),
            P(None, both),
        ),
        check_vma=False,
    )
```
